32 devices in a mesh: seq: 8 (over z, x), head: 4 (over y, core).
Axes of the slice: x: 2, y: 2, z: 4, core: 2. Of those that a mesh axis runs over, the one named last changes fastest.
Arguments:
- x_in: bfloat16 [8, 1024, 1536], P(None, 'seq'), may hold values from -6 to 6
- seg_ids: int32 [8, 1024], P(None, 'seq'), may hold values from 0 to 31, as said below
- norm1_gain: float32 [1536], P('seq'), may hold values from 0.5 to 1.5
- w_in_x: float32 [1536, 3072], P('seq', 'head'), may hold values from -0.15625 to 0.15625
- w_in_z: float32 [1536, 3072], P('seq', 'head'), may hold values from -0.15625 to 0.15625
- conv_w: float32 [4, 3072], P(None, ('head', 'seq')), may hold values from -3 to 3
- conv_b: float32 [3072], P(('head', 'seq')), may hold values from -3 to 3
- w_xproj: float32 [3072, 128], P(('head', 'seq')), may hold values from -0.109375 to 0.109375
- ssm_gain: float32 [128], P('seq'), may hold values from 0.5 to 1.5
- w_dt: float32 [96, 3072], P(None, ('head', 'seq')), may hold values from -0.625 to 0.625
- dt_bias: float32 [3072], P(('head', 'seq')), may hold values from -14 to -2
- a_log: float32 [3072, 16], P(('head', 'seq')), may hold values from -1 to 1.5
- d_skip: float32 [3072], P(('head', 'seq')), may hold values from 0.5 to 2
- w_out: float32 [3072, 1536], P('head', 'seq'), may hold values from -0.109375 to 0.109375
- norm2_gain: float32 [1536], P('seq'), may hold values from 0.5 to 1.5
- w_gate: float32 [1536, 4096], P('seq', 'head'), may hold values from -0.15625 to 0.15625
- w_up: float32 [1536, 4096], P('seq', 'head'), may hold values from -0.15625 to 0.15625
- w_down: float32 [4096, 1536], P('head', 'seq'), may hold values from -0.09375 to 0.09375
- d_out: bfloat16 [8, 1024, 1536], P(None, 'seq'), may hold values from -6 to 6
Outputs:
- block_out: bfloat16 [8, 1024, 1536], P(None, 'seq')
- grad_input: float32 [8, 1024, 1536], P(None, 'seq')
- grad_norm1_gain: float32 [1536], P('seq')
- grad_w_in_x: float32 [1536, 3072], P('seq', 'head')
- grad_w_in_z: float32 [1536, 3072], P('seq', 'head')
- grad_conv_w: float32 [4, 3072], P(None, ('head', 'seq'))
- grad_conv_b: float32 [3072], P(('head', 'seq'))
- grad_w_xproj: float32 [3072, 128], P(('head', 'seq'))
- grad_ssm_gain: float32 [128], P('seq')
- grad_w_dt: float32 [96, 3072], P(None, ('head', 'seq'))
- grad_dt_bias: float32 [3072], P(('head', 'seq'))
- grad_a_log: float32 [3072, 16], P(('head', 'seq'))
- grad_d_skip: float32 [3072], P(('head', 'seq'))
- grad_w_out: float32 [3072, 1536], P('head', 'seq')
- grad_norm2_gain: float32 [1536], P('seq')
- grad_w_gate: float32 [1536, 4096], P('seq', 'head')
- grad_w_up: float32 [1536, 4096], P('seq', 'head')
- grad_w_down: float32 [4096, 1536], P('head', 'seq')
The draws below stay inside these ranges and needn't reach their ends.
Inputs may be any that keep to these rules, and one draw needn't show every extreme that they name: `seg_ids`: document numbers never fall along a sequence; a document begins where the number changes. The last document of every sequence has number 31. One sequence, chosen by the seed, is a single document. Documents other than a sequence's last have 1024 // 20 to 512 tokens.
All inputs are finite; a program needn't handle non-finite values.
Results may differ from the reference program's by a relative error of at most 0.015.
The reference program's roundings to bfloat16 on the way count: a program that leaves them out, or rounds other values in their place, can miss the bound.
Values may be sent and summed in bfloat16 or wider, within the bound.
A program may use at most 192 MiB of HBM per device.

```python
import jax
import jax.numpy as jnp
from jax import lax

D = 1536
E = 3072
N = 16
K = 4
R = 96
FF = 4096
SEQS = 8
LEN = 1024


def draw_seg_ids(key, part):
    key = jax.random.fold_in(key, 7)
    key_lengths, key_single = jax.random.split(key)
    low_len = max(LEN // 20, 1)
    high_len = max(LEN // 2, low_len)
    lengths = jax.random.randint(key_lengths, (SEQS, 32), low_len, high_len + 1)
    bounds = jnp.cumsum(lengths, axis=1)
    positions = jnp.arange(LEN, dtype=jnp.int32)
    later_bounds = (positions[None, :, None] < bounds[:, None, :]) & (bounds[:, None, :] < LEN)
    numbers = 31 - jnp.sum(later_bounds.astype(jnp.int32), axis=2)
    single_row = jax.random.randint(key_single, (), 0, SEQS)
    numbers = jnp.where(jnp.arange(SEQS)[:, None] == single_row, 31, numbers)
    return numbers.astype(jnp.int32)


def draw_dt_bias(key, part):
    key = jax.random.fold_in(key, 11)
    top_step = 0.05
    exponent = jax.random.uniform(key, (E,), jnp.float32, jnp.log(0.01 / LEN), jnp.log(top_step))
    step_size = jnp.exp(exponent)
    return jnp.log(jnp.expm1(step_size)).astype(jnp.float32)


def block_scale(key, dims, pieces, low, top_value):
    def one(axis_at, blocks):
        draws = jax.random.uniform(jax.random.fold_in(jax.random.fold_in(key, 6), axis_at), (blocks,), jnp.float32, low / len(pieces), top_value / len(pieces))
        return jnp.repeat(jnp.exp(draws), dims[axis_at] // blocks).reshape((-1,) + (1,) * (len(dims) - axis_at - 1))

    loudness = one(*pieces[0])
    for cut in pieces[1:]:
        loudness = loudness * one(*cut)
    return loudness


def centred(stream_key, extent, deviation, reach, pieces=(), kind=jnp.bfloat16):
    level = block_scale(stream_key, extent, pieces, -0.22, 0.18) if pieces else 1.0
    values = jax.random.normal(stream_key, extent, jnp.float32) * deviation * level
    return jnp.minimum(jnp.maximum(values, -reach), reach).astype(kind)


def setup_inputs(seed: int = 0) -> dict:
    keys = jax.random.split(jax.random.key(seed), 20)
    return {
        "x_in": centred(keys[0], (SEQS, LEN, D), 1.0, 6.0, ((1, 8),)),
        "seg_ids": draw_seg_ids(jax.random.fold_in(keys[19], 71), 0),
        "norm1_gain": jnp.clip(1.0 + 0.1 * jax.random.normal(keys[2], (D,), jnp.float32), 0.5, 1.5),
        "w_in_x": centred(keys[3], (D, E), D ** -0.5, 0.15625, ((0, 8), (1, 4)), jnp.float32),
        "w_in_z": centred(keys[4], (D, E), D ** -0.5, 0.15625, ((0, 8), (1, 4)), jnp.float32),
        "conv_w": centred(keys[5], (K, E), K ** -0.5, 3.0, ((1, 32),), jnp.float32),
        "conv_b": centred(keys[6], (E,), 0.5, 3.0, ((0, 32),), jnp.float32),
        "w_xproj": centred(keys[7], (E, R + 2 * N), E ** -0.5, 0.109375, ((0, 32),), jnp.float32),
        "ssm_gain": jnp.clip(1.0 + 0.1 * jax.random.normal(keys[8], (R + 2 * N,), jnp.float32), 0.5, 1.5),
        "w_dt": centred(keys[9], (R, E), R ** -0.5, 0.625, ((1, 32),), jnp.float32),
        "dt_bias": draw_dt_bias(jax.random.fold_in(keys[19], 71), 0),
        "a_log": jnp.clip(-1.0 + 2.5 * jax.random.uniform(keys[11], (E, N), jnp.float32) ** block_scale(keys[11], (E, N), ((0, 32),), -0.2, 0.2), -1.0, 1.5),
        "d_skip": jnp.clip(0.5 + 1.5 * jax.random.uniform(keys[12], (E,), jnp.float32) ** block_scale(keys[12], (E,), ((0, 32),), -0.2, 0.2), 0.5, 2.0),
        "w_out": centred(keys[13], (E, D), E ** -0.5, 0.109375, ((0, 4), (1, 8)), jnp.float32),
        "norm2_gain": jnp.clip(1.0 + 0.1 * jax.random.normal(keys[14], (D,), jnp.float32), 0.5, 1.5),
        "w_gate": centred(keys[15], (D, FF), D ** -0.5, 0.15625, ((0, 8), (1, 4)), jnp.float32),
        "w_up": centred(keys[16], (D, FF), D ** -0.5, 0.15625, ((0, 8), (1, 4)), jnp.float32),
        "w_down": centred(keys[17], (FF, D), FF ** -0.5, 0.09375, ((0, 4), (1, 8)), jnp.float32),
        "d_out": centred(keys[18], (SEQS, LEN, D), 1.0, 6.0, ((1, 8),)),
    }


EPS = 1e-06
HIGH = lax.Precision.HIGHEST

@jax.custom_vjp
def low(v):
    return lax.optimization_barrier(v.astype(jnp.bfloat16)).astype(jnp.float32)

@jax.custom_vjp
def low_back(v):
    return v

def low_keep(v):
    return (low(v), None)

def low_pass(kept, grad):
    return (grad,)

def back_keep(v):
    return (v, None)

def back_low(kept, grad):
    return (low(grad),)
low.defvjp(low_keep, low_pass)
low_back.defvjp(back_keep, back_low)

def matmul(left, right):
    return jnp.dot(left, right, precision=HIGH, preferred_element_type=jnp.float32)

def rms_norm(values, gain_vec):
    return values * lax.rsqrt(lax.optimization_barrier(jnp.mean(values * values, axis=-1, keepdims=True)) + EPS) * gain_vec

def state_scan(u_val, step_size, b_norm, c_norm, decay_rates, keep_flag):
    seq_len = u_val.shape[0]
    block_len = 64 if seq_len % 64 == 0 else seq_len

    def one_token(carried, token_items):
        u_t, step_t, b_t, c_t, keep_t = token_items
        carried = keep_t * jnp.exp(step_t[:, None] * decay_rates) * carried + (step_t * u_t)[:, None] * b_t[None, :]
        return (carried, matmul(carried, c_t))

    @jax.checkpoint
    def one_block(carried, block_items):
        return lax.scan(one_token, carried, block_items)
    block_items = tuple((member.reshape((seq_len // block_len, block_len) + member.shape[1:]) for member in (u_val, step_size, b_norm, c_norm, keep_flag)))
    initial = jnp.zeros(decay_rates.shape, jnp.float32)
    unused, results = lax.scan(one_block, initial, block_items)
    return results.reshape(seq_len, -1)

def forward_one(params, x_seq, seg_seq):
    norm1_gain, w_in_x, w_in_z, conv_w, conv_b, w_xproj, ssm_gain, w_dt, dt_bias, a_log, d_skip, w_out, norm2_gain, w_gate, w_up, w_down = tuple((low(member) for member in params))
    seq_len = x_seq.shape[0]
    step_rank = w_dt.shape[0]
    state_dim = a_log.shape[1]
    kernel = conv_w.shape[0]
    x_norm = low(rms_norm(x_seq, norm1_gain))
    x_inner = low_back(low(matmul(x_norm, w_in_x)))
    z_gate = low_back(matmul(x_norm, w_in_z))
    padded = jnp.concatenate([jnp.zeros((kernel - 1, x_inner.shape[1]), jnp.float32), x_inner], axis=0)
    seg_pad = jnp.concatenate([jnp.full((kernel - 1,), -1, jnp.int32), seg_seq.astype(jnp.int32)])
    x_conv = conv_b[None, :]
    for offset in range(kernel):
        first_row = kernel - 1 - offset
        shifted = padded[first_row:first_row + seq_len]
        same_doc = (seg_pad[first_row:first_row + seq_len] == seg_seq).astype(jnp.float32)
        x_conv = x_conv + conv_w[offset][None, :] * shifted * same_doc[:, None]
    u_val = low(jax.nn.silu(x_conv))
    projected = matmul(u_val, w_xproj)
    dt_norm = low(rms_norm(projected[:, :step_rank], ssm_gain[:step_rank]))
    b_norm = rms_norm(projected[:, step_rank:step_rank + state_dim], ssm_gain[step_rank:step_rank + state_dim])
    c_norm = rms_norm(projected[:, step_rank + state_dim:], ssm_gain[step_rank + state_dim:])
    dt_pre = low_back(matmul(dt_norm, w_dt))
    step_size = jax.nn.softplus(dt_pre + dt_bias)
    decay_rates = -jnp.exp(a_log)
    previous = jnp.concatenate([jnp.full((1,), -1, jnp.int32), seg_seq[:-1].astype(jnp.int32)])
    keep_flag = (seg_seq == previous).astype(jnp.float32)
    y_state = state_scan(u_val, step_size, b_norm, c_norm, decay_rates, keep_flag)
    y_full = y_state + d_skip * u_val
    g_val = low(y_full * jax.nn.silu(z_gate))
    hidden = x_seq + low_back(matmul(g_val, w_out))
    x_norm2 = low(rms_norm(hidden, norm2_gain))
    gate_proj = low_back(matmul(x_norm2, w_gate))
    up_proj = low_back(matmul(x_norm2, w_up))
    act_val = low(jax.nn.silu(gate_proj) * up_proj)
    return hidden + low_back(matmul(act_val, w_down))

def reference(x_in, seg_ids, norm1_gain, w_in_x, w_in_z, conv_w, conv_b, w_xproj, ssm_gain, w_dt, dt_bias, a_log, d_skip, w_out, norm2_gain, w_gate, w_up, w_down, d_out):
    params = (norm1_gain, w_in_x, w_in_z, conv_w, conv_b, w_xproj, ssm_gain, w_dt, dt_bias, a_log, d_skip, w_out, norm2_gain, w_gate, w_up, w_down)

    def per_sequence(totals, inputs):
        x_seq, seg_seq, cot_seq = inputs

        def forward(weights, x_values):
            return forward_one(weights, x_values, seg_seq)
        result, pullback = jax.vjp(forward, params, x_seq.astype(jnp.float32))
        weight_grads, input_grad = pullback(cot_seq.astype(jnp.float32))
        totals = jax.tree.map(lambda a, b: a + b, totals, weight_grads)
        return (totals, (result.astype(jnp.bfloat16), input_grad))
    zeros = jax.tree.map(jnp.zeros_like, params)
    totals, outputs = lax.scan(per_sequence, zeros, (x_in, seg_ids, d_out))
    block_out, grad_input = outputs
    return (block_out, grad_input, totals[0], totals[1], totals[2], totals[3], totals[4], totals[5], totals[6], totals[7], totals[8], totals[9], totals[10], totals[11], totals[12], totals[13], totals[14], totals[15])
```

```python
import functools

import jax
import jax.numpy as jnp
from jax import lax
from jax.experimental import pallas as pl
from jax.experimental.pallas import tpu as pltpu
from jax.sharding import PartitionSpec as P

EPS = 1e-06
LOG2E = 1.4426950408889634
LN2 = 0.6931471805599453
STOP = 1e30
LANES = 128
BF = jnp.bfloat16
F32 = jnp.float32


def shifted(value, axis, steps):
    count = lax.axis_size(axis)
    initial, last = (max(0, -steps), min(count, count - steps))
    return lax.ppermute(value, axis, [(source, source + steps) for source in range(initial, last)])


def norm_rows(values, gain_vec):
    inv_rms = lax.rsqrt(jnp.mean(values * values, axis=-1, keepdims=True) + EPS)
    return (values * inv_rms * gain_vec, inv_rms)


def norm_back(values, inv_rms, gain_vec, grad_rows):
    normed = values * inv_rms
    gain_grad = jnp.sum(grad_rows * normed, axis=0)
    scaled = grad_rows * gain_vec
    value_grad = inv_rms * (scaled - normed * jnp.mean(scaled * normed, axis=-1, keepdims=True))
    return (value_grad, gain_grad)


def silu_slope(values):
    logistic = jax.nn.sigmoid(values)
    return logistic * (1.0 + values * (1.0 - logistic))


def spread(column_ref, seqs, tokens, first, count, target):
    def one(token, carry):
        block = column_ref[pl.ds(pl.multiple_of(token * seqs, seqs), seqs), :]
        for n in range(count):
            column = block[:, first + n : first + n + 1]
            target[token * count + n] = jnp.broadcast_to(column, (seqs, LANES))
        return carry

    lax.fori_loop(0, tokens, one, 0)


def pair_rows(ref, pair, seqs):
    both = ref[pl.ds(pl.multiple_of(pair * 2 * seqs, 2 * seqs), 2 * seqs), :]
    both = both.astype(F32)
    return both[:seqs], both[seqs:]


def token_rows(ref, token, seqs):
    return ref[pl.ds(pl.multiple_of(token * seqs, seqs), seqs), :]


def end_kernel(seqs, tokens, states, bc_ref, step_ref, u_ref, rate_ref, end_ref, sum_ref, bb, pen):
    @pl.when(pl.program_id(0) == 0)
    def _():
        spread(bc_ref, seqs, tokens, 0, states, bb)
        spread(bc_ref, seqs, tokens, 2 * states, 1, pen)

    def one(pair, carry):
        state, total = carry
        u_pair = pair_rows(u_ref, pair, seqs)
        for half in range(2):
            token = pair * 2 + half
            step = token_rows(step_ref, token, seqs)
            drive = step * u_pair[half]
            stop = step + pen[token]
            total = total + stop
            fresh = []
            for n in range(states):
                decay = jnp.exp2(stop * rate_ref[pl.ds(n * seqs, seqs), :])
                fresh.append(decay * state[n] + drive * bb[token * states + n])
            state = tuple(fresh)
        return state, total

    zero = jnp.zeros((seqs, LANES), F32)
    state, total = lax.fori_loop(0, tokens // 2, one, ((zero,) * states, zero))
    for n in range(states):
        end_ref[pl.ds(n * seqs, seqs), :] = state[n].astype(end_ref.dtype)
    sum_ref[...] = total


def out_kernel(
    seqs, tokens, states, bc_ref, step_ref, u_ref, rate_ref, start_ref, y_ref, bb, cc, pen
):
    @pl.when(pl.program_id(0) == 0)
    def _():
        spread(bc_ref, seqs, tokens, 0, states, bb)
        spread(bc_ref, seqs, tokens, states, states, cc)
        spread(bc_ref, seqs, tokens, 2 * states, 1, pen)

    def one(pair, state):
        u_pair = pair_rows(u_ref, pair, seqs)
        for half in range(2):
            token = pair * 2 + half
            step = token_rows(step_ref, token, seqs)
            drive = step * u_pair[half]
            stop = step + pen[token]
            fresh = []
            out = jnp.zeros((seqs, LANES), F32)
            for n in range(states):
                decay = jnp.exp2(stop * rate_ref[pl.ds(n * seqs, seqs), :])
                value = decay * state[n] + drive * bb[token * states + n]
                out = out + value * cc[token * states + n]
                fresh.append(value)
            y_ref[pl.ds(pl.multiple_of(token * seqs, seqs), seqs), :] = out
            state = tuple(fresh)
        return state

    initial = tuple(start_ref[pl.ds(n * seqs, seqs), :] for n in range(states))
    lax.fori_loop(0, tokens // 2, one, initial)


def own_kernel(seqs, tokens, states, bc_ref, step_ref, dy_ref, rate_ref, own_ref, cc, pen):
    @pl.when(pl.program_id(0) == 0)
    def _():
        spread(bc_ref, seqs, tokens, states, states, cc)
        spread(bc_ref, seqs, tokens, 2 * states, 1, pen)

    def one(back, grads):
        for half in range(2):
            token = tokens - 1 - (back * 2 + half)
            stop = token_rows(step_ref, token, seqs) + pen[token]
            dy = token_rows(dy_ref, token, seqs)
            fresh = []
            for n in range(states):
                decay = jnp.exp2(stop * rate_ref[pl.ds(n * seqs, seqs), :])
                fresh.append(decay * (grads[n] + dy * cc[token * states + n]))
            grads = tuple(fresh)
        return grads

    zero = jnp.zeros((seqs, LANES), F32)
    grads = lax.fori_loop(0, tokens // 2, one, (zero,) * states)
    for n in range(states):
        own_ref[pl.ds(n * seqs, seqs), :] = grads[n].astype(own_ref.dtype)


def back_kernel(
    seqs,
    tokens,
    states,
    bc_ref,
    step_ref,
    u_ref,
    dy_ref,
    rate_ref,
    start_ref,
    last_ref,
    du_ref,
    dstep_ref,
    dbc_ref,
    dlog_ref,
    bb,
    cc,
    pen,
    held,
    acc_b,
    acc_c,
):
    tile = pl.program_id(0)

    @pl.when(tile == 0)
    def _():
        spread(bc_ref, seqs, tokens, 0, states, bb)
        spread(bc_ref, seqs, tokens, states, states, cc)
        spread(bc_ref, seqs, tokens, 2 * states, 1, pen)

        def clear(token, carry):
            for n in range(states):
                acc_b[token * states + n] = jnp.zeros((seqs, LANES), F32)
                acc_c[token * states + n] = jnp.zeros((seqs, LANES), F32)
            return carry

        lax.fori_loop(0, tokens, clear, 0)

    def again(pair, state):
        u_pair = pair_rows(u_ref, pair, seqs)
        for half in range(2):
            token = pair * 2 + half
            step = token_rows(step_ref, token, seqs)
            drive = step * u_pair[half]
            stop = step + pen[token]
            fresh = []
            for n in range(states):
                held[token * states + n] = state[n]
                decay = jnp.exp2(stop * rate_ref[pl.ds(n * seqs, seqs), :])
                fresh.append(decay * state[n] + drive * bb[token * states + n])
            state = tuple(fresh)
        return state

    initial = tuple(start_ref[pl.ds(n * seqs, seqs), :] for n in range(states))
    state = lax.fori_loop(0, tokens // 2, again, initial)
    for n in range(states):
        held[tokens * states + n] = state[n]

    def one(back, carry):
        grads, logs = carry
        pair = tokens // 2 - 1 - back
        u_pair = pair_rows(u_ref, pair, seqs)
        for half in (1, 0):
            token = pair * 2 + half
            step = token_rows(step_ref, token, seqs)
            dy = token_rows(dy_ref, token, seqs)
            u_one = u_pair[half]
            drive = step * u_one
            stop = step + pen[token]
            fresh = []
            fresh_logs = []
            on_b = jnp.zeros((seqs, LANES), F32)
            on_rate = jnp.zeros((seqs, LANES), F32)
            for n in range(states):
                at = token * states + n
                rate = rate_ref[pl.ds(n * seqs, seqs), :]
                decay = jnp.exp2(stop * rate)
                lam = grads[n] + dy * cc[at]
                carried = lam * decay
                fresh.append(carried)
                kept = carried * held[at]
                on_b = on_b + lam * bb[at]
                on_rate = on_rate + kept * rate
                fresh_logs.append(logs[n] + kept * step)
                acc_b[at] = acc_b[at] + lam * drive
                acc_c[at] = acc_c[at] + dy * held[at + states]
            rows = pl.ds(pl.multiple_of(token * seqs, seqs), seqs)
            du_ref[rows, :] = step * on_b
            dstep_ref[rows, :] = on_rate * LN2 + u_one * on_b
            grads = tuple(fresh)
            logs = tuple(fresh_logs)
        return grads, logs

    zero = jnp.zeros((seqs, LANES), F32)
    grads = tuple(last_ref[pl.ds(n * seqs, seqs), :] for n in range(states))
    grads, logs = lax.fori_loop(0, tokens // 2, one, (grads, (zero,) * states))
    for n in range(states):
        dlog_ref[pl.ds(n, 1), :] = jnp.sum(logs[n], axis=0, keepdims=True)

    @pl.when(tile == pl.num_programs(0) - 1)
    def _():
        lane = lax.broadcasted_iota(jnp.int32, (seqs, LANES), 1)

        def gather(token, carry):
            block = jnp.zeros((seqs, LANES), F32)
            for n in range(states):
                sum_b = jnp.sum(acc_b[token * states + n], axis=1, keepdims=True)
                block = jnp.where(lane == n, sum_b, block)
                sum_c = jnp.sum(acc_c[token * states + n], axis=1, keepdims=True)
                block = jnp.where(lane == states + n, sum_c, block)
            dbc_ref[pl.ds(pl.multiple_of(token * seqs, seqs), seqs), :] = block
            return carry

        lax.fori_loop(0, tokens, gather, 0)


def state_call(body, seqs, tokens, states, channels, ins, outs, scratch, cost):
    def spec(shape, shared):
        if shared:
            return pl.BlockSpec(shape, lambda tile: (0, 0))
        return pl.BlockSpec((shape[0], LANES), lambda tile: (0, tile))

    return pl.pallas_call(
        functools.partial(body, seqs, tokens, states),
        grid=(channels // LANES,),
        in_specs=[spec(value.shape, shared) for value, shared in ins],
        out_specs=tuple(spec(value.shape, shared) for value, shared in outs),
        out_shape=tuple(value for value, _ in outs),
        scratch_shapes=[pltpu.VMEM((count, seqs, LANES), F32) for count in scratch],
        compiler_params=pltpu.CompilerParams(vmem_limit_bytes=58 * 1024 * 1024),
        cost_estimate=pl.CostEstimate(flops=cost, bytes_accessed=16 * 1024 * 1024, transcendentals=0),
    )(*[value for value, _ in ins])


def shards(
    x_in,
    seg_ids,
    norm1_gain,
    w_in_x,
    w_in_z,
    conv_w,
    conv_b,
    w_xproj,
    ssm_gain,
    w_dt,
    dt_bias,
    a_log,
    d_skip,
    w_out,
    norm2_gain,
    w_gate,
    w_up,
    w_down,
    d_out,
):
    gathered = lambda value, axis: lax.all_gather(value.astype(BF), "seq", axis=axis, tiled=True)
    full_norm1 = gathered(norm1_gain, 0)
    full_in_x = gathered(w_in_x, 0)
    full_in_z = gathered(w_in_z, 0)
    full_conv_w = gathered(conv_w, 1)
    full_conv_b = gathered(conv_b, 0)
    full_xproj = gathered(w_xproj, 0)
    full_ssm_gain = gathered(ssm_gain, 0)
    full_w_dt = gathered(w_dt, 1)
    full_dt_bias = gathered(dt_bias, 0)
    full_a_log = gathered(a_log, 0)
    full_d_skip = gathered(d_skip, 0)
    full_w_out = gathered(w_out, 1)
    full_norm2 = gathered(norm2_gain, 0)
    full_gate = gathered(w_gate, 0)
    full_up = gathered(w_up, 0)
    full_down = gathered(w_down, 1)
    count = lax.axis_size("seq")
    place = lax.axis_index("seq")
    seqs, tokens, width = x_in.shape
    rows = seqs * tokens
    taps = full_conv_w.shape[0]
    rank = full_w_dt.shape[0]
    states = full_a_log.shape[1]
    channels = full_in_x.shape[1]
    halo = (taps - 1) * seqs
    head_sum = lambda value: lax.psum(value.astype(BF), "head").astype(F32)

    norm1_vec = full_norm1.astype(F32)
    x_rows = x_in.transpose(1, 0, 2).reshape(rows, width).astype(F32)
    ids = seg_ids.T.reshape(rows)
    normed1, scale_one = norm_rows(x_rows, norm1_vec)
    x_norm = normed1.astype(BF)
    x_inner = jnp.dot(x_norm, full_in_x, preferred_element_type=F32).astype(BF)
    z_gate = jnp.dot(x_norm, full_in_z, preferred_element_type=F32)
    prev_tail, prev_ids = shifted((x_inner[rows - halo :], ids[rows - halo :]), "seq", 1)
    extended = jnp.concatenate([prev_tail, x_inner], axis=0).astype(F32)
    ext_ids = jnp.concatenate([prev_ids, ids])
    conv_weight = full_conv_w.astype(F32)
    x_conv = full_conv_b.astype(F32)[None, :]
    same_docs = []
    for offset in range(taps):
        first = (taps - 1 - offset) * seqs
        same = (ext_ids[first : first + rows] == ids).astype(F32)[:, None]
        same_docs.append(same)
        x_conv = x_conv + conv_weight[offset] * extended[first : first + rows] * same
    u_low = jax.nn.silu(x_conv).astype(BF)
    projected = head_sum(jnp.dot(u_low, full_xproj, preferred_element_type=F32))
    ssm_vec = full_ssm_gain.astype(F32)
    b_end = rank + states
    dt_normed, dt_scale = norm_rows(projected[:, :rank], ssm_vec[:rank])
    b_normed, b_scale = norm_rows(projected[:, rank:b_end], ssm_vec[rank:b_end])
    c_normed, c_scale = norm_rows(projected[:, b_end:], ssm_vec[b_end:])
    dt_low = dt_normed.astype(BF)
    dt_pre = jnp.dot(dt_low, full_w_dt, preferred_element_type=F32) + full_dt_bias.astype(F32)
    step = jax.nn.softplus(dt_pre)
    rates = -jnp.exp(full_a_log.astype(F32))
    rate_rows = jnp.repeat((rates * LOG2E).T, seqs, axis=0)
    pen = (1.0 - same_docs[1]) * STOP
    bc = jnp.concatenate(
        [b_normed, c_normed, pen, jnp.zeros((rows, LANES - 2 * states - 1), F32)], axis=1
    )
    run = lambda body, ins, outs, scratch, ops: state_call(
        body, seqs, tokens, states, channels, ins, outs, scratch, ops * rows * channels * states
    )
    shape = jax.ShapeDtypeStruct
    per_token = tokens * states
    state_rows = states * seqs
    local_end, step_sum = run(
        end_kernel,
        [(bc, True), (step, False), (u_low, False), (rate_rows, False)],
        [(shape((state_rows, channels), BF), False), (shape((seqs, channels), F32), False)],
        [per_token, tokens],
        6,
    )
    all_ends = lax.all_gather(local_end, "seq")
    all_sums = lax.all_gather(step_sum, "seq")

    def passed(sum_one):
        whole = sum_one[None] * (rates * LOG2E).T[:, None, :]
        return jnp.exp2(whole).reshape(state_rows, channels)

    start = jnp.zeros((state_rows, channels), F32)
    for source in range(count - 1):
        moved = start * passed(all_sums[source]) + all_ends[source].astype(F32)
        start = jnp.where(source < place, moved, start)
    (y_state,) = run(
        out_kernel,
        [(bc, True), (step, False), (u_low, False), (rate_rows, False), (start, False)],
        [(shape((rows, channels), F32), False)],
        [per_token, per_token, tokens],
        8,
    )
    skip_vec = full_d_skip.astype(F32)
    u_rows = u_low.astype(F32)
    y_full = y_state + skip_vec * u_rows
    silu_z = jax.nn.silu(z_gate)
    g_low = (y_full * silu_z).astype(BF)
    norm2_vec = full_norm2.astype(F32)
    hidden = x_rows + head_sum(jnp.dot(g_low, full_w_out, preferred_element_type=F32))
    normed2, scale_two = norm_rows(hidden, norm2_vec)
    x_norm2 = normed2.astype(BF)
    gate_proj = jnp.dot(x_norm2, full_gate, preferred_element_type=F32)
    up_proj = jnp.dot(x_norm2, full_up, preferred_element_type=F32)
    silu_gate = jax.nn.silu(gate_proj)
    act_low = (silu_gate * up_proj).astype(BF)
    ffn_out = head_sum(jnp.dot(act_low, full_down, preferred_element_type=F32))
    block_out = (hidden + ffn_out).astype(BF).reshape(tokens, seqs, width).transpose(1, 0, 2)
    grad_low = d_out.transpose(1, 0, 2).reshape(rows, width)
    grad_rows = grad_low.astype(F32)
    grad_down = jnp.einsum("rf,rd->fd", act_low, grad_low, preferred_element_type=F32)
    d_act = jnp.einsum("rd,fd->rf", grad_low, full_down, preferred_element_type=F32)
    d_gate = (d_act * up_proj * silu_slope(gate_proj)).astype(BF)
    d_up = (d_act * silu_gate).astype(BF)
    grad_gate = jnp.einsum("rd,rf->df", x_norm2, d_gate, preferred_element_type=F32)
    grad_up = jnp.einsum("rd,rf->df", x_norm2, d_up, preferred_element_type=F32)
    d_norm2 = head_sum(
        jnp.einsum("rf,df->rd", d_gate, full_gate, preferred_element_type=F32)
        + jnp.einsum("rf,df->rd", d_up, full_up, preferred_element_type=F32)
    )
    d_hidden_part, grad_norm2 = norm_back(hidden, scale_two, norm2_vec, d_norm2)
    d_hidden = grad_rows + d_hidden_part
    d_mix = d_hidden.astype(BF)
    grad_out_w = jnp.einsum("re,rd->ed", g_low, d_mix, preferred_element_type=F32)
    d_g = jnp.einsum("rd,ed->re", d_mix, full_w_out, preferred_element_type=F32)
    d_y = d_g * silu_z
    d_z = (d_g * y_full * silu_slope(z_gate)).astype(BF)
    grad_skip = jnp.sum(d_y * u_rows, axis=0)
    (own,) = run(
        own_kernel,
        [(bc, True), (step, False), (d_y, False), (rate_rows, False)],
        [(shape((state_rows, channels), BF), False)],
        [per_token, tokens],
        6,
    )
    all_own = lax.all_gather(own, "seq")
    last = jnp.zeros((state_rows, channels), F32)
    for source in range(count - 1, 0, -1):
        moved = last * passed(all_sums[source]) + all_own[source].astype(F32)
        last = jnp.where(source > place, moved, last)
    d_u_state, d_step, d_bc, d_log = run(
        back_kernel,
        [
            (bc, True),
            (step, False),
            (u_low, False),
            (d_y, False),
            (rate_rows, False),
            (start, False),
            (last, False),
        ],
        [
            (shape((rows, channels), F32), False),
            (shape((rows, channels), F32), False),
            (shape((rows, LANES), F32), True),
            (shape((states, channels), F32), False),
        ],
        [per_token, per_token, tokens, per_token + states, per_token, per_token],
        24,
    )
    grad_alog = d_log.T * rates
    d_pre = d_step * jax.nn.sigmoid(dt_pre)
    grad_bias = jnp.sum(d_pre, axis=0)
    d_pre_low = d_pre.astype(BF)
    grad_step_w = jnp.einsum("rk,re->ke", dt_low, d_pre_low, preferred_element_type=F32)
    d_dt_part = jnp.einsum("re,ke->rk", d_pre_low, full_w_dt, preferred_element_type=F32)
    d_stats = head_sum(jnp.concatenate([d_dt_part, d_bc[:, : 2 * states]], axis=1))
    d_dt_raw, grad_dt_gain = norm_back(
        projected[:, :rank], dt_scale, ssm_vec[:rank], d_stats[:, :rank]
    )
    d_b_raw, grad_b_gain = norm_back(
        projected[:, rank:b_end], b_scale, ssm_vec[rank:b_end], d_stats[:, rank:b_end]
    )
    d_c_raw, grad_c_gain = norm_back(
        projected[:, b_end:], c_scale, ssm_vec[b_end:], d_stats[:, b_end:]
    )
    d_proj = jnp.concatenate([d_dt_raw, d_b_raw, d_c_raw], axis=1)
    grad_ssm = jnp.concatenate([grad_dt_gain, grad_b_gain, grad_c_gain])
    grad_xproj = jnp.einsum("re,rk->ek", u_low, d_proj, preferred_element_type=F32)
    d_u = (
        d_y * skip_vec
        + d_u_state
        + jnp.einsum("rk,ek->re", d_proj, full_xproj, preferred_element_type=F32)
    )
    d_conv = d_u * silu_slope(x_conv)
    grad_conv_b = jnp.sum(d_conv, axis=0)
    d_extended = jnp.zeros((rows + halo, channels), F32)
    conv_grads = []
    for offset in range(taps):
        first = (taps - 1 - offset) * seqs
        masked = d_conv * same_docs[offset]
        conv_grads.append(jnp.sum(masked * extended[first : first + rows], axis=0))
        d_extended = d_extended + jnp.pad(
            conv_weight[offset] * masked, ((first, halo - first), (0, 0))
        )
    grad_conv_w = jnp.stack(conv_grads)
    from_next = shifted(d_extended[:halo].astype(BF), "seq", -1).astype(F32)
    d_inner = d_extended[halo:] + jnp.pad(from_next, ((rows - halo, 0), (0, 0)))
    d_inner_low = d_inner.astype(BF)
    grad_in_x = jnp.einsum("rd,re->de", x_norm, d_inner_low, preferred_element_type=F32)
    grad_in_z = jnp.einsum("rd,re->de", x_norm, d_z, preferred_element_type=F32)
    d_norm1 = head_sum(
        jnp.einsum("re,de->rd", d_inner_low, full_in_x, preferred_element_type=F32)
        + jnp.einsum("re,de->rd", d_z, full_in_z, preferred_element_type=F32)
    )
    d_input_part, grad_norm1 = norm_back(x_rows, scale_one, norm1_vec, d_norm1)
    grad_input = (d_hidden + d_input_part).reshape(tokens, seqs, width).transpose(1, 0, 2)
    scattered = lambda value, axis: lax.psum_scatter(
        value, "seq", scatter_dimension=axis, tiled=True
    )
    shrunk = lambda value, axis: scattered(value.astype(BF), axis).astype(F32)
    return (
        block_out,
        grad_input,
        scattered(grad_norm1, 0),
        shrunk(grad_in_x, 0),
        shrunk(grad_in_z, 0),
        scattered(grad_conv_w, 1),
        scattered(grad_conv_b, 0),
        shrunk(grad_xproj, 0),
        scattered(grad_ssm, 0),
        shrunk(grad_step_w, 1),
        scattered(grad_bias, 0),
        scattered(grad_alog, 0),
        scattered(grad_skip, 0),
        shrunk(grad_out_w, 1),
        scattered(grad_norm2, 0),
        shrunk(grad_gate, 0),
        shrunk(grad_up, 0),
        shrunk(grad_down, 1),
    )


def solution(mesh):
    placed = (
        P(None, "seq", None),
        P(None, "seq"),
        P("seq"),
        P("seq", "head"),
        P("seq", "head"),
        P(None, ("head", "seq")),
        P(("head", "seq")),
        P(("head", "seq"), None),
        P("seq"),
        P(None, ("head", "seq")),
        P(("head", "seq")),
        P(("head", "seq"), None),
        P(("head", "seq")),
        P("head", "seq"),
        P("seq"),
        P("seq", "head"),
        P("seq", "head"),
        P("head", "seq"),
        P(None, "seq", None),
    )
    return jax.shard_map(
        shards,
        mesh=mesh,
        in_specs=placed,
        out_specs=(
            P(None, "seq", None),
            P(None, "seq", None),
            P("seq"),
            P("seq", "head"),
            P("seq", "head"),
            P(None, ("head", "seq")),
            P(("head", "seq")),
            P(("head", "seq"), None),
            P("seq"),
            P(None, ("head", "seq")),
            P(("head", "seq")),
            P(("head", "seq"), None),
            P(("head", "seq")),
            P("head", "seq"),
            P("seq"),
            P("seq", "head"),
            P("seq", "head"),
            P("head", "seq"),
        ),
        check_vma=False,
    )
```

```python
import functools

import jax
import jax.numpy as jnp
from jax import lax
from jax.experimental import pallas as pl
from jax.experimental.pallas import tpu as pltpu
from jax.sharding import PartitionSpec as P

EPS = 1e-06
LOG2E = 1.4426950408889634
LN2 = 0.6931471805599453
STOP = 1e30
LANES = 128
BF = jnp.bfloat16
F32 = jnp.float32


def shifted(value, axis, steps):
    count = lax.axis_size(axis)
    initial, last = (max(0, -steps), min(count, count - steps))
    return lax.ppermute(value, axis, [(source, source + steps) for source in range(initial, last)])


def norm_rows(values, gain_vec):
    inv_rms = lax.rsqrt(jnp.mean(values * values, axis=-1, keepdims=True) + EPS)
    return (values * inv_rms * gain_vec, inv_rms)


def norm_back(values, inv_rms, gain_vec, grad_rows):
    normed = values * inv_rms
    gain_grad = jnp.sum(grad_rows * normed, axis=0)
    scaled = grad_rows * gain_vec
    value_grad = inv_rms * (scaled - normed * jnp.mean(scaled * normed, axis=-1, keepdims=True))
    return (value_grad, gain_grad)


def silu_slope(values):
    logistic = jax.nn.sigmoid(values)
    return logistic * (1.0 + values * (1.0 - logistic))


def spread(column_ref, seqs, tokens, first, count, target):
    def one(token, carry):
        block = column_ref[pl.ds(pl.multiple_of(token * seqs, seqs), seqs), :]
        for n in range(count):
            column = block[:, first + n : first + n + 1]
            target[token * count + n] = jnp.broadcast_to(column, (seqs, LANES))
        return carry

    lax.fori_loop(0, tokens, one, 0)


def pair_rows(ref, pair, seqs):
    both = ref[pl.ds(pl.multiple_of(pair * 2 * seqs, 2 * seqs), 2 * seqs), :]
    both = both.astype(F32)
    return both[:seqs], both[seqs:]


def token_rows(ref, token, seqs):
    return ref[pl.ds(pl.multiple_of(token * seqs, seqs), seqs), :]


def end_kernel(seqs, tokens, states, bc_ref, step_ref, u_ref, rate_ref, end_ref, sum_ref, bb, pen):
    @pl.when(pl.program_id(0) == 0)
    def _():
        spread(bc_ref, seqs, tokens, 0, states, bb)
        spread(bc_ref, seqs, tokens, 2 * states, 1, pen)

    def one(pair, carry):
        state, total = carry
        u_pair = pair_rows(u_ref, pair, seqs)
        for half in range(2):
            token = pair * 2 + half
            step = token_rows(step_ref, token, seqs)
            drive = step * u_pair[half]
            stop = step + pen[token]
            total = total + stop
            fresh = []
            for n in range(states):
                decay = jnp.exp2(stop * rate_ref[pl.ds(n * seqs, seqs), :])
                fresh.append(decay * state[n] + drive * bb[token * states + n])
            state = tuple(fresh)
        return state, total

    zero = jnp.zeros((seqs, LANES), F32)
    state, total = lax.fori_loop(0, tokens // 2, one, ((zero,) * states, zero))
    for n in range(states):
        end_ref[pl.ds(n * seqs, seqs), :] = state[n].astype(end_ref.dtype)
    sum_ref[...] = total


def out_kernel(
    seqs, tokens, states, bc_ref, step_ref, u_ref, rate_ref, start_ref, y_ref, bb, cc, pen
):
    @pl.when(pl.program_id(0) == 0)
    def _():
        spread(bc_ref, seqs, tokens, 0, states, bb)
        spread(bc_ref, seqs, tokens, states, states, cc)
        spread(bc_ref, seqs, tokens, 2 * states, 1, pen)

    def one(pair, state):
        u_pair = pair_rows(u_ref, pair, seqs)
        for half in range(2):
            token = pair * 2 + half
            step = token_rows(step_ref, token, seqs)
            drive = step * u_pair[half]
            stop = step + pen[token]
            fresh = []
            out = jnp.zeros((seqs, LANES), F32)
            for n in range(states):
                decay = jnp.exp2(stop * rate_ref[pl.ds(n * seqs, seqs), :])
                value = decay * state[n] + drive * bb[token * states + n]
                out = out + value * cc[token * states + n]
                fresh.append(value)
            y_ref[pl.ds(pl.multiple_of(token * seqs, seqs), seqs), :] = out
            state = tuple(fresh)
        return state

    initial = tuple(start_ref[pl.ds(n * seqs, seqs), :] for n in range(states))
    lax.fori_loop(0, tokens // 2, one, initial)


def own_kernel(seqs, tokens, states, bc_ref, step_ref, dy_ref, rate_ref, own_ref, cc, pen):
    @pl.when(pl.program_id(0) == 0)
    def _():
        spread(bc_ref, seqs, tokens, states, states, cc)
        spread(bc_ref, seqs, tokens, 2 * states, 1, pen)

    def one(back, grads):
        for half in range(2):
            token = tokens - 1 - (back * 2 + half)
            stop = token_rows(step_ref, token, seqs) + pen[token]
            dy = token_rows(dy_ref, token, seqs)
            fresh = []
            for n in range(states):
                decay = jnp.exp2(stop * rate_ref[pl.ds(n * seqs, seqs), :])
                fresh.append(decay * (grads[n] + dy * cc[token * states + n]))
            grads = tuple(fresh)
        return grads

    zero = jnp.zeros((seqs, LANES), F32)
    grads = lax.fori_loop(0, tokens // 2, one, (zero,) * states)
    for n in range(states):
        own_ref[pl.ds(n * seqs, seqs), :] = grads[n].astype(own_ref.dtype)


def back_kernel(
    seqs,
    tokens,
    states,
    bc_ref,
    step_ref,
    u_ref,
    dy_ref,
    rate_ref,
    start_ref,
    last_ref,
    du_ref,
    dstep_ref,
    dbc_ref,
    dlog_ref,
    bb,
    cc,
    pen,
    held,
    acc_b,
    acc_c,
):
    tile = pl.program_id(0)

    @pl.when(tile == 0)
    def _():
        spread(bc_ref, seqs, tokens, 0, states, bb)
        spread(bc_ref, seqs, tokens, states, states, cc)
        spread(bc_ref, seqs, tokens, 2 * states, 1, pen)

        def clear(token, carry):
            for n in range(states):
                acc_b[token * states + n] = jnp.zeros((seqs, LANES), F32)
                acc_c[token * states + n] = jnp.zeros((seqs, LANES), F32)
            return carry

        lax.fori_loop(0, tokens, clear, 0)

    def again(pair, state):
        u_pair = pair_rows(u_ref, pair, seqs)
        for half in range(2):
            token = pair * 2 + half
            step = token_rows(step_ref, token, seqs)
            drive = step * u_pair[half]
            stop = step + pen[token]
            fresh = []
            for n in range(states):
                held[token * states + n] = state[n]
                decay = jnp.exp2(stop * rate_ref[pl.ds(n * seqs, seqs), :])
                fresh.append(decay * state[n] + drive * bb[token * states + n])
            state = tuple(fresh)
        return state

    initial = tuple(start_ref[pl.ds(n * seqs, seqs), :] for n in range(states))
    state = lax.fori_loop(0, tokens // 2, again, initial)
    for n in range(states):
        held[tokens * states + n] = state[n]

    def one(back, carry):
        grads, logs = carry
        pair = tokens // 2 - 1 - back
        u_pair = pair_rows(u_ref, pair, seqs)
        for half in (1, 0):
            token = pair * 2 + half
            step = token_rows(step_ref, token, seqs)
            dy = token_rows(dy_ref, token, seqs)
            u_one = u_pair[half]
            drive = step * u_one
            stop = step + pen[token]
            fresh = []
            fresh_logs = []
            on_b = jnp.zeros((seqs, LANES), F32)
            on_rate = jnp.zeros((seqs, LANES), F32)
            for n in range(states):
                at = token * states + n
                rate = rate_ref[pl.ds(n * seqs, seqs), :]
                decay = jnp.exp2(stop * rate)
                lam = grads[n] + dy * cc[at]
                carried = lam * decay
                fresh.append(carried)
                kept = carried * held[at]
                on_b = on_b + lam * bb[at]
                on_rate = on_rate + kept * rate
                fresh_logs.append(logs[n] + kept * step)
                acc_b[at] = acc_b[at] + lam * drive
                acc_c[at] = acc_c[at] + dy * held[at + states]
            rows = pl.ds(pl.multiple_of(token * seqs, seqs), seqs)
            du_ref[rows, :] = step * on_b
            dstep_ref[rows, :] = on_rate * LN2 + u_one * on_b
            grads = tuple(fresh)
            logs = tuple(fresh_logs)
        return grads, logs

    zero = jnp.zeros((seqs, LANES), F32)
    grads = tuple(last_ref[pl.ds(n * seqs, seqs), :] for n in range(states))
    grads, logs = lax.fori_loop(0, tokens // 2, one, (grads, (zero,) * states))
    for n in range(states):
        dlog_ref[pl.ds(n, 1), :] = jnp.sum(logs[n], axis=0, keepdims=True)

    @pl.when(tile == pl.num_programs(0) - 1)
    def _():
        lane = lax.broadcasted_iota(jnp.int32, (seqs, LANES), 1)

        def gather(token, carry):
            block = jnp.zeros((seqs, LANES), F32)
            for n in range(states):
                sum_b = jnp.sum(acc_b[token * states + n], axis=1, keepdims=True)
                block = jnp.where(lane == n, sum_b, block)
                sum_c = jnp.sum(acc_c[token * states + n], axis=1, keepdims=True)
                block = jnp.where(lane == states + n, sum_c, block)
            dbc_ref[pl.ds(pl.multiple_of(token * seqs, seqs), seqs), :] = block
            return carry

        lax.fori_loop(0, tokens, gather, 0)


def state_call(body, seqs, tokens, states, channels, ins, outs, scratch, cost):
    def spec(shape, shared):
        if shared:
            return pl.BlockSpec(shape, lambda tile: (0, 0))
        return pl.BlockSpec((shape[0], LANES), lambda tile: (0, tile))

    return pl.pallas_call(
        functools.partial(body, seqs, tokens, states),
        grid=(channels // LANES,),
        in_specs=[spec(value.shape, shared) for value, shared in ins],
        out_specs=tuple(spec(value.shape, shared) for value, shared in outs),
        out_shape=tuple(value for value, _ in outs),
        scratch_shapes=[pltpu.VMEM((count, seqs, LANES), F32) for count in scratch],
        compiler_params=pltpu.CompilerParams(vmem_limit_bytes=58 * 1024 * 1024),
        cost_estimate=pl.CostEstimate(flops=cost, bytes_accessed=16 * 1024 * 1024, transcendentals=0),
    )(*[value for value, _ in ins])


def pairs_of(axis):
    return lax.axis_size(axis) // 2


def hop(value, steps):
    count = lax.axis_size("seq")
    return lax.ppermute(value, "seq", [(s, (s + 2 * steps) % count) for s in range(count)])


def swap(value, axis, bit):
    return lax.ppermute(value, axis, [(s, s ^ bit) for s in range(lax.axis_size(axis))])


def gather_rows(value):
    size = value.shape[0]
    place = lax.axis_index("seq")
    around = pairs_of("seq")
    low, high = place % 2, place // 2
    own = [value] + [hop(value, steps) for steps in range(1, around)]
    other = [swap(part, "seq", 1) for part in own]
    full = jnp.zeros((2 * around * size,) + value.shape[1:], value.dtype)
    for steps in range(around):
        source = (high - steps + around) % around * 2
        full = lax.dynamic_update_slice_in_dim(full, own[steps], (source + low) * size, 0)
        full = lax.dynamic_update_slice_in_dim(full, other[steps], (source + 1 - low) * size, 0)
    return full


def scatter_rows(value, kind=BF):
    place = lax.axis_index("seq")
    around = pairs_of("seq")
    low, high = place % 2, place // 2
    size = value.shape[0] // (2 * around)
    blocks = value.astype(kind).reshape((around, 2, size) + value.shape[1:])
    theirs = lax.dynamic_index_in_dim(blocks, 1 - low, 1, False)
    mine = lax.dynamic_index_in_dim(blocks, low, 1, False)
    half = mine.astype(F32) + swap(theirs, "seq", 1).astype(F32)
    total = lax.dynamic_index_in_dim(half, high, 0, False)
    half = half.astype(kind)
    for steps in range(1, around):
        part = lax.dynamic_index_in_dim(half, (high + steps) % around, 0, False)
        total = total + hop(part, steps).astype(F32)
    return total


def head_bits():
    return (lax.axis_size("head") - 1).bit_length()


def head_scatter(value):
    place = lax.axis_index("head")
    for k in range(head_bits()):
        bit = place // 2**k % 2
        halves = value.astype(BF).reshape((2, value.shape[0] // 2) + value.shape[1:])
        keep = lax.dynamic_index_in_dim(halves, bit, 0, False)
        send = lax.dynamic_index_in_dim(halves, 1 - bit, 0, False)
        value = keep.astype(F32) + swap(send, "head", 2**k).astype(F32)
    return value


def head_part(value):
    place = lax.axis_index("head")
    for k in range(head_bits()):
        size = value.shape[0] // 2
        value = lax.dynamic_slice_in_dim(value, place // 2**k % 2 * size, size, 0)
    return value


def head_gather(value):
    place = lax.axis_index("head")
    for k in reversed(range(head_bits())):
        got = swap(value, "head", 2**k)
        first = (place // 2**k % 2 == 0)
        value = jnp.concatenate([jnp.where(first, value, got), jnp.where(first, got, value)])
    return value


def head_total(value, kind):
    for k in range(head_bits()):
        value = value.astype(kind)
        value = value.astype(F32) + swap(value, "head", 2**k).astype(F32)
    return value


def first_kernel(count, *refs):
    kinds = (len(refs) - 5) // 2
    sources, targets = refs[:kinds], refs[kinds : 2 * kinds]
    hop_send, hop_recv, swap_send, swap_recv, local_sem = refs[2 * kinds :]
    place = lax.axis_index("seq")
    around = count // 2
    low, high = lax.rem(place, 2), place // 2
    mate = high * 2 + 1 - low
    at = lambda steps: lax.rem(high + steps + around, around) * 2 + low
    barrier = pltpu.get_barrier_semaphore()

    def greet(device):
        pl.semaphore_signal(
            barrier, inc=1, device_id={"seq": device}, device_id_type=pl.DeviceIdType.MESH
        )

    for steps in range(1, around):
        greet(at(steps))
    greet(mate)
    pl.semaphore_wait(barrier, around)

    def send(source, target, sems, device):
        copy = pltpu.make_async_remote_copy(
            src_ref=source,
            dst_ref=target,
            send_sem=sems[0],
            recv_sem=sems[1],
            device_id={"seq": device},
            device_id_type=pl.DeviceIdType.MESH,
        )
        copy.start()
        return copy

    hops, swaps, own = {}, {}, []
    for k in range(kinds):
        copy = pltpu.make_async_copy(sources[k], targets[k].at[place], local_sem.at[k])
        copy.start()
        own.append(copy)
        for steps in range(1, around):
            sems = hop_send.at[k, steps], hop_recv.at[k, steps]
            hops[k, steps] = send(sources[k], targets[k].at[place], sems, at(steps))
        sems = swap_send.at[k, 0], swap_recv.at[k, 0]
        swaps[k, 0] = send(sources[k], targets[k].at[place], sems, mate)
    for k in range(kinds):
        for steps in range(1, around):
            hops[k, steps].wait_recv()
            block = targets[k].at[at(-steps)]
            sems = swap_send.at[k, steps], swap_recv.at[k, steps]
            swaps[k, steps] = send(block, block, sems, mate)
    for k in range(kinds):
        own[k].wait()
        for steps in range(1, around):
            hops[k, steps].wait_send()
        for steps in range(around):
            swaps[k, steps].wait()


def first_gather(*values):
    count = lax.axis_size("seq")
    around = count // 2
    kinds = len(values)
    sems = pltpu.SemaphoreType.DMA
    return pl.pallas_call(
        functools.partial(first_kernel, count),
        out_shape=tuple(jax.ShapeDtypeStruct((count,) + v.shape, v.dtype) for v in values),
        in_specs=[pl.BlockSpec(memory_space=pl.ANY)] * kinds,
        out_specs=tuple([pl.BlockSpec(memory_space=pl.ANY)] * kinds),
        scratch_shapes=[sems((kinds, around))] * 4 + [sems((kinds,))],
        compiler_params=pltpu.CompilerParams(collective_id=0, has_side_effects=True),
    )(*values)


def shards(
    x_in,
    seg_ids,
    norm1_gain,
    w_in_x,
    w_in_z,
    conv_w,
    conv_b,
    w_xproj,
    ssm_gain,
    w_dt,
    dt_bias,
    a_log,
    d_skip,
    w_out,
    norm2_gain,
    w_gate,
    w_up,
    w_down,
    d_out,
):
    count = lax.axis_size("seq")
    place = lax.axis_index("seq")
    seqs, tokens, width = x_in.shape
    rows = seqs * tokens
    taps = conv_w.shape[0]
    rank = w_dt.shape[0]
    states = a_log.shape[1]
    channels = w_in_x.shape[1]
    halo = (taps - 1) * seqs

    per = channels // count
    fields = [w_xproj, w_dt.T, a_log, conv_w.T, conv_b[:, None], dt_bias[:, None], d_skip[:, None]]
    starts = [0]
    for field in fields:
        starts.append(starts[-1] + field.shape[1])
    pack_width = -(-starts[-1] // LANES) * LANES
    gains = [norm1_gain, norm2_gain, ssm_gain]
    gain_starts = [0]
    for gain in gains:
        gain_starts.append(gain_starts[-1] + gain.shape[0])
    pack_rows = -(-(per + -(-gain_starts[-1] // pack_width)) // 16) * 16

    def pack(channel_fields, gain_fields):
        table = jnp.concatenate([f.astype(F32) for f in channel_fields], axis=1)
        table = jnp.pad(table, ((0, 0), (0, pack_width - table.shape[1])))
        table = table.reshape(-1, per, pack_width)
        rest = jnp.concatenate([g.astype(F32).reshape(table.shape[0], -1) for g in gain_fields], 1)
        rest = jnp.pad(rest, ((0, 0), (0, (pack_rows - per) * pack_width - rest.shape[1])))
        return jnp.concatenate([table, rest.reshape(-1, pack_rows - per, pack_width)], axis=1)

    def unpack(block):
        table = block[:, :per].reshape(-1, pack_width)
        rest = block[:, per:].reshape(block.shape[0], -1)
        return (
            [table[:, starts[k] : starts[k + 1]] for k in range(len(fields))],
            [rest[:, gain_starts[k] : gain_starts[k + 1]].reshape(-1) for k in range(len(gains))],
        )

    in_x_blocks, pack_blocks = first_gather(w_in_x.astype(BF), pack(fields, gains)[0].astype(BF))
    full_in_x = in_x_blocks.reshape(width, channels)
    fulls, full_gains = unpack(pack_blocks)
    full_xproj, w_dt_cols, full_a_log, conv_cols, conv_b_col, bias_col, skip_col = fulls
    full_w_dt = w_dt_cols.T
    full_conv_w = conv_cols.T
    full_conv_b, full_dt_bias, full_d_skip = conv_b_col[:, 0], bias_col[:, 0], skip_col[:, 0]
    full_norm1, full_norm2, full_ssm_gain = full_gains

    w_mix = jnp.concatenate([w_in_z.astype(BF), w_out.astype(BF).T], axis=1)
    w_ffn = jnp.concatenate([w_gate.astype(BF), w_up.astype(BF), w_down.astype(BF).T], axis=1)
    w_mix, w_ffn, full_in_x = lax.optimization_barrier((w_mix, w_ffn, full_in_x))
    full_mix = gather_rows(w_mix)
    full_ffn = gather_rows(w_ffn)
    full_in_z, full_out_t = full_mix[:, :channels], full_mix[:, channels:]
    hidden_units = w_gate.shape[1]
    full_gate, full_up, full_down_t = (
        full_ffn[:, k * hidden_units : (k + 1) * hidden_units] for k in range(3)
    )

    norm1_vec = full_norm1.astype(F32)
    x_rows = x_in.transpose(1, 0, 2).reshape(rows, width).astype(F32)
    ids = seg_ids.T.reshape(rows)
    normed1, scale_one = norm_rows(x_rows, norm1_vec)
    x_norm = normed1.astype(BF)
    x_inner = jnp.dot(x_norm, full_in_x, preferred_element_type=F32).astype(BF)
    z_gate = jnp.dot(x_norm, full_in_z, preferred_element_type=F32)
    prev_tail, prev_ids = shifted((x_inner[rows - halo :], ids[rows - halo :]), "seq", 1)
    extended = jnp.concatenate([prev_tail, x_inner], axis=0).astype(F32)
    ext_ids = jnp.concatenate([prev_ids, ids])
    conv_weight = full_conv_w.astype(F32)
    x_conv = full_conv_b.astype(F32)[None, :]
    same_docs = []
    for offset in range(taps):
        first = (taps - 1 - offset) * seqs
        same = (ext_ids[first : first + rows] == ids).astype(F32)[:, None]
        same_docs.append(same)
        x_conv = x_conv + conv_weight[offset] * extended[first : first + rows] * same
    u_low = jax.nn.silu(x_conv).astype(BF)
    projected = head_total(jnp.dot(u_low, full_xproj, preferred_element_type=F32), BF)
    ssm_vec = full_ssm_gain.astype(F32)
    b_end = rank + states
    dt_normed, dt_scale = norm_rows(projected[:, :rank], ssm_vec[:rank])
    b_normed, b_scale = norm_rows(projected[:, rank:b_end], ssm_vec[rank:b_end])
    c_normed, c_scale = norm_rows(projected[:, b_end:], ssm_vec[b_end:])
    dt_low = dt_normed.astype(BF)
    dt_pre = jnp.dot(dt_low, full_w_dt, preferred_element_type=F32) + full_dt_bias.astype(F32)
    step = jax.nn.softplus(dt_pre)
    rates = -jnp.exp(full_a_log.astype(F32))
    rate_rows = jnp.repeat((rates * LOG2E).T, seqs, axis=0)
    pen = (1.0 - same_docs[1]) * STOP
    bc = jnp.concatenate(
        [b_normed, c_normed, pen, jnp.zeros((rows, LANES - 2 * states - 1), F32)], axis=1
    )
    run = lambda body, ins, outs, scratch, ops: state_call(
        body, seqs, tokens, states, channels, ins, outs, scratch, ops * rows * channels * states
    )
    shape = jax.ShapeDtypeStruct
    per_token = tokens * states
    state_rows = states * seqs
    local_end, step_sum = run(
        end_kernel,
        [(bc, True), (step, False), (u_low, False), (rate_rows, False)],
        [(shape((state_rows, channels), BF), False), (shape((seqs, channels), F32), False)],
        [per_token, tokens],
        6,
    )
    all_ends = lax.all_gather(local_end, "seq")
    all_sums = lax.all_gather(step_sum, "seq")

    def passed(sum_one):
        whole = sum_one[None] * (rates * LOG2E).T[:, None, :]
        return jnp.exp2(whole).reshape(state_rows, channels)

    start = jnp.zeros((state_rows, channels), F32)
    for source in range(count - 1):
        moved = start * passed(all_sums[source]) + all_ends[source].astype(F32)
        start = jnp.where(source < place, moved, start)
    (y_state,) = run(
        out_kernel,
        [(bc, True), (step, False), (u_low, False), (rate_rows, False), (start, False)],
        [(shape((rows, channels), F32), False)],
        [per_token, per_token, tokens],
        8,
    )
    skip_vec = full_d_skip.astype(F32)
    u_rows = u_low.astype(F32)
    y_full = y_state + skip_vec * u_rows
    silu_z = jax.nn.silu(z_gate)
    g_low = (y_full * silu_z).astype(BF)
    norm2_vec = full_norm2.astype(F32)
    mixed = jnp.einsum("re,de->rd", g_low, full_out_t, preferred_element_type=F32)
    hidden = head_part(x_rows) + head_scatter(mixed)
    normed2, scale_two = norm_rows(hidden, norm2_vec)
    x_norm2 = head_gather(normed2.astype(BF))
    gate_proj = jnp.dot(x_norm2, full_gate, preferred_element_type=F32)
    up_proj = jnp.dot(x_norm2, full_up, preferred_element_type=F32)
    silu_gate = jax.nn.silu(gate_proj)
    act_low = (silu_gate * up_proj).astype(BF)
    ffn_part = jnp.einsum("rf,df->rd", act_low, full_down_t, preferred_element_type=F32)
    block_rows = head_gather((hidden + head_scatter(ffn_part)).astype(BF))
    block_out = block_rows.reshape(tokens, seqs, width).transpose(1, 0, 2)
    grad_low = d_out.transpose(1, 0, 2).reshape(rows, width)
    grad_rows = grad_low.astype(F32)
    grad_down = jnp.einsum("rd,rf->df", grad_low, act_low, preferred_element_type=F32)
    d_act = jnp.dot(grad_low, full_down_t, preferred_element_type=F32)
    d_gate = (d_act * up_proj * silu_slope(gate_proj)).astype(BF)
    d_up = (d_act * silu_gate).astype(BF)
    grad_gate = jnp.einsum("rd,rf->df", x_norm2, d_gate, preferred_element_type=F32)
    grad_up = jnp.einsum("rd,rf->df", x_norm2, d_up, preferred_element_type=F32)
    d_norm2 = head_scatter(
        jnp.einsum("rf,df->rd", d_gate, full_gate, preferred_element_type=F32)
        + jnp.einsum("rf,df->rd", d_up, full_up, preferred_element_type=F32)
    )
    d_hidden_part, grad_norm2 = norm_back(hidden, scale_two, norm2_vec, d_norm2)
    d_hidden = head_part(grad_rows) + d_hidden_part
    d_mix = head_gather(d_hidden.astype(BF))
    grad_out_w = jnp.einsum("rd,re->de", d_mix, g_low, preferred_element_type=F32)
    d_g = jnp.dot(d_mix, full_out_t, preferred_element_type=F32)
    d_y = d_g * silu_z
    d_z = (d_g * y_full * silu_slope(z_gate)).astype(BF)
    grad_skip = jnp.sum(d_y * u_rows, axis=0)
    (own,) = run(
        own_kernel,
        [(bc, True), (step, False), (d_y, False), (rate_rows, False)],
        [(shape((state_rows, channels), BF), False)],
        [per_token, tokens],
        6,
    )
    all_own = lax.all_gather(own, "seq")
    last = jnp.zeros((state_rows, channels), F32)
    for source in range(count - 1, 0, -1):
        moved = last * passed(all_sums[source]) + all_own[source].astype(F32)
        last = jnp.where(source > place, moved, last)
    d_u_state, d_step, d_bc, d_log = run(
        back_kernel,
        [
            (bc, True),
            (step, False),
            (u_low, False),
            (d_y, False),
            (rate_rows, False),
            (start, False),
            (last, False),
        ],
        [
            (shape((rows, channels), F32), False),
            (shape((rows, channels), F32), False),
            (shape((rows, LANES), F32), True),
            (shape((states, channels), F32), False),
        ],
        [per_token, per_token, tokens, per_token + states, per_token, per_token],
        24,
    )
    grad_alog = d_log.T * rates
    d_pre = d_step * jax.nn.sigmoid(dt_pre)
    grad_bias = jnp.sum(d_pre, axis=0)
    d_pre_low = d_pre.astype(BF)
    grad_step_w = jnp.einsum("rk,re->ke", dt_low, d_pre_low, preferred_element_type=F32)
    d_dt_part = jnp.einsum("re,ke->rk", d_pre_low, full_w_dt, preferred_element_type=F32)
    d_stats = head_total(jnp.concatenate([d_dt_part, d_bc[:, : 2 * states]], axis=1), BF)
    d_dt_raw, grad_dt_gain = norm_back(
        projected[:, :rank], dt_scale, ssm_vec[:rank], d_stats[:, :rank]
    )
    d_b_raw, grad_b_gain = norm_back(
        projected[:, rank:b_end], b_scale, ssm_vec[rank:b_end], d_stats[:, rank:b_end]
    )
    d_c_raw, grad_c_gain = norm_back(
        projected[:, b_end:], c_scale, ssm_vec[b_end:], d_stats[:, b_end:]
    )
    d_proj = jnp.concatenate([d_dt_raw, d_b_raw, d_c_raw], axis=1)
    grad_ssm = jnp.concatenate([grad_dt_gain, grad_b_gain, grad_c_gain])
    grad_xproj = jnp.einsum("re,rk->ek", u_low, d_proj, preferred_element_type=F32)
    d_u = (
        d_y * skip_vec
        + d_u_state
        + jnp.einsum("rk,ek->re", d_proj, full_xproj, preferred_element_type=F32)
    )
    d_conv = d_u * silu_slope(x_conv)
    grad_conv_b = jnp.sum(d_conv, axis=0)
    d_extended = jnp.zeros((rows + halo, channels), F32)
    conv_grads = []
    for offset in range(taps):
        first = (taps - 1 - offset) * seqs
        masked = d_conv * same_docs[offset]
        conv_grads.append(jnp.sum(masked * extended[first : first + rows], axis=0))
        d_extended = d_extended + jnp.pad(
            conv_weight[offset] * masked, ((first, halo - first), (0, 0))
        )
    grad_conv_w = jnp.stack(conv_grads)
    from_next = shifted(d_extended[:halo].astype(BF), "seq", -1).astype(F32)
    d_inner = d_extended[halo:] + jnp.pad(from_next, ((rows - halo, 0), (0, 0)))
    d_inner_low = d_inner.astype(BF)
    grad_in_x = jnp.einsum("rd,re->de", x_norm, d_inner_low, preferred_element_type=F32)
    grad_in_z = jnp.einsum("rd,re->de", x_norm, d_z, preferred_element_type=F32)
    d_norm1 = head_scatter(
        jnp.einsum("re,de->rd", d_inner_low, full_in_x, preferred_element_type=F32)
        + jnp.einsum("re,de->rd", d_z, full_in_z, preferred_element_type=F32)
    )
    d_input_part, grad_norm1 = norm_back(head_part(x_rows), head_part(scale_one), norm1_vec, d_norm1)
    input_rows = head_gather((d_hidden + d_input_part).astype(BF)).astype(F32)
    grad_input = input_rows.reshape(tokens, seqs, width).transpose(1, 0, 2)

    grad_ssm = grad_ssm * (lax.axis_index("head") == 0).astype(F32)
    small = pack(
        [
            grad_xproj,
            grad_step_w.T,
            grad_alog,
            grad_conv_w.T,
            grad_conv_b[:, None],
            grad_bias[:, None],
            grad_skip[:, None],
        ],
        [grad_norm1, grad_norm2, grad_ssm],
    )
    small = scatter_rows(small.reshape(-1, pack_width), F32)
    small = jnp.concatenate([small[:per], head_total(small[per:], F32)])[None]
    small_fields, small_gains = unpack(small)
    own_down = scatter_rows(grad_down)
    own_gate = scatter_rows(grad_gate)
    own_up = scatter_rows(grad_up)
    own_out = scatter_rows(grad_out_w)
    own_in_z = scatter_rows(grad_in_z)
    own_in_x = scatter_rows(grad_in_x)
    return (
        block_out,
        grad_input,
        small_gains[0],
        own_in_x,
        own_in_z,
        small_fields[3].T,
        small_fields[4][:, 0],
        small_fields[0],
        small_gains[2],
        small_fields[1].T,
        small_fields[5][:, 0],
        small_fields[2],
        small_fields[6][:, 0],
        own_out.T,
        small_gains[1],
        own_gate,
        own_up,
        own_down.T,
    )


def solution(mesh):
    placed = (
        P(None, "seq", None),
        P(None, "seq"),
        P("seq"),
        P("seq", "head"),
        P("seq", "head"),
        P(None, ("head", "seq")),
        P(("head", "seq")),
        P(("head", "seq"), None),
        P("seq"),
        P(None, ("head", "seq")),
        P(("head", "seq")),
        P(("head", "seq"), None),
        P(("head", "seq")),
        P("head", "seq"),
        P("seq"),
        P("seq", "head"),
        P("seq", "head"),
        P("head", "seq"),
        P(None, "seq", None),
    )
    return jax.shard_map(
        shards,
        mesh=mesh,
        in_specs=placed,
        out_specs=(
            P(None, "seq", None),
            P(None, "seq", None),
            P("seq"),
            P("seq", "head"),
            P("seq", "head"),
            P(None, ("head", "seq")),
            P(("head", "seq")),
            P(("head", "seq"), None),
            P("seq"),
            P(None, ("head", "seq")),
            P(("head", "seq")),
            P(("head", "seq"), None),
            P(("head", "seq")),
            P("head", "seq"),
            P("seq"),
            P("seq", "head"),
            P("seq", "head"),
            P("head", "seq"),
        ),
        check_vma=False,
    )
```

```python
import functools

import jax
import jax.numpy as jnp
from jax import lax
from jax.experimental import pallas as pl
from jax.experimental.pallas import tpu as pltpu
from jax.sharding import PartitionSpec as P

EPS = 1e-06
LOG2E = 1.4426950408889634
LN2 = 0.6931471805599453
STOP = 1e30
LANES = 128
BF = jnp.bfloat16
F32 = jnp.float32


def shifted(value, axis, steps):
    count = lax.axis_size(axis)
    initial, last = (max(0, -steps), min(count, count - steps))
    return lax.ppermute(value, axis, [(source, source + steps) for source in range(initial, last)])


def norm_rows(values, gain_vec):
    inv_rms = lax.rsqrt(jnp.mean(values * values, axis=-1, keepdims=True) + EPS)
    return (values * inv_rms * gain_vec, inv_rms)


def norm_back(values, inv_rms, gain_vec, grad_rows):
    normed = values * inv_rms
    gain_grad = jnp.sum(grad_rows * normed, axis=0)
    scaled = grad_rows * gain_vec
    value_grad = inv_rms * (scaled - normed * jnp.mean(scaled * normed, axis=-1, keepdims=True))
    return (value_grad, gain_grad)


def silu_slope(values):
    logistic = jax.nn.sigmoid(values)
    return logistic * (1.0 + values * (1.0 - logistic))


GROUP = 4


def at_rows(index, size):
    return pl.ds(pl.multiple_of(index * size, size), size)


def spread(parts_ref, states, target):
    rows = parts_ref.shape[0]
    wide = 2 * LANES
    chunk = 256 if rows % 256 == 0 else rows
    source = lax.broadcasted_iota(jnp.int32, (LANES, wide), 0)
    half = lax.broadcasted_iota(jnp.int32, (LANES, wide), 1) // LANES
    columns = 2 * states

    def one(pair, carry):
        column = pair * 2 + half
        third = source % columns == column
        hot = jnp.where((source < 3 * columns) & third, 1.0, 0.0)
        stop = (column == columns) & (source == 3 * columns)
        hot = jnp.where(stop, 1.0, hot).astype(BF)
        for k in range(rows // chunk):
            target[pl.ds(k * chunk, chunk), at_rows(pair, wide)] = jnp.dot(
                parts_ref[pl.ds(k * chunk, chunk), :], hot, preferred_element_type=F32
            )
        return carry

    lax.fori_loop(0, states + 1, one, 0)


def group_tokens(ref, group, lanes, seqs):
    both = ref[at_rows(group, GROUP * seqs), lanes].astype(F32)
    return [both[k * seqs : (k + 1) * seqs] for k in range(GROUP)]


class Exchange:
    def __init__(self, count, forward, arrays, sems):
        place = lax.axis_index("seq")
        self.around = count // 2
        self.low, self.high = lax.rem(place, 2), place // 2
        self.place = place
        self.forward = forward
        self.arrays = arrays
        self.sems = sems
        self.mate = self.high * 2 + 1 - self.low

    def copies(self, steps, tile, source, device, kind):
        send, recv = self.sems[2 * kind], self.sems[2 * kind + 1]
        lanes = at_rows(tile, LANES)
        return [
            pltpu.make_async_remote_copy(
                src_ref=array.at[source, :, lanes],
                dst_ref=array.at[source, :, lanes],
                send_sem=send.at[k, steps, tile],
                recv_sem=recv.at[k, steps, tile],
                device_id={"seq": device},
                device_id_type=pl.DeviceIdType.MESH,
            )
            for k, array in enumerate(self.arrays)
        ]

    def away(self, steps):
        return self.high + steps if self.forward else self.high - steps

    def inside(self, pair):
        return pair < self.around if self.forward else pair >= 0

    def behind(self, steps):
        return self.high - steps if self.forward else self.high + steps

    def has_behind(self, steps):
        pair = self.behind(steps)
        return pair >= 0 if self.forward else pair < self.around

    def gives(self):
        return self.low == (0 if self.forward else 1)

    def hop(self, steps, tile):
        pair = jnp.clip(self.away(steps), 0, self.around - 1)
        return self.copies(steps, tile, self.place, pair * 2 + self.low, 0)

    def relay(self, steps, tile):
        pair = jnp.clip(self.behind(steps), 0, self.around - 1)
        return self.copies(steps, tile, pair * 2 + self.low, self.mate, 1)

    def start(self, tile):
        for steps in range(1, self.around):

            @pl.when(self.inside(self.away(steps)))
            def _():
                for copy in self.hop(steps, tile):
                    copy.start()

        @pl.when(self.gives())
        def _():
            for copy in self.relay(0, tile):
                copy.start()

    def pass_on(self, tile):
        for steps in range(1, self.around):

            @pl.when(self.has_behind(steps))
            def _():
                for copy in self.hop(steps, tile):
                    copy.wait_recv()
                for copy in self.relay(steps, tile):
                    copy.start()

    def arrive(self, tile):
        @pl.when(jnp.logical_not(self.gives()))
        def _():
            for copy in self.relay(0, tile):
                copy.wait_recv()

        for steps in range(1, self.around):

            @pl.when(self.has_behind(steps))
            def _():
                for copy in self.relay(steps, tile):
                    copy.wait_recv()

    def finish(self, tile):
        @pl.when(self.gives())
        def _():
            for copy in self.relay(0, tile):
                copy.wait_send()

        for steps in range(1, self.around):

            @pl.when(self.inside(self.away(steps)))
            def _():
                for copy in self.hop(steps, tile):
                    copy.wait_send()

            @pl.when(self.has_behind(steps))
            def _():
                for copy in self.relay(steps, tile):
                    copy.wait_send()


def chained(state, block_ref, sums_ref, rate_ref, source, lanes, seqs):
    total = sums_ref[source, :, lanes]
    block = block_ref[source, :, lanes].astype(F32)
    after = []
    for n in range(len(state)):
        decay = jnp.exp2(total * rate_ref[pl.ds(n * seqs, seqs), lanes])
        after.append(decay * state[n] + block[n * seqs : (n + 1) * seqs])
    return tuple(after)


def state_blocks(ref, lanes, seqs, states):
    return tuple(ref[pl.ds(n * seqs, seqs), lanes] for n in range(states))


def put_blocks(ref, lead, lanes, blocks):
    stacked = jnp.concatenate(blocks, axis=0)
    if lead is None:
        ref[:, lanes] = stacked.astype(ref.dtype)
    else:
        ref[lead, :, lanes] = stacked.astype(ref.dtype)


def entry_kernel(
    count, seqs, states, parts_ref, step_ref, u_ref, rate_ref, start_ref, sum_ref, *scratch
):
    spread_ref, ends, sums, *sems = scratch
    rows, channels = step_ref.shape
    tokens, tiles = rows // seqs, channels // LANES
    stop_lanes = pl.ds(2 * states * LANES, LANES)
    exchange = Exchange(count, True, (ends, sums), sems)
    place = exchange.place
    zero = jnp.zeros((seqs, LANES), F32)
    greet_pairs(count)
    spread(parts_ref, states, spread_ref)

    def local(tile, carry):
        lanes = at_rows(tile, LANES)

        def one(group, carry):
            state, total = carry
            us = group_tokens(u_ref, group, lanes, seqs)
            for k in range(GROUP):
                here = at_rows(group * GROUP + k, seqs)
                step = step_ref[here, lanes]
                drive = step * us[k]
                stop = step + spread_ref[here, stop_lanes]
                total = total + stop
                fresh = []
                for n in range(states):
                    decay = jnp.exp2(stop * rate_ref[pl.ds(n * seqs, seqs), lanes])
                    b_one = spread_ref[here, pl.ds(n * LANES, LANES)]
                    fresh.append(decay * state[n] + drive * b_one)
                state = tuple(fresh)
            return state, total

        state, total = lax.fori_loop(0, tokens // GROUP, one, ((zero,) * states, zero))
        put_blocks(ends, place, lanes, state)
        sums[place, :, lanes] = total
        exchange.start(tile)
        return carry

    lax.fori_loop(0, tiles, local, 0)
    finish_exchange(exchange, tiles, lambda first, lanes: lax.fori_loop(
        0,
        place,
        lambda source, state: chained(state, ends, sums, rate_ref, source, lanes, seqs),
        first,
    ), start_ref, states, zero)
    sum_ref[...] = sums[place]


def finish_exchange(exchange, tiles, chain, target_ref, states, zero):
    def pass_on(tile, carry):
        exchange.pass_on(tile)
        return carry

    lax.fori_loop(0, tiles, pass_on, 0)

    def take(tile, carry):
        lanes = at_rows(tile, LANES)
        exchange.arrive(tile)
        put_blocks(target_ref, None, lanes, chain((zero,) * states, lanes))
        return carry

    lax.fori_loop(0, tiles, take, 0)

    def finish(tile, carry):
        exchange.finish(tile)
        return carry

    lax.fori_loop(0, tiles, finish, 0)


def forward_kernel(
    count,
    seqs,
    states,
    parts_ref,
    step_ref,
    u_ref,
    rate_ref,
    start_ref,
    block_ref,
    y_ref,
    gathered_ref,
    *scratch,
):
    spread_ref, *sems = scratch
    gather = BlockGather(count, block_ref, gathered_ref, sems)
    rows, channels = step_ref.shape
    tokens, tiles = rows // seqs, channels // LANES
    stop_lanes = pl.ds(2 * states * LANES, LANES)
    zero = jnp.zeros((seqs, LANES), F32)
    greet_pairs(count)
    gather.start()
    spread(parts_ref, states, spread_ref)

    def whole(tile, carry):
        lanes = at_rows(tile, LANES)

        def one(group, state):
            us = group_tokens(u_ref, group, lanes, seqs)
            for k in range(GROUP):
                here = at_rows(group * GROUP + k, seqs)
                step = step_ref[here, lanes]
                drive = step * us[k]
                stop = step + spread_ref[here, stop_lanes]
                fresh = []
                out = zero
                for n in range(states):
                    decay = jnp.exp2(stop * rate_ref[pl.ds(n * seqs, seqs), lanes])
                    b_one = spread_ref[here, pl.ds(n * LANES, LANES)]
                    value = decay * state[n] + drive * b_one
                    out = out + value * spread_ref[here, pl.ds((states + n) * LANES, LANES)]
                    fresh.append(value)
                y_ref[here, lanes] = out
                state = tuple(fresh)
            return state

        lax.fori_loop(0, tokens // GROUP, one, state_blocks(start_ref, lanes, seqs, states))
        for piece in range(gather.pieces):
            if 3 * piece + 2 < tiles:

                @pl.when(tile == 3 * piece + 2)
                def _():
                    gather.relay(piece)

        return carry

    lax.fori_loop(0, tiles, whole, 0)
    for piece in range(gather.pieces):
        if 3 * piece + 2 >= tiles:
            gather.relay(piece)
    gather.finish()


def adjoint_kernel(
    count, seqs, states, parts_ref, step_ref, dy_ref, rate_ref, sum_ref, last_ref, *scratch
):
    spread_ref, ends, sums, *sems = scratch
    rows, channels = step_ref.shape
    tokens, tiles = rows // seqs, channels // LANES
    groups = tokens // GROUP
    stop_lanes = pl.ds(2 * states * LANES, LANES)
    exchange = Exchange(count, False, (ends, sums), sems)
    place = exchange.place
    zero = jnp.zeros((seqs, LANES), F32)
    greet_pairs(count)
    spread(parts_ref, states, spread_ref)

    def own(tile, carry):
        lanes = at_rows(tile, LANES)

        def one(back, grads):
            group = groups - 1 - back
            for k in reversed(range(GROUP)):
                here = at_rows(group * GROUP + k, seqs)
                stop = step_ref[here, lanes] + spread_ref[here, stop_lanes]
                dy = dy_ref[here, lanes]
                fresh = []
                for n in range(states):
                    decay = jnp.exp2(stop * rate_ref[pl.ds(n * seqs, seqs), lanes])
                    c_one = spread_ref[here, pl.ds((states + n) * LANES, LANES)]
                    fresh.append(decay * (grads[n] + dy * c_one))
                grads = tuple(fresh)
            return grads

        put_blocks(ends, place, lanes, lax.fori_loop(0, groups, one, (zero,) * states))
        sums[place, :, lanes] = sum_ref[:, lanes]
        exchange.start(tile)
        return carry

    lax.fori_loop(0, tiles, own, 0)
    finish_exchange(exchange, tiles, lambda first, lanes: lax.fori_loop(
        0,
        count - 1 - place,
        lambda hop, state: chained(state, ends, sums, rate_ref, count - 1 - hop, lanes, seqs),
        first,
    ), last_ref, states, zero)


def backward_kernel(
    count,
    seqs,
    states,
    parts_ref,
    step_ref,
    u_ref,
    dy_ref,
    rate_ref,
    start_ref,
    last_ref,
    *refs,
):
    kinds = (len(refs) - 16) // 3
    grad_refs, refs = refs[:kinds], refs[kinds:]
    du_ref, dpre_ref, dbc_ref, dlog_ref, dbias_ref, *refs = refs
    given_refs, came_refs, scratch = refs[:kinds], refs[kinds : 2 * kinds], refs[2 * kinds :]
    spread_ref, held, acc, *scratch = scratch
    rows, channels = step_ref.shape
    tokens, tiles = rows // seqs, channels // LANES
    groups = tokens // GROUP
    stop_lanes = pl.ds(2 * states * LANES, LANES)
    place = lax.axis_index("seq")
    low, high = lax.rem(place, 2), place // 2
    zero = jnp.zeros((seqs, LANES), F32)
    greet_pairs(count)

    scatter = PairScatter(count, grad_refs, given_refs, came_refs, scratch)
    scatter.start()
    spread(parts_ref, states, spread_ref)

    def clear(row, carry):
        acc[at_rows(row, seqs), :] = jnp.zeros((seqs, acc.shape[1]), F32)
        return carry

    lax.fori_loop(0, tokens, clear, 0)

    def whole(tile, carry):
        lanes = at_rows(tile, LANES)

        def again(group, state):
            us = group_tokens(u_ref, group, lanes, seqs)
            for k in range(GROUP):
                token = group * GROUP + k
                here = at_rows(token, seqs)
                step = step_ref[here, lanes]
                drive = step * us[k]
                stop = step + spread_ref[here, stop_lanes]
                fresh = []
                for n in range(states):
                    held[token * states + n] = state[n]
                    decay = jnp.exp2(stop * rate_ref[pl.ds(n * seqs, seqs), lanes])
                    b_one = spread_ref[here, pl.ds(n * LANES, LANES)]
                    fresh.append(decay * state[n] + drive * b_one)
                state = tuple(fresh)
            return state

        state = lax.fori_loop(0, groups, again, state_blocks(start_ref, lanes, seqs, states))
        for n in range(states):
            held[tokens * states + n] = state[n]
        for k in range(tiles):

            @pl.when(tile == k)
            def _():
                scatter.advance(2 * k)

        grads = state_blocks(last_ref, lanes, seqs, states)

        def one(back, carry):
            grads, logs, bias = carry
            group = groups - 1 - back
            us = group_tokens(u_ref, group, lanes, seqs)
            pres = [None] * GROUP
            for k in reversed(range(GROUP)):
                token = group * GROUP + k
                here = at_rows(token, seqs)
                step = step_ref[here, lanes]
                dy = dy_ref[here, lanes]
                drive = step * us[k]
                stop = step + spread_ref[here, stop_lanes]
                fresh, fresh_logs = [], []
                on_b, on_rate = zero, zero
                for n in range(states):
                    at = token * states + n
                    on_lanes = pl.ds(n * LANES, LANES)
                    other_lanes = pl.ds((states + n) * LANES, LANES)
                    rate = rate_ref[pl.ds(n * seqs, seqs), lanes]
                    decay = jnp.exp2(stop * rate)
                    lam = grads[n] + dy * spread_ref[here, other_lanes]
                    carried = lam * decay
                    fresh.append(carried)
                    kept = carried * held[at]
                    on_b = on_b + lam * spread_ref[here, on_lanes]
                    on_rate = on_rate + kept * rate
                    fresh_logs.append(logs[n] + kept * step)
                    acc[here, on_lanes] = acc[here, on_lanes] + lam * drive
                    acc[here, other_lanes] = acc[here, other_lanes] + dy * held[at + states]
                du_ref[here, lanes] = step * on_b
                series = step * (1.0 - step * (0.5 - step * (1.0 / 6.0 - step * (1.0 / 24.0))))
                slope = jnp.where(step < 0.05, series, 1.0 - jnp.exp2(step * (-LOG2E)))
                pres[k] = (on_rate * LN2 + us[k] * on_b) * slope
                bias = bias + pres[k]
                grads, logs = tuple(fresh), tuple(fresh_logs)
            dpre_ref[at_rows(group, GROUP * seqs), lanes] = jnp.concatenate(pres, 0).astype(BF)
            return grads, logs, bias

        grads, logs, bias = lax.fori_loop(0, groups, one, (grads, (zero,) * states, zero))
        dlog_ref[:, lanes] = jnp.concatenate(
            [jnp.sum(log, axis=0, keepdims=True) for log in logs], axis=0
        )
        dbias_ref[:, lanes] = bias
        for k in range(tiles):

            @pl.when(tile == k)
            def _():
                scatter.advance(2 * k + 1)

        return carry

    lax.fori_loop(0, tiles, whole, 0)

    wide = 2 * LANES
    chunk = 256 if rows % 256 == 0 else rows
    target = lax.broadcasted_iota(jnp.int32, (wide, LANES), 1)
    half = lax.broadcasted_iota(jnp.int32, (wide, LANES), 0) // LANES
    dbc_ref[...] = jnp.zeros(dbc_ref.shape, F32)

    def reduce(pair, carry):
        hot = jnp.where(target == pair * 2 + half, 1.0, 0.0).astype(BF)
        for k in range(rows // chunk):
            here = pl.ds(k * chunk, chunk)
            values = acc[here, at_rows(pair, wide)]
            main = values.astype(BF)
            rest = (values - main.astype(F32)).astype(BF)
            dbc_ref[here, :] += jnp.dot(main, hot, preferred_element_type=F32) + jnp.dot(
                rest, hot, preferred_element_type=F32
            )
        return carry

    lax.fori_loop(0, states, reduce, 0)

    for turn in range(2 * tiles, scatter.turns):
        scatter.advance(turn)
    scatter.finish()


class PairScatter:
    def __init__(self, count, grads, given, came, scratch):
        place = lax.axis_index("seq")
        self.around = count // 2
        self.low, self.high = lax.rem(place, 2), place // 2
        self.grads, self.given, self.came = grads, given, came
        self.mine_buf, self.given_buf, self.sum_buf = scratch[:3]
        self.swap_send, self.swap_recv, self.hop_send, self.hop_recv, self.load_sem = scratch[3:]
        self.items = [(k, steps) for k in range(len(grads)) for steps in range(1, self.around)]
        self.turns = len(self.items) + 1

    def pair(self, steps):
        return lax.rem(self.high + steps, self.around)

    def swap(self, kind, steps):
        return pltpu.make_async_remote_copy(
            src_ref=self.grads[kind].at[self.pair(steps), 1 - self.low],
            dst_ref=self.given[kind].at[steps],
            send_sem=self.swap_send.at[kind, steps],
            recv_sem=self.swap_recv.at[kind, steps],
            device_id={"seq": self.high * 2 + 1 - self.low},
            device_id_type=pl.DeviceIdType.MESH,
        )

    def hop(self, item):
        kind, steps = self.items[item]
        wide = self.grads[kind].shape[-1]
        return pltpu.make_async_remote_copy(
            src_ref=self.sum_buf.at[item % 2, :, pl.ds(0, wide)],
            dst_ref=self.came[kind].at[steps - 1],
            send_sem=self.hop_send.at[kind, steps],
            recv_sem=self.hop_recv.at[kind, steps],
            device_id={"seq": self.pair(steps) * 2 + self.low},
            device_id_type=pl.DeviceIdType.MESH,
        )

    def loads(self, item):
        kind, steps = self.items[item]
        lanes = pl.ds(0, self.grads[kind].shape[-1])
        return [
            pltpu.make_async_copy(
                self.grads[kind].at[self.pair(steps), self.low],
                self.mine_buf.at[item % 2, :, lanes],
                self.load_sem.at[item % 2, 0],
            ),
            pltpu.make_async_copy(
                self.given[kind].at[steps],
                self.given_buf.at[item % 2, :, lanes],
                self.load_sem.at[item % 2, 1],
            ),
        ]

    def start(self):
        for kind, steps in self.items:
            self.swap(kind, steps).start()
        for kind in range(len(self.grads)):
            self.swap(kind, 0).start()

    def advance(self, turn):
        if turn < len(self.items):
            self.swap(*self.items[turn]).wait_recv()
            for load in self.loads(turn):
                load.start()
        item = turn - 1
        if 0 <= item < len(self.items):
            for load in self.loads(item):
                load.wait()
            if item >= 2:
                self.hop(item - 2).wait_send()
            wide = self.grads[self.items[item][0]].shape[-1]
            rows = self.mine_buf.shape[1]

            def add(row, carry):
                here = at_rows(row, 16)
                lanes = pl.ds(0, wide)
                total = self.mine_buf[item % 2, here, lanes].astype(F32) + self.given_buf[
                    item % 2, here, lanes
                ].astype(F32)
                self.sum_buf[item % 2, here, lanes] = total.astype(BF)
                return carry

            lax.fori_loop(0, rows // 16, add, 0)
            self.hop(item).start()

    def finish(self):
        for item in range(max(0, len(self.items) - 2), len(self.items)):
            self.hop(item).wait_send()
        for item in range(len(self.items)):
            self.hop(item).wait_recv()
            self.swap(*self.items[item]).wait_send()
        for kind in range(len(self.grads)):
            self.swap(kind, 0).wait()


def scatter_scratch(count, grads):
    rows = grads[0].shape[2]
    wide = max(grad.shape[3] for grad in grads)
    sems = pltpu.SemaphoreType.DMA((len(grads), count // 2))
    return [pltpu.VMEM((2, rows, wide), BF)] * 3 + [sems] * 4 + [pltpu.SemaphoreType.DMA((2, 2))]


def exchange_scratch(count, seqs, states, channels):
    sems = pltpu.SemaphoreType.DMA((2, count // 2, channels // LANES))
    return [
        pltpu.VMEM((count, states * seqs, channels), BF),
        pltpu.VMEM((count, seqs, channels), F32),
    ] + [sems] * 4


def state_call(body, ident, seqs, states, ins, outs, scratch, ops, hosted):
    count = lax.axis_size("seq")
    rows, channels = ins[1].shape
    in_vmem = pl.BlockSpec(memory_space=pltpu.VMEM)
    anywhere = pl.BlockSpec(memory_space=pl.ANY)
    return pl.pallas_call(
        functools.partial(body, count, seqs, states),
        in_specs=[in_vmem] * (len(ins) - hosted[0]) + [anywhere] * hosted[0],
        out_specs=tuple([in_vmem] * (len(outs) - hosted[1]) + [anywhere] * hosted[1]),
        out_shape=tuple(outs),
        scratch_shapes=[pltpu.VMEM((rows, 2 * (states + 1) * LANES), F32)] + scratch,
        compiler_params=pltpu.CompilerParams(
            collective_id=ident, has_side_effects=True, vmem_limit_bytes=62 * 1024 * 1024
        ),
        cost_estimate=pl.CostEstimate(
            flops=ops * rows * channels * states,
            bytes_accessed=16 * 1024 * 1024,
            transcendentals=0,
        ),
    )(*ins)


class BlockGather:
    def __init__(self, count, source, target, sems):
        place = lax.axis_index("seq")
        self.around = count // 2
        self.low, self.high = lax.rem(place, 2), place // 2
        self.place = place
        self.source, self.target = source, target
        self.hop_send, self.hop_recv, self.swap_send, self.swap_recv, self.local_sem = sems
        self.mate = self.high * 2 + 1 - self.low
        self.pieces = pieces_of(source.shape[-1])

    def pair(self, steps):
        return lax.rem(self.high + steps + self.around, self.around) * 2 + self.low

    def lanes(self, piece):
        size = self.source.shape[-1] // self.pieces
        return pl.ds(piece * size, size)

    def local(self):
        return pltpu.make_async_copy(self.source, self.target.at[self.place], self.local_sem.at[0])

    def hop(self, piece, steps):
        return pltpu.make_async_remote_copy(
            src_ref=self.source.at[:, self.lanes(piece)],
            dst_ref=self.target.at[self.place, :, self.lanes(piece)],
            send_sem=self.hop_send.at[piece, steps],
            recv_sem=self.hop_recv.at[piece, steps],
            device_id={"seq": self.pair(steps)},
            device_id_type=pl.DeviceIdType.MESH,
        )

    def swap(self, piece, steps):
        block = self.target.at[self.pair(-steps), :, self.lanes(piece)]
        return pltpu.make_async_remote_copy(
            src_ref=block if steps else self.source.at[:, self.lanes(piece)],
            dst_ref=block,
            send_sem=self.swap_send.at[piece, steps],
            recv_sem=self.swap_recv.at[piece, steps],
            device_id={"seq": self.mate},
            device_id_type=pl.DeviceIdType.MESH,
        )

    def start(self):
        self.local().start()
        for piece in range(self.pieces):
            for steps in range(1, self.around):
                self.hop(piece, steps).start()
        for piece in range(self.pieces):
            self.swap(piece, 0).start()

    def relay(self, piece):
        for steps in range(1, self.around):
            self.hop(piece, steps).wait_recv()
            self.swap(piece, steps).start()

    def finish(self):
        self.local().wait()
        for piece in range(self.pieces):
            for steps in range(1, self.around):
                self.hop(piece, steps).wait_send()
            for steps in range(self.around):
                self.swap(piece, steps).wait()


def pieces_of(width):
    for size in (384, 256):
        if width % size == 0:
            return width // size
    return 1


def gather_sems(around, width):
    pieces = pieces_of(width)
    return [pltpu.SemaphoreType.DMA((pieces, around))] * 4 + [pltpu.SemaphoreType.DMA((1,))]


def greet_pairs(count, heads=False):
    place = lax.axis_index("seq")
    around = count // 2
    low, high = lax.rem(place, 2), place // 2
    barrier = pltpu.get_barrier_semaphore()
    peers = [lax.rem(high + steps, around) * 2 + low for steps in range(1, around)]
    peers = [{"seq": device} for device in peers + [high * 2 + 1 - low]]
    if heads:
        head = lax.axis_index("head")
        low, high = lax.rem(head, 2), head // 2
        peers += [{"head": high * 2 + 1 - low}, {"head": 2 - 2 * high + low}]
    for device in peers:
        pl.semaphore_signal(barrier, inc=1, device_id=device, device_id_type=pl.DeviceIdType.MESH)
    pl.semaphore_wait(barrier, len(peers))


class HeadSum:
    def __init__(self, part, half, give, take, whole, sems):
        head = lax.axis_index("head")
        self.low, self.high = lax.rem(head, 2), head // 2
        self.near = {"head": self.high * 2 + 1 - self.low}
        self.far = {"head": 2 - 2 * self.high + self.low}
        self.part, self.half, self.give, self.take, self.whole = part, half, give, take, whole
        self.sems = sems
        self.size = half.shape[1]

    def copy(self, source, target, kind, chunk, device):
        return pltpu.make_async_remote_copy(
            src_ref=source,
            dst_ref=target,
            send_sem=self.sems.at[kind, 0, chunk],
            recv_sem=self.sems.at[kind, 1, chunk],
            device_id=device,
            device_id_type=pl.DeviceIdType.MESH,
        )

    def rows(self, chunk, bit):
        start = pl.multiple_of((chunk * 2 + bit) * self.size, self.size)
        return pl.ds(start, self.size)

    def own_rows(self, chunk):
        quarter = self.size // 2
        start = (chunk * 2 + self.low) * self.size + self.high * quarter
        return pl.ds(pl.multiple_of(start, quarter), quarter)

    def near_copy(self, chunk):
        return self.copy(
            self.part.at[self.rows(chunk, 1 - self.low)], self.half.at[chunk], 0, chunk, self.near
        )

    def far_copy(self, chunk):
        return self.copy(self.give.at[chunk], self.take.at[chunk], 1, chunk, self.far)

    def far_back(self, chunk):
        here = self.whole.at[self.own_rows(chunk)]
        return self.copy(here, here, 2, chunk, self.far)

    def near_back(self, chunk):
        here = self.whole.at[self.rows(chunk, self.low)]
        return self.copy(here, here, 3, chunk, self.near)

    def fold(self, chunk, kept):
        self.near_copy(chunk).wait_recv()
        quarter = self.size // 2
        base = (chunk * 2 + self.low) * self.size
        for mine in (False, True):
            bit = self.high if mine else 1 - self.high
            start = pl.multiple_of(bit * quarter, quarter)
            at = pl.multiple_of(base + bit * quarter, quarter)
            total = self.part[pl.ds(at, quarter), :].astype(F32)
            total = total + self.half[chunk, pl.ds(start, quarter), :].astype(F32)
            if mine:
                kept[chunk] = total
            else:
                self.give[chunk] = total.astype(BF)
                self.far_copy(chunk).start()

    def finish(self, chunk):
        for copy in (self.near_copy, self.far_copy, self.far_back, self.near_back):
            copy(chunk).wait_send()


def transposed_dot(left, right):
    return lax.dot_general(left, right, (((1,), (1,)), ((), ())), preferred_element_type=F32)


def ffn_kernel(count, chunks, hosted, *refs):
    g_ref, out_ref, x_ref, gain_ref, low_ref, dout_ref, *refs = refs
    ready, refs = refs[: 3 - hosted], refs[3 - hosted :]
    shards_in, refs = refs[:hosted], refs[hosted:]
    hidden_ref, norm_ref, act_ref, dgate_ref, dup_ref, dnorm_gain_ref, part_out_ref, *refs = refs
    dhidden_ref, dmix_ref, *refs = refs
    landed, refs = refs[:hosted], refs[hosted:]
    part_a, half_a, give_a, take_a, part_b, half_b, give_b, take_b, kept, *refs = refs
    sems_a, sems_b, *refs = refs
    gathers = [
        BlockGather(count, shards_in[k], landed[k], refs[5 * k : 5 * k + 5]) for k in range(hosted)
    ]
    gate_ref, up_ref, down_ref = list(ready) + list(landed)
    mix = HeadSum(part_a, half_a, give_a, take_a, norm_ref, sems_a)
    back = HeadSum(part_b, half_b, give_b, take_b, dmix_ref, sems_b)
    size = g_ref.shape[0] // chunks
    quarter = size // 4
    width = x_ref.shape[1]
    shard, units = gate_ref.shape[1:]
    greet_pairs(count, True)
    for gather in gathers:
        gather.start()
    relays = [(gather, piece) for gather in gathers for piece in range(gather.pieces)]
    fourth = -(-len(relays) // chunks)

    def project(chunk, carry):
        here = at_rows(chunk, size)
        part_a[here, :] = transposed_dot(g_ref[here, :], out_ref[...]).astype(BF)
        mix.near_copy(chunk).start()
        return carry

    lax.fori_loop(0, chunks, project, 0)

    def fold(chunk, carry):
        mix.fold(chunk, kept)
        return carry

    lax.fori_loop(0, chunks, fold, 0)

    def normalise(chunk, carry):
        mix.far_copy(chunk).wait_recv()
        here = at_rows(chunk, quarter)
        hidden = x_ref[here, :] + kept[chunk] + take_a[chunk].astype(F32)
        hidden_ref[here, :] = hidden
        scale = lax.rsqrt(jnp.mean(hidden * hidden, axis=1, keepdims=True) + EPS)
        norm_ref[mix.own_rows(chunk), :] = (hidden * scale * gain_ref[...]).astype(BF)
        mix.far_back(chunk).start()
        for k in range(chunks):
            if relays[k * fourth : (k + 1) * fourth]:

                @pl.when(chunk == k)
                def _():
                    for gather, piece in relays[k * fourth : (k + 1) * fourth]:
                        gather.relay(piece)

        return carry

    lax.fori_loop(0, chunks, normalise, 0)
    mix.far_back(0).wait_recv()
    mix.near_back(0).start()
    for gather in gathers:
        gather.finish()
    per_block = max(1, count // 4)
    wide = per_block * shard
    lanes_block = 256 if units % 256 == 0 else units

    def feed(chunk, carry):
        here = at_rows(chunk, size)

        @pl.when(chunk + 1 < chunks)
        def _():
            mix.far_back(chunk + 1).wait_recv()
            mix.near_back(chunk + 1).start()

        mix.near_back(chunk).wait_recv()
        rows = norm_ref[here, :]
        grads = low_ref[here, :]
        for k in range(units // lanes_block):
            lanes = pl.ds(k * lanes_block, lanes_block)
            block = lambda ref: ref[:, :, lanes].reshape(width, lanes_block)
            gate = jnp.dot(rows, block(gate_ref), preferred_element_type=F32)
            up = jnp.dot(rows, block(up_ref), preferred_element_type=F32)
            d_act = jnp.dot(grads, block(down_ref), preferred_element_type=F32)
            logistic = 1.0 / (1.0 + jnp.exp(-gate))
            silu = gate * logistic
            act_ref[here, lanes] = (silu * up).astype(BF)
            slope = logistic * (1.0 + gate * (1.0 - logistic))
            dgate_ref[here, lanes] = (d_act * up * slope).astype(BF)
            dup_ref[here, lanes] = (d_act * silu).astype(BF)
        for k in range(count // per_block):
            lanes = pl.ds(k * wide, wide)
            block = lambda ref: ref[pl.ds(k * per_block, per_block)].reshape(wide, units)
            total = transposed_dot(dgate_ref[here, :], block(gate_ref))
            total = total + transposed_dot(dup_ref[here, :], block(up_ref))
            part_b[here, lanes] = total.astype(BF)
        back.near_copy(chunk).start()
        for k in range(count // per_block):
            lanes = pl.ds(k * wide, wide)
            block = down_ref[pl.ds(k * per_block, per_block)].reshape(wide, units)
            part_out_ref[here, lanes] = transposed_dot(act_ref[here, :], block).astype(BF)

        @pl.when(chunk >= 1)
        def _():
            back.fold(chunk - 1, kept)

        return carry

    lax.fori_loop(0, chunks, feed, 0)
    back.fold(chunks - 1, kept)
    dnorm_gain_ref[...] = jnp.zeros(dnorm_gain_ref.shape, F32)

    def turn(chunk, carry):
        back.far_copy(chunk).wait_recv()
        here = at_rows(chunk, quarter)
        hidden = hidden_ref[here, :]
        scale = lax.rsqrt(jnp.mean(hidden * hidden, axis=1, keepdims=True) + EPS)
        normed = hidden * scale
        d_norm = kept[chunk] + take_b[chunk].astype(F32)
        dnorm_gain_ref[...] += jnp.sum(d_norm * normed, axis=0, keepdims=True)
        scaled = d_norm * gain_ref[...]
        shift = jnp.mean(scaled * normed, axis=1, keepdims=True)
        d_hidden = dout_ref[here, :] + scale * (scaled - normed * shift)
        dhidden_ref[here, :] = d_hidden
        dmix_ref[back.own_rows(chunk), :] = d_hidden.astype(BF)
        back.far_back(chunk).start()
        return carry

    lax.fori_loop(0, chunks, turn, 0)

    def spread_out(chunk, carry):
        back.far_back(chunk).wait_recv()
        back.near_back(chunk).start()
        return carry

    lax.fori_loop(0, chunks, spread_out, 0)

    def finish(chunk, carry):
        back.near_back(chunk).wait_recv()
        mix.finish(chunk)
        back.finish(chunk)
        return carry

    lax.fori_loop(0, chunks, finish, 0)


CHUNKS = 4


def ffn_call(g_low, out_t, x_own, gain, grad_low, dout_own, ready, waiting):
    count = lax.axis_size("seq")
    rows, width = grad_low.shape
    units = waiting[0].shape[1]
    chunk = rows // CHUNKS
    shape = jax.ShapeDtypeStruct
    in_vmem = pl.BlockSpec(memory_space=pltpu.VMEM)
    anywhere = pl.BlockSpec(memory_space=pl.ANY)
    sums = [
        pltpu.VMEM((rows, width), BF),
        pltpu.VMEM((CHUNKS, chunk // 2, width), BF),
        pltpu.VMEM((CHUNKS, chunk // 4, width), BF),
        pltpu.VMEM((CHUNKS, chunk // 4, width), BF),
    ]
    outs = [
        shape((rows // 4, width), F32),
        shape((rows, width), BF),
        shape((rows, units), BF),
        shape((rows, units), BF),
        shape((rows, units), BF),
        shape((1, width), F32),
        shape((rows, width), BF),
        shape((rows // 4, width), F32),
        shape((rows, width), BF),
    ]
    return pl.pallas_call(
        functools.partial(ffn_kernel, count, CHUNKS, len(waiting)),
        in_specs=[in_vmem] * (6 + len(ready)) + [anywhere] * len(waiting),
        out_specs=tuple([in_vmem] * len(outs)),
        out_shape=tuple(outs),
        scratch_shapes=[pltpu.VMEM((count,) + w.shape, BF) for w in waiting]
        + sums
        + sums
        + [pltpu.VMEM((CHUNKS, chunk // 4, width), F32)]
        + [pltpu.SemaphoreType.DMA((4, 2, CHUNKS))] * 2
        + [sem for w in waiting for sem in gather_sems(count // 2, w.shape[1])],
        compiler_params=pltpu.CompilerParams(
            collective_id=5, has_side_effects=True, vmem_limit_bytes=62 * 1024 * 1024
        ),
        cost_estimate=pl.CostEstimate(
            flops=14 * rows * width * units, bytes_accessed=40 * 1024 * 1024, transcendentals=0
        ),
    )(g_low, out_t, x_own, gain, grad_low, dout_own, *ready, *waiting)


def pairs_of(axis):
    return lax.axis_size(axis) // 2


def hop(value, steps):
    count = lax.axis_size("seq")
    return lax.ppermute(value, "seq", [(s, (s + 2 * steps) % count) for s in range(count)])


def swap(value, axis, bit):
    return lax.ppermute(value, axis, [(s, s ^ bit) for s in range(lax.axis_size(axis))])


def owner_blocks(value):
    return value.reshape((pairs_of("seq"), 2, -1) + value.shape[1:])


def scatter_half(blocks, theirs):
    place = lax.axis_index("seq")
    around = pairs_of("seq")
    low, high = place % 2, place // 2
    mine = lax.dynamic_index_in_dim(blocks, low, 1, False)
    half = mine.astype(F32) + theirs.astype(F32)
    total = lax.dynamic_index_in_dim(half, high, 0, False)
    half = half.astype(blocks.dtype)
    for steps in range(1, around):
        part = lax.dynamic_index_in_dim(half, (high + steps) % around, 0, False)
        total = total + hop(part, steps).astype(F32)
    return total


def scatter_rows(value, kind=BF):
    low = lax.axis_index("seq") % 2
    blocks = owner_blocks(value.astype(kind))
    theirs = lax.dynamic_index_in_dim(blocks, 1 - low, 1, False)
    return scatter_half(blocks, swap(theirs, "seq", 1))


def scatter_own(blocks, given, came):
    place = lax.axis_index("seq")
    own = blocks.reshape((-1,) + blocks.shape[2:])
    total = lax.dynamic_index_in_dim(own, place, 0, False).astype(F32) + given[0].astype(F32)
    for k in range(came.shape[0]):
        total = total + came[k].astype(F32)
    return total


def head_bits():
    return (lax.axis_size("head") - 1).bit_length()


def head_scatter(value):
    place = lax.axis_index("head")
    width = value.shape[1]
    value = value.reshape(CHUNKS, -1, width)
    for k in range(head_bits()):
        bit = place // 2**k % 2
        halves = value.astype(BF).reshape(CHUNKS, 2, -1, width)
        keep = lax.dynamic_index_in_dim(halves, bit, 1, False)
        send = lax.dynamic_index_in_dim(halves, 1 - bit, 1, False)
        value = keep.astype(F32) + swap(send, "head", 2**k).astype(F32)
    return value.reshape(-1, width)


def head_part(value):
    place = lax.axis_index("head")
    width = value.shape[1]
    value = value.reshape(CHUNKS, -1, width)
    for k in range(head_bits()):
        halves = value.reshape(CHUNKS, 2, -1, width)
        value = lax.dynamic_index_in_dim(halves, place // 2**k % 2, 1, False)
    return value.reshape(-1, width)


def head_gather(value):
    place = lax.axis_index("head")
    width = value.shape[1]
    value = value.reshape(CHUNKS, -1, width)
    for k in reversed(range(head_bits())):
        got = swap(value, "head", 2**k)
        first = place // 2**k % 2 == 0
        both = [jnp.where(first, value, got), jnp.where(first, got, value)]
        value = jnp.concatenate(both, axis=1)
    return value.reshape(-1, width)


def head_total(value, kind):
    for k in range(head_bits()):
        value = value.astype(kind)
        value = value.astype(F32) + swap(value, "head", 2**k).astype(F32)
    return value


def first_kernel(count, *refs):
    kinds = len(refs) // 7
    gathers = [
        BlockGather(count, refs[k], refs[kinds + k], refs[2 * kinds + 5 * k : 2 * kinds + 5 * k + 5])
        for k in range(kinds)
    ]
    greet_pairs(count)
    for gather in gathers:
        gather.start()
    for gather in gathers:
        for piece in range(gather.pieces):
            gather.relay(piece)
    for gather in gathers:
        gather.finish()


def first_gather(*values):
    count = lax.axis_size("seq")
    around = count // 2
    kinds = len(values)
    return pl.pallas_call(
        functools.partial(first_kernel, count),
        out_shape=tuple(jax.ShapeDtypeStruct((count,) + v.shape, v.dtype) for v in values),
        in_specs=[pl.BlockSpec(memory_space=pl.ANY)] * kinds,
        out_specs=tuple([pl.BlockSpec(memory_space=pl.ANY)] * kinds),
        scratch_shapes=[sem for v in values for sem in gather_sems(around, v.shape[-1])],
        compiler_params=pltpu.CompilerParams(collective_id=0, has_side_effects=True),
    )(*values)


def shards(
    x_in,
    seg_ids,
    norm1_gain,
    w_in_x,
    w_in_z,
    conv_w,
    conv_b,
    w_xproj,
    ssm_gain,
    w_dt,
    dt_bias,
    a_log,
    d_skip,
    w_out,
    norm2_gain,
    w_gate,
    w_up,
    w_down,
    d_out,
):
    count = lax.axis_size("seq")
    place = lax.axis_index("seq")
    seqs, tokens, width = x_in.shape
    rows = seqs * tokens
    taps = conv_w.shape[0]
    rank = w_dt.shape[0]
    states = a_log.shape[1]
    channels = w_in_x.shape[1]
    halo = (taps - 1) * seqs

    per = channels // count
    fields = [w_xproj, w_dt.T, a_log, conv_w.T, conv_b[:, None], dt_bias[:, None], d_skip[:, None]]
    starts = [0]
    for field in fields:
        starts.append(starts[-1] + field.shape[1])
    pack_width = -(-starts[-1] // LANES) * LANES
    gains = [norm1_gain, norm2_gain, ssm_gain]
    gain_starts = [0]
    for gain in gains:
        gain_starts.append(gain_starts[-1] + gain.shape[0])
    pack_rows = -(-(per + -(-gain_starts[-1] // pack_width)) // 16) * 16

    def pack(channel_fields, gain_fields):
        table = jnp.concatenate([f.astype(F32) for f in channel_fields], axis=1)
        table = jnp.pad(table, ((0, 0), (0, pack_width - table.shape[1])))
        table = table.reshape(-1, per, pack_width)
        rest = jnp.concatenate([g.astype(F32).reshape(table.shape[0], -1) for g in gain_fields], 1)
        rest = jnp.pad(rest, ((0, 0), (0, (pack_rows - per) * pack_width - rest.shape[1])))
        return jnp.concatenate([table, rest.reshape(-1, pack_rows - per, pack_width)], axis=1)

    def unpack(block):
        table = block[:, :per].reshape(-1, pack_width)
        rest = block[:, per:].reshape(block.shape[0], -1)
        return (
            [table[:, starts[k] : starts[k + 1]] for k in range(len(fields))],
            [rest[:, gain_starts[k] : gain_starts[k + 1]].reshape(-1) for k in range(len(gains))],
        )

    in_x_blocks, pack_blocks = first_gather(w_in_x.astype(BF), pack(fields, gains)[0].astype(BF))
    full_in_x = in_x_blocks.reshape(width, channels)
    fulls, full_gains = unpack(pack_blocks)
    full_xproj, w_dt_cols, full_a_log, conv_cols, conv_b_col, bias_col, skip_col = fulls
    full_w_dt = w_dt_cols.T
    full_conv_w = conv_cols.T
    full_conv_b, full_dt_bias, full_d_skip = conv_b_col[:, 0], bias_col[:, 0], skip_col[:, 0]
    full_norm1, full_norm2, full_ssm_gain = full_gains

    w_mix = jnp.concatenate([w_in_z.astype(BF), w_out.astype(BF).T], axis=1)
    w_wide = jnp.concatenate([w_gate.astype(BF), w_up.astype(BF)], axis=1)
    full_wide = lax.all_gather(w_wide, "seq", axis=0, tiled=True)
    hidden_units = w_gate.shape[1]

    norm1_vec = full_norm1.astype(F32)
    x_rows = x_in.transpose(1, 0, 2).reshape(rows, width).astype(F32)
    ids = seg_ids.T.reshape(rows)
    normed1, scale_one = norm_rows(x_rows, norm1_vec)
    x_norm = normed1.astype(BF)
    x_inner = jnp.dot(x_norm, full_in_x, preferred_element_type=F32).astype(BF)
    prev_tail, prev_ids = shifted((x_inner[rows - halo :], ids[rows - halo :]), "seq", 1)
    extended = jnp.concatenate([prev_tail, x_inner], axis=0).astype(F32)
    ext_ids = jnp.concatenate([prev_ids, ids])
    conv_weight = full_conv_w.astype(F32)
    x_conv = full_conv_b.astype(F32)[None, :]
    same_docs = []
    for offset in range(taps):
        first = (taps - 1 - offset) * seqs
        same = (ext_ids[first : first + rows] == ids).astype(F32)[:, None]
        same_docs.append(same)
        x_conv = x_conv + conv_weight[offset] * extended[first : first + rows] * same
    u_low = jax.nn.silu(x_conv).astype(BF)
    projected = head_total(jnp.dot(u_low, full_xproj, preferred_element_type=F32), BF)
    ssm_vec = full_ssm_gain.astype(F32)
    b_end = rank + states
    dt_normed, dt_scale = norm_rows(projected[:, :rank], ssm_vec[:rank])
    b_normed, b_scale = norm_rows(projected[:, rank:b_end], ssm_vec[rank:b_end])
    c_normed, c_scale = norm_rows(projected[:, b_end:], ssm_vec[b_end:])
    dt_low = dt_normed.astype(BF)
    dt_pre = jnp.dot(dt_low, full_w_dt, preferred_element_type=F32) + full_dt_bias.astype(F32)
    step = jax.nn.softplus(dt_pre)
    rates = -jnp.exp(full_a_log.astype(F32))
    rate_rows = jnp.repeat((rates * LOG2E).T, seqs, axis=0)
    bc = jnp.concatenate([b_normed, c_normed], axis=1)
    part_one = bc.astype(BF)
    part_two = (bc - part_one.astype(F32)).astype(BF)
    part_three = (bc - part_one.astype(F32) - part_two.astype(F32)).astype(BF)
    stops = ((1.0 - same_docs[1]) * STOP).astype(BF)
    spare = jnp.zeros((rows, LANES - 6 * states - 1), BF)
    parts = jnp.concatenate([part_one, part_two, part_three, stops, spare], axis=1)
    shape = jax.ShapeDtypeStruct
    state_rows = states * seqs
    step, full_wide = lax.optimization_barrier((step, full_wide))
    full_gate, full_up = full_wide[:, :hidden_units], full_wide[:, hidden_units:]
    start, step_sum = state_call(
        entry_kernel,
        1,
        seqs,
        states,
        [parts, step, u_low, rate_rows],
        [shape((state_rows, channels), F32), shape((seqs, channels), F32)],
        exchange_scratch(count, seqs, states, channels),
        6,
        (0, 0),
    )
    y_state, mix_blocks = state_call(
        forward_kernel,
        2,
        seqs,
        states,
        [parts, step, u_low, rate_rows, start, w_mix],
        [shape((rows, channels), F32), shape((count,) + w_mix.shape, BF)],
        gather_sems(count // 2, w_mix.shape[1]),
        8,
        (1, 1),
    )
    full_mix = mix_blocks.reshape(width, 2 * channels)
    full_in_z, full_out_t = full_mix[:, :channels], full_mix[:, channels:]
    z_gate = jnp.dot(x_norm, full_in_z, preferred_element_type=F32)
    skip_vec = full_d_skip.astype(F32)
    u_rows = u_low.astype(F32)
    y_full = y_state + skip_vec * u_rows
    silu_z = jax.nn.silu(z_gate)
    g_low = (y_full * silu_z).astype(BF)
    grad_low = d_out.transpose(1, 0, 2).reshape(rows, width)
    blocks = lambda full: full.reshape(count, -1, full.shape[1])
    hidden, x_norm2, act_low, d_gate, d_up, norm2_sums, ffn_part, d_hidden, d_mix = ffn_call(
        g_low,
        full_out_t,
        head_part(x_rows),
        full_norm2.astype(F32)[None, :],
        grad_low,
        head_part(grad_low).astype(F32),
        [blocks(full_gate), blocks(full_up)],
        [w_down.astype(BF).T],
    )
    grad_norm2 = norm2_sums[0]
    grad_down = jnp.einsum("rd,rf->df", grad_low, act_low, preferred_element_type=F32)
    grad_gate = jnp.einsum("rd,rf->df", x_norm2, d_gate, preferred_element_type=F32)
    grad_up = jnp.einsum("rd,rf->df", x_norm2, d_up, preferred_element_type=F32)
    ffn_own = head_scatter(ffn_part)
    grad_out_w = jnp.einsum("rd,re->de", d_mix, g_low, preferred_element_type=F32)
    d_g = jnp.dot(d_mix, full_out_t, preferred_element_type=F32)
    d_y = d_g * silu_z
    d_z = (d_g * y_full * silu_slope(z_gate)).astype(BF)
    grad_skip = jnp.sum(d_y * u_rows, axis=0)
    grad_in_z = jnp.einsum("rd,re->de", x_norm, d_z, preferred_element_type=F32)
    big_grads = [
        owner_blocks(grad.astype(BF))
        for grad in (grad_down, grad_gate, grad_up, grad_out_w, grad_in_z)
    ]
    (last,) = state_call(
        adjoint_kernel,
        3,
        seqs,
        states,
        [parts, step, d_y, rate_rows, step_sum],
        [shape((state_rows, channels), F32)],
        exchange_scratch(count, seqs, states, channels),
        6,
        (0, 0),
    )
    last, ffn_own = lax.optimization_barrier((last, ffn_own))
    block_rows = head_gather((hidden + ffn_own).astype(BF))
    d_u_state, d_pre_low, d_bc, d_log, d_bias, *moved = state_call(
        backward_kernel,
        4,
        seqs,
        states,
        [parts, step, u_low, d_y, rate_rows, start, last] + big_grads,
        [
            shape((rows, channels), F32),
            shape((rows, channels), BF),
            shape((rows, LANES), F32),
            shape((states, channels), F32),
            shape((seqs, channels), F32),
        ]
        + [shape((count // 2,) + grad.shape[2:], BF) for grad in big_grads]
        + [shape((count // 2 - 1,) + grad.shape[2:], BF) for grad in big_grads],
        [
            pltpu.VMEM(((tokens + 1) * states, seqs, LANES), F32),
            pltpu.VMEM((rows, 2 * states * LANES), F32),
        ]
        + scatter_scratch(count, big_grads),
        30,
        (len(big_grads), 2 * len(big_grads)),
    )
    d_bc, block_rows = lax.optimization_barrier((d_bc, block_rows))
    block_out = block_rows.reshape(tokens, seqs, width).transpose(1, 0, 2)
    own_down, own_gate, own_up, own_out, own_in_z = (
        scatter_own(grad, given, came)
        for grad, given, came in zip(big_grads, moved[: len(big_grads)], moved[len(big_grads) :])
    )
    grad_alog = d_log.T * rates
    grad_bias = jnp.sum(d_bias, axis=0)
    grad_step_w = jnp.einsum("rk,re->ke", dt_low, d_pre_low, preferred_element_type=F32)
    d_dt_part = jnp.einsum("re,ke->rk", d_pre_low, full_w_dt, preferred_element_type=F32)
    d_stats = head_total(jnp.concatenate([d_dt_part, d_bc[:, : 2 * states]], axis=1), BF)
    d_dt_raw, grad_dt_gain = norm_back(
        projected[:, :rank], dt_scale, ssm_vec[:rank], d_stats[:, :rank]
    )
    d_b_raw, grad_b_gain = norm_back(
        projected[:, rank:b_end], b_scale, ssm_vec[rank:b_end], d_stats[:, rank:b_end]
    )
    d_c_raw, grad_c_gain = norm_back(
        projected[:, b_end:], c_scale, ssm_vec[b_end:], d_stats[:, b_end:]
    )
    d_proj = jnp.concatenate([d_dt_raw, d_b_raw, d_c_raw], axis=1)
    grad_ssm = jnp.concatenate([grad_dt_gain, grad_b_gain, grad_c_gain])
    grad_xproj = jnp.einsum("re,rk->ek", u_low, d_proj, preferred_element_type=F32)
    d_u = (
        d_y * skip_vec
        + d_u_state
        + jnp.einsum("rk,ek->re", d_proj, full_xproj, preferred_element_type=F32)
    )
    d_conv = d_u * silu_slope(x_conv)
    grad_conv_b = jnp.sum(d_conv, axis=0)
    d_extended = jnp.zeros((rows + halo, channels), F32)
    conv_grads = []
    for offset in range(taps):
        first = (taps - 1 - offset) * seqs
        masked = d_conv * same_docs[offset]
        conv_grads.append(jnp.sum(masked * extended[first : first + rows], axis=0))
        d_extended = d_extended + jnp.pad(
            conv_weight[offset] * masked, ((first, halo - first), (0, 0))
        )
    grad_conv_w = jnp.stack(conv_grads)
    from_next = shifted(d_extended[:halo].astype(BF), "seq", -1).astype(F32)
    d_inner = d_extended[halo:] + jnp.pad(from_next, ((rows - halo, 0), (0, 0)))
    d_inner_low = d_inner.astype(BF)
    grad_in_x = jnp.einsum("rd,re->de", x_norm, d_inner_low, preferred_element_type=F32)
    d_norm1 = head_scatter(
        jnp.einsum("re,de->rd", d_inner_low, full_in_x, preferred_element_type=F32)
        + jnp.einsum("re,de->rd", d_z, full_in_z, preferred_element_type=F32)
    )
    d_input_part, grad_norm1 = norm_back(head_part(x_rows), head_part(scale_one), norm1_vec, d_norm1)
    input_rows = head_gather((d_hidden + d_input_part).astype(BF)).astype(F32)
    grad_input = input_rows.reshape(tokens, seqs, width).transpose(1, 0, 2)

    grad_ssm = grad_ssm * (lax.axis_index("head") == 0).astype(F32)
    small = pack(
        [
            grad_xproj,
            grad_step_w.T,
            grad_alog,
            grad_conv_w.T,
            grad_conv_b[:, None],
            grad_bias[:, None],
            grad_skip[:, None],
        ],
        [grad_norm1, grad_norm2, grad_ssm],
    )
    small = scatter_rows(small.reshape(-1, pack_width), F32)
    small = jnp.concatenate([small[:per], head_total(small[per:], F32)])[None]
    small_fields, small_gains = unpack(small)
    own_in_x = scatter_rows(grad_in_x)
    return (
        block_out,
        grad_input,
        small_gains[0],
        own_in_x,
        own_in_z,
        small_fields[3].T,
        small_fields[4][:, 0],
        small_fields[0],
        small_gains[2],
        small_fields[1].T,
        small_fields[5][:, 0],
        small_fields[2],
        small_fields[6][:, 0],
        own_out.T,
        small_gains[1],
        own_gate,
        own_up,
        own_down.T,
    )


def solution(mesh):
    placed = (
        P(None, "seq", None),
        P(None, "seq"),
        P("seq"),
        P("seq", "head"),
        P("seq", "head"),
        P(None, ("head", "seq")),
        P(("head", "seq")),
        P(("head", "seq"), None),
        P("seq"),
        P(None, ("head", "seq")),
        P(("head", "seq")),
        P(("head", "seq"), None),
        P(("head", "seq")),
        P("head", "seq"),
        P("seq"),
        P("seq", "head"),
        P("seq", "head"),
        P("head", "seq"),
        P(None, "seq", None),
    )
    return jax.shard_map(
        shards,
        mesh=mesh,
        in_specs=placed,
        out_specs=(
            P(None, "seq", None),
            P(None, "seq", None),
            P("seq"),
            P("seq", "head"),
            P("seq", "head"),
            P(None, ("head", "seq")),
            P(("head", "seq")),
            P(("head", "seq"), None),
            P("seq"),
            P(None, ("head", "seq")),
            P(("head", "seq")),
            P(("head", "seq"), None),
            P(("head", "seq")),
            P("head", "seq"),
            P("seq"),
            P("seq", "head"),
            P("seq", "head"),
            P("head", "seq"),
        ),
        check_vma=False,
    )
```

```python
import functools

import jax
import jax.numpy as jnp
from jax import lax
from jax.experimental import pallas as pl
from jax.experimental.pallas import tpu as pltpu
from jax.sharding import PartitionSpec as P

EPS = 1e-06
LOG2E = 1.4426950408889634
LN2 = 0.6931471805599453
STOP = 1e30
LANES = 128
BF = jnp.bfloat16
F32 = jnp.float32


def shifted(value, axis, steps):
    count = lax.axis_size(axis)
    initial, last = (max(0, -steps), min(count, count - steps))
    return lax.ppermute(value, axis, [(source, source + steps) for source in range(initial, last)])


def norm_rows(values, gain_vec):
    inv_rms = lax.rsqrt(jnp.mean(values * values, axis=-1, keepdims=True) + EPS)
    return (values * inv_rms * gain_vec, inv_rms)


def norm_back(values, inv_rms, gain_vec, grad_rows):
    normed = values * inv_rms
    gain_grad = jnp.sum(grad_rows * normed, axis=0)
    scaled = grad_rows * gain_vec
    value_grad = inv_rms * (scaled - normed * jnp.mean(scaled * normed, axis=-1, keepdims=True))
    return (value_grad, gain_grad)


def silu_slope(values):
    logistic = jax.nn.sigmoid(values)
    return logistic * (1.0 + values * (1.0 - logistic))


GROUP = 4


def at_rows(index, size):
    return pl.ds(pl.multiple_of(index * size, size), size)


def spread(parts_ref, states, target, first=0):
    rows = parts_ref.shape[0]
    wide = 2 * LANES
    chunk = 256 if rows % 256 == 0 else rows
    source = lax.broadcasted_iota(jnp.int32, (LANES, wide), 0)
    half = lax.broadcasted_iota(jnp.int32, (LANES, wide), 1) // LANES
    columns = 2 * states

    def one(pair, carry):
        column = pair * 2 + half
        third = source % columns == column
        hot = jnp.where((source < 3 * columns) & third, 1.0, 0.0)
        stop = (column == columns) & (source == 3 * columns)
        hot = jnp.where(stop, 1.0, hot).astype(BF)
        for k in range(rows // chunk):
            target[pl.ds(k * chunk, chunk), at_rows(pair - first, wide)] = jnp.dot(
                parts_ref[pl.ds(k * chunk, chunk), :], hot, preferred_element_type=F32
            )
        return carry

    lax.fori_loop(first, states + 1, one, 0)


def group_tokens(ref, group, lanes, seqs):
    both = ref[at_rows(group, GROUP * seqs), lanes].astype(F32)
    return [both[k * seqs : (k + 1) * seqs] for k in range(GROUP)]


class Exchange:
    def __init__(self, count, forward, arrays, sems):
        place = lax.axis_index("seq")
        self.around = count // 2
        self.low, self.high = lax.rem(place, 2), place // 2
        self.place = place
        self.forward = forward
        self.arrays = arrays
        self.sems = sems
        self.mate = self.high * 2 + 1 - self.low

    def copies(self, steps, tile, source, device, kind):
        send, recv = self.sems[2 * kind], self.sems[2 * kind + 1]
        lanes = at_rows(tile, LANES)
        return [
            pltpu.make_async_remote_copy(
                src_ref=array.at[source, :, lanes],
                dst_ref=array.at[source, :, lanes],
                send_sem=send.at[k, steps, tile],
                recv_sem=recv.at[k, steps, tile],
                device_id={"seq": device},
                device_id_type=pl.DeviceIdType.MESH,
            )
            for k, array in enumerate(self.arrays)
        ]

    def away(self, steps):
        return self.high + steps if self.forward else self.high - steps

    def inside(self, pair):
        return pair < self.around if self.forward else pair >= 0

    def behind(self, steps):
        return self.high - steps if self.forward else self.high + steps

    def has_behind(self, steps):
        pair = self.behind(steps)
        return pair >= 0 if self.forward else pair < self.around

    def gives(self):
        return self.low == (0 if self.forward else 1)

    def hop(self, steps, tile):
        pair = jnp.clip(self.away(steps), 0, self.around - 1)
        return self.copies(steps, tile, self.place, pair * 2 + self.low, 0)

    def relay(self, steps, tile):
        pair = jnp.clip(self.behind(steps), 0, self.around - 1)
        return self.copies(steps, tile, pair * 2 + self.low, self.mate, 1)

    def start(self, tile):
        for steps in range(1, self.around):

            @pl.when(self.inside(self.away(steps)))
            def _():
                for copy in self.hop(steps, tile):
                    copy.start()

        @pl.when(self.gives())
        def _():
            for copy in self.relay(0, tile):
                copy.start()

    def pass_on(self, tile):
        for steps in range(1, self.around):

            @pl.when(self.has_behind(steps))
            def _():
                for copy in self.hop(steps, tile):
                    copy.wait_recv()
                for copy in self.relay(steps, tile):
                    copy.start()

    def arrive(self, tile):
        @pl.when(jnp.logical_not(self.gives()))
        def _():
            for copy in self.relay(0, tile):
                copy.wait_recv()

        for steps in range(1, self.around):

            @pl.when(self.has_behind(steps))
            def _():
                for copy in self.relay(steps, tile):
                    copy.wait_recv()

    def finish(self, tile):
        @pl.when(self.gives())
        def _():
            for copy in self.relay(0, tile):
                copy.wait_send()

        for steps in range(1, self.around):

            @pl.when(self.inside(self.away(steps)))
            def _():
                for copy in self.hop(steps, tile):
                    copy.wait_send()

            @pl.when(self.has_behind(steps))
            def _():
                for copy in self.relay(steps, tile):
                    copy.wait_send()


def chained(state, block_ref, sums_ref, rate_ref, source, lanes, seqs):
    total = sums_ref[source, :, lanes]
    block = block_ref[source, :, lanes].astype(F32)
    after = []
    for n in range(len(state)):
        decay = jnp.exp2(total * rate_ref[pl.ds(n * seqs, seqs), lanes])
        after.append(decay * state[n] + block[n * seqs : (n + 1) * seqs])
    return tuple(after)


def state_blocks(ref, lanes, seqs, states):
    return tuple(ref[pl.ds(n * seqs, seqs), lanes] for n in range(states))


def put_blocks(ref, lead, lanes, blocks):
    stacked = jnp.concatenate(blocks, axis=0)
    if lead is None:
        ref[:, lanes] = stacked.astype(ref.dtype)
    else:
        ref[lead, :, lanes] = stacked.astype(ref.dtype)


def entry_kernel(
    count, seqs, states, parts_ref, step_ref, u_ref, rate_ref, start_ref, sum_ref, *scratch
):
    spread_ref, ends, sums, *sems = scratch
    rows, channels = step_ref.shape
    tokens, tiles = rows // seqs, channels // LANES
    stop_lanes = pl.ds(2 * states * LANES, LANES)
    exchange = Exchange(count, True, (ends, sums), sems)
    place = exchange.place
    zero = jnp.zeros((seqs, LANES), F32)
    greet_pairs(count)
    spread(parts_ref, states, spread_ref)

    def local(tile, carry):
        lanes = at_rows(tile, LANES)

        def one(group, carry):
            state, total = carry
            us = group_tokens(u_ref, group, lanes, seqs)
            for k in range(GROUP):
                here = at_rows(group * GROUP + k, seqs)
                step = step_ref[here, lanes]
                drive = step * us[k]
                stop = step + spread_ref[here, stop_lanes]
                total = total + stop
                fresh = []
                for n in range(states):
                    decay = jnp.exp2(stop * rate_ref[pl.ds(n * seqs, seqs), lanes])
                    b_one = spread_ref[here, pl.ds(n * LANES, LANES)]
                    fresh.append(decay * state[n] + drive * b_one)
                state = tuple(fresh)
            return state, total

        state, total = lax.fori_loop(0, tokens // GROUP, one, ((zero,) * states, zero))
        put_blocks(ends, place, lanes, state)
        sums[place, :, lanes] = total
        exchange.start(tile)
        return carry

    lax.fori_loop(0, tiles, local, 0)
    finish_exchange(exchange, tiles, lambda first, lanes: lax.fori_loop(
        0,
        place,
        lambda source, state: chained(state, ends, sums, rate_ref, source, lanes, seqs),
        first,
    ), start_ref, states, zero)
    sum_ref[...] = sums[place]


def finish_exchange(exchange, tiles, chain, target_ref, states, zero, relay=True):
    def pass_on(tile, carry):
        exchange.pass_on(tile)
        return carry

    if relay:
        lax.fori_loop(0, tiles, pass_on, 0)

    def take(tile, carry):
        lanes = at_rows(tile, LANES)
        exchange.arrive(tile)
        put_blocks(target_ref, None, lanes, chain((zero,) * states, lanes))
        return carry

    lax.fori_loop(0, tiles, take, 0)

    def finish(tile, carry):
        exchange.finish(tile)
        return carry

    lax.fori_loop(0, tiles, finish, 0)


def forward_kernel(
    count,
    seqs,
    states,
    parts_ref,
    step_ref,
    u_ref,
    rate_ref,
    start_ref,
    block_ref,
    y_ref,
    gathered_ref,
    *scratch,
):
    spread_ref, *sems = scratch
    gather = BlockGather(count, block_ref, gathered_ref, sems)
    rows, channels = step_ref.shape
    tokens, tiles = rows // seqs, channels // LANES
    stop_lanes = pl.ds(2 * states * LANES, LANES)
    zero = jnp.zeros((seqs, LANES), F32)
    greet_pairs(count)
    gather.start()
    spread(parts_ref, states, spread_ref)

    def whole(tile, carry):
        lanes = at_rows(tile, LANES)

        def one(group, state):
            us = group_tokens(u_ref, group, lanes, seqs)
            for k in range(GROUP):
                here = at_rows(group * GROUP + k, seqs)
                step = step_ref[here, lanes]
                drive = step * us[k]
                stop = step + spread_ref[here, stop_lanes]
                fresh = []
                out = zero
                for n in range(states):
                    decay = jnp.exp2(stop * rate_ref[pl.ds(n * seqs, seqs), lanes])
                    b_one = spread_ref[here, pl.ds(n * LANES, LANES)]
                    value = decay * state[n] + drive * b_one
                    out = out + value * spread_ref[here, pl.ds((states + n) * LANES, LANES)]
                    fresh.append(value)
                y_ref[here, lanes] = out
                state = tuple(fresh)
            return state

        lax.fori_loop(0, tokens // GROUP, one, state_blocks(start_ref, lanes, seqs, states))
        for piece in range(gather.pieces):
            if 3 * piece + 2 < tiles:

                @pl.when(tile == 3 * piece + 2)
                def _():
                    gather.relay(piece)

        return carry

    lax.fori_loop(0, tiles, whole, 0)
    for piece in range(gather.pieces):
        if 3 * piece + 2 >= tiles:
            gather.relay(piece)
    gather.finish()


def adjoint_kernel(
    count,
    seqs,
    states,
    parts_ref,
    step_ref,
    dy_ref,
    rate_ref,
    sum_ref,
    norm_ref,
    low_ref,
    act_ref,
    dgate_ref,
    dup_ref,
    part_ref,
    hidden_ref,
    last_ref,
    gdown_ref,
    ggate_ref,
    gup_ref,
    out_ref,
    *scratch,
):
    spread_ref, ends, sums, *scratch = scratch
    sems, (half, give, take, kept, block_ref, buffer, sum_sems) = scratch[:4], scratch[4:]
    total = HeadSum(part_ref, half, give, take, block_ref, sum_sems)
    chunks = kept.shape[0]
    quarter = kept.shape[1]
    rows, channels = step_ref.shape
    tokens, tiles = rows // seqs, channels // LANES
    groups = tokens // GROUP
    stop_lanes = pl.ds(states * LANES, LANES)
    exchange = Exchange(count, False, (ends, sums), sems)
    place = exchange.place
    zero = jnp.zeros((seqs, LANES), F32)
    greet_pairs(count, True)
    for chunk in range(chunks):
        total.near_copy(chunk).start()
    spread(parts_ref, states, spread_ref, states // 2)

    def own(tile, carry):
        lanes = at_rows(tile, LANES)

        def one(back, grads):
            group = groups - 1 - back
            for k in reversed(range(GROUP)):
                here = at_rows(group * GROUP + k, seqs)
                stop = step_ref[here, lanes] + spread_ref[here, stop_lanes]
                dy = dy_ref[here, lanes]
                fresh = []
                for n in range(states):
                    decay = jnp.exp2(stop * rate_ref[pl.ds(n * seqs, seqs), lanes])
                    c_one = spread_ref[here, pl.ds(n * LANES, LANES)]
                    fresh.append(decay * (grads[n] + dy * c_one))
                grads = tuple(fresh)
            return grads

        put_blocks(ends, place, lanes, lax.fori_loop(0, groups, one, (zero,) * states))
        sums[place, :, lanes] = sum_ref[:, lanes]
        exchange.start(tile)
        return carry

    lax.fori_loop(0, tiles, own, 0)
    for chunk in range(chunks):
        total.fold(chunk, kept)
    around, _, shard, units = gdown_ref.shape
    together = max(1, 384 // (2 * shard))
    wide = together * 2 * shard

    def multiply(block):
        lanes = pl.ds(block * wide, wide)
        pairs = pl.ds(block * together, together)
        mine = norm_ref[:, lanes].T
        for d_ref, grad_ref in ((dgate_ref, ggate_ref), (dup_ref, gup_ref)):
            grad = jnp.dot(mine, d_ref[...], preferred_element_type=F32).astype(BF)
            grad_ref[pairs] = grad.reshape(together, 2, shard, units)
        grad = jnp.dot(low_ref[:, lanes].T, act_ref[...], preferred_element_type=F32).astype(BF)
        gdown_ref[pairs] = grad.reshape(together, 2, shard, units)

    blocks = list(range(around // together))
    for block in blocks[:2]:
        multiply(block)

    def pass_on(tile, carry):
        exchange.pass_on(tile)
        return carry

    lax.fori_loop(0, tiles, pass_on, 0)

    def bring(chunk, carry):
        total.far_copy(chunk).wait_recv()
        here = at_rows(chunk, quarter)
        rows_out = hidden_ref[here, :] + kept[chunk] + take[chunk].astype(F32)
        block_ref[total.own_rows(chunk), :] = rows_out.astype(BF)
        total.far_back(chunk).start()
        return carry

    lax.fori_loop(0, chunks, bring, 0)
    for block in blocks[2:]:
        multiply(block)
    finish_exchange(exchange, tiles, lambda first, lanes: lax.fori_loop(
        0,
        count - 1 - place,
        lambda hop, state: chained(state, ends, sums, rate_ref, count - 1 - hop, lanes, seqs),
        first,
    ), last_ref, states, zero, False)

    def spread_out(chunk, carry):
        total.far_back(chunk).wait_recv()
        total.near_back(chunk).start()
        return carry

    lax.fori_loop(0, chunks, spread_out, 0)

    def finish(chunk, carry):
        total.near_back(chunk).wait_recv()
        put_sequences(out_ref, block_ref, chunk, 4 * quarter, buffer)
        total.finish(chunk)
        return carry

    lax.fori_loop(0, chunks, finish, 0)


def backward_kernel(
    count,
    seqs,
    states,
    parts_ref,
    step_ref,
    u_ref,
    dy_ref,
    rate_ref,
    start_ref,
    last_ref,
    *refs,
):
    kinds = (len(refs) - 35) // 3
    dtlow_ref, wdt_ref, xproj_ref, gain_ref, taps_ref, *refs = refs
    xconv_ref, ext_ref, proj_ref, *refs = refs
    grad_refs, refs = refs[:kinds], refs[kinds:]
    inner_ref, ssm_ref, gx_ref, gw_ref, dlog_ref, sums_ref, *refs = refs
    given_refs, came_refs, scratch = refs[:kinds], refs[kinds : 2 * kinds], refs[2 * kinds :]
    spread_ref, held, acc, du_ref, dpre_ref, *scratch = scratch
    sent, got, tail, edge, from_next, head_sems, edge_sems, load_sems, *scratch = scratch
    rows, channels = step_ref.shape
    tokens, tiles = rows // seqs, channels // LANES
    groups = tokens // GROUP
    stop_lanes = pl.ds(2 * states * LANES, LANES)
    place = lax.axis_index("seq")
    low, high = lax.rem(place, 2), place // 2
    zero = jnp.zeros((seqs, LANES), F32)
    greet_pairs(count, True, True)
    scatter = PairScatter(count, grad_refs, given_refs, came_refs, scratch)
    scatter.start()
    spread(parts_ref, states, spread_ref)

    def clear(row, carry):
        acc[at_rows(row, seqs), :] = jnp.zeros((seqs, acc.shape[1]), F32)
        return carry

    lax.fori_loop(0, tokens, clear, 0)

    def whole(tile, carry):
        lanes = at_rows(tile, LANES)

        def again(group, state):
            us = group_tokens(u_ref, group, lanes, seqs)
            for k in range(GROUP):
                token = group * GROUP + k
                here = at_rows(token, seqs)
                step = step_ref[here, lanes]
                drive = step * us[k]
                stop = step + spread_ref[here, stop_lanes]
                fresh = []
                for n in range(states):
                    held[token * states + n] = state[n]
                    decay = jnp.exp2(stop * rate_ref[pl.ds(n * seqs, seqs), lanes])
                    b_one = spread_ref[here, pl.ds(n * LANES, LANES)]
                    fresh.append(decay * state[n] + drive * b_one)
                state = tuple(fresh)
            return state

        state = lax.fori_loop(0, groups, again, state_blocks(start_ref, lanes, seqs, states))
        for n in range(states):
            held[tokens * states + n] = state[n]
        grads = state_blocks(last_ref, lanes, seqs, states)

        def one(back, carry):
            grads, logs, bias = carry
            group = groups - 1 - back
            us = group_tokens(u_ref, group, lanes, seqs)
            pres = [None] * GROUP
            for k in reversed(range(GROUP)):
                token = group * GROUP + k
                here = at_rows(token, seqs)
                step = step_ref[here, lanes]
                dy = dy_ref[here, lanes]
                drive = step * us[k]
                stop = step + spread_ref[here, stop_lanes]
                fresh, fresh_logs = [], []
                on_b, on_rate = zero, zero
                for n in range(states):
                    at = token * states + n
                    on_lanes = pl.ds(n * LANES, LANES)
                    other_lanes = pl.ds((states + n) * LANES, LANES)
                    rate = rate_ref[pl.ds(n * seqs, seqs), lanes]
                    decay = jnp.exp2(stop * rate)
                    lam = grads[n] + dy * spread_ref[here, other_lanes]
                    carried = lam * decay
                    fresh.append(carried)
                    kept = carried * held[at]
                    on_b = on_b + lam * spread_ref[here, on_lanes]
                    on_rate = on_rate + kept * rate
                    fresh_logs.append(logs[n] + kept * step)
                    acc[here, on_lanes] = acc[here, on_lanes] + lam * drive
                    acc[here, other_lanes] = acc[here, other_lanes] + dy * held[at + states]
                du_ref[here, lanes] = step * on_b
                series = step * (1.0 - step * (0.5 - step * (1.0 / 6.0 - step * (1.0 / 24.0))))
                slope = jnp.where(step < 0.05, series, 1.0 - jnp.exp2(step * (-LOG2E)))
                pres[k] = (on_rate * LN2 + us[k] * on_b) * slope
                bias = bias + pres[k]
                grads, logs = tuple(fresh), tuple(fresh_logs)
            dpre_ref[at_rows(group, GROUP * seqs), lanes] = jnp.concatenate(pres, 0).astype(BF)
            return grads, logs, bias

        grads, logs, bias = lax.fori_loop(0, groups, one, (grads, (zero,) * states, zero))
        dlog_ref[:, lanes] = jnp.concatenate(
            [jnp.sum(log, axis=0, keepdims=True) for log in logs], axis=0
        )
        sums_ref[pl.ds(5 * seqs, seqs), lanes] = bias
        for k in range(tiles):

            @pl.when(tile == k)
            def _():
                scatter.advance(k)

        return carry

    lax.fori_loop(0, tiles, whole, 0)

    wide = 2 * LANES
    chunk = 256 if rows % 256 == 0 else rows
    target = lax.broadcasted_iota(jnp.int32, (wide, LANES), 1)
    half = lax.broadcasted_iota(jnp.int32, (wide, LANES), 0) // LANES
    past = taps_ref.shape[0] // 2 - 1
    dbc_ref = spread_ref.at[:, pl.ds((past + 2) * LANES, LANES)]
    dbc_ref[...] = jnp.zeros((rows, LANES), F32)

    def reduce(pair, carry):
        hot = jnp.where(target == LANES - 2 * states + pair * 2 + half, 1.0, 0.0).astype(BF)
        for k in range(rows // chunk):
            here = pl.ds(k * chunk, chunk)
            values = acc[here, at_rows(pair, wide)]
            main = values.astype(BF)
            rest = (values - main.astype(F32)).astype(BF)
            dbc_ref[here, :] += jnp.dot(main, hot, preferred_element_type=F32) + jnp.dot(
                rest, hot, preferred_element_type=F32
            )
        return carry

    lax.fori_loop(0, states, reduce, 0)

    scatter.advance(tiles)

    span = tokens + past
    value_at = tiles * span
    tap_at = [value_at + k * span for k in range(past + 1)]
    proj_lanes = pl.ds((past + 1) * LANES, LANES)
    loads = [
        pltpu.make_async_copy(xconv_ref, acc.at[:, pl.ds(0, channels)], load_sems.at[tiles]),
        pltpu.make_async_copy(proj_ref, spread_ref.at[:, proj_lanes], load_sems.at[tiles + 1]),
    ]
    for tile in range(tiles):
        source = ext_ref.at[:, :, pl.ds(tile * LANES, LANES)]
        target_tiles = held.at[pl.ds(tile * span, span)]
        loads.append(pltpu.make_async_copy(source, target_tiles, load_sems.at[tile]))
    for load in loads:
        load.start()
    head = lax.axis_index("head")
    near = {"head": head // 2 * 2 + 1 - lax.rem(head, 2)}
    far = {"head": lax.rem(head + 2, 4)}
    trade = [
        pltpu.make_async_remote_copy(
            src_ref=sent.at[k],
            dst_ref=got.at[k],
            send_sem=head_sems.at[0, k],
            recv_sem=head_sems.at[1, k],
            device_id=device,
            device_id_type=pl.DeviceIdType.MESH,
        )
        for k, device in enumerate((near, far))
    ]
    for k in range(rows // chunk):
        here = pl.ds(k * chunk, chunk)
        stats = jnp.dot(dpre_ref[here, :], wdt_ref[...], preferred_element_type=F32)
        sent[0, here, :] = (dbc_ref[here, :] + stats).astype(BF)
    trade[0].start()

    source = lax.broadcasted_iota(jnp.int32, (LANES, LANES), 0)
    for k in range(1, past + 1):
        hot = jnp.where(source == 6 * states + k, 1.0, 0.0).astype(BF)
        for m in range(rows // chunk):
            here = pl.ds(m * chunk, chunk)
            spread_ref[here, pl.ds(k * LANES, LANES)] = jnp.dot(
                parts_ref[here, :], hot, preferred_element_type=F32
            )
    scatter.advance(tiles + 1)
    trade[0].wait_recv()
    for k in range(rows // chunk):
        here = pl.ds(k * chunk, chunk)
        sent[1, here, :] = (sent[0, here, :].astype(F32) + got[0, here, :].astype(F32)).astype(BF)
    trade[1].start()

    def step_weights(tile, carry):
        lanes = at_rows(tile, LANES)
        gw_ref[lanes, :] = jnp.dot(
            dpre_ref[:, lanes].T, dtlow_ref[...], preferred_element_type=F32
        )
        return carry

    lax.fori_loop(0, tiles, step_weights, 0)
    scatter.advance(tiles + 2)
    trade[0].wait_send()
    for load in loads:
        load.wait()
    trade[1].wait_recv()
    ssm_ref[...] = jnp.zeros(ssm_ref.shape, F32)
    for k in range(rows // chunk):
        here = pl.ds(k * chunk, chunk)
        stats = sent[1, here, :].astype(F32) + got[1, here, :].astype(F32)
        d_proj, gain_rows = stats_back(stats, spread_ref[here, proj_lanes], gain_ref[...], states)
        sent[0, here, :] = d_proj.astype(BF)
        share = jnp.sum(gain_rows, axis=0, keepdims=True)
        ssm_ref[...] += jnp.broadcast_to(share, ssm_ref.shape)
    block = 16
    size = block * seqs
    edge[...] = jnp.zeros(edge.shape, BF)

    def convolve(tile, carry):
        lanes = at_rows(tile, LANES)
        gx_ref[lanes, :] = jnp.dot(u_ref[:, lanes].T, sent[0], preferred_element_type=F32)
        weights = xproj_ref[lanes, :]
        skip = taps_ref[pl.ds(past + 1, 1), lanes]
        ext_at = tile * span

        def one(part, sums):
            here = at_rows(part, size)
            token = part * block
            d_u = du_ref[here, lanes] + dy_ref[here, lanes] * skip
            d_u = d_u + transposed_dot(sent[0, here, :], weights)
            conv = acc[here, lanes]
            logistic = 1.0 / (1.0 + jnp.exp(-conv))
            d_conv = d_u * logistic * (1.0 + conv * (1.0 - logistic))
            fresh = []
            for k in range(past + 1):
                masked = d_conv
                if k:
                    masked = d_conv * spread_ref[here, pl.ds(k * LANES, LANES)]
                before = held[pl.ds(ext_at + token + past - k, block)]
                blocks = masked.reshape(block, seqs, LANES)
                fresh.append(sums[k] + jnp.sum(blocks * before, axis=0))
                tap = taps_ref[pl.ds(k, 1), lanes]
                held[pl.ds(tap_at[k] + token, block)] = blocks * tap[None]
            fresh.append(sums[past + 1] + jnp.sum(d_conv.reshape(block, seqs, LANES), axis=0))
            return tuple(fresh)

        sums = lax.fori_loop(0, rows // size, one, (zero,) * (past + 2))
        for k in range(past + 2):
            sums_ref[pl.ds(k * seqs, seqs), lanes] = sums[k]
        for k in range(1, past + 1):
            for later in range(past):
                held[tap_at[k] + tokens + later] = zero

        def gather(part, carry):
            token = part * block
            total = held[pl.ds(tap_at[0] + token, block)]
            for k in range(1, past + 1):
                total = total + held[pl.ds(tap_at[k] + token + k, block)]
            total = total.reshape(size, LANES)
            inner_ref[at_rows(part, size), lanes] = total.astype(BF)

            @pl.when(part == rows // size - 1)
            def _():
                tail[:, lanes] = total[size - tail.shape[0] :]

            return carry

        lax.fori_loop(0, rows // size, gather, 0)
        first = [zero] * (tail.shape[0] // seqs - past)
        for token in range(past):
            total = zero
            for k in range(past - token, past + 1):
                total = total + held[tap_at[k] + token - past + k]
            first.append(total)
        edge[:, lanes] = jnp.concatenate(first, axis=0).astype(BF)
        for k in range(tiles):

            @pl.when(tile == k)
            def _():
                scatter.advance(tiles + 3 + k)

        return carry

    lax.fori_loop(0, tiles, convolve, 0)
    hand = pltpu.make_async_remote_copy(
        src_ref=edge,
        dst_ref=from_next,
        send_sem=edge_sems.at[0],
        recv_sem=edge_sems.at[1],
        device_id={"seq": lax.rem(place + count - 1, count)},
        device_id_type=pl.DeviceIdType.MESH,
    )

    @pl.when(place > 0)
    def _():
        hand.start()

    @pl.when(place < count - 1)
    def _():
        hand.wait_recv()
        last_rows = pl.ds(rows - tail.shape[0], tail.shape[0])
        inner_ref[last_rows, :] = (tail[...] + from_next[...].astype(F32)).astype(BF)

    @pl.when(place > 0)
    def _():
        hand.wait_send()

    trade[1].wait_send()
    for turn in range(2 * tiles + 3, scatter.turns):
        scatter.advance(turn)
    scatter.finish()


def stats_back(stats, projected, gains, states):
    rank = LANES - 2 * states
    lane = lax.broadcasted_iota(jnp.int32, stats.shape, 1)
    parts = [
        (lane < rank, rank),
        ((lane >= rank) & (lane < rank + states), states),
        (lane >= rank + states, states),
    ]

    def means(values):
        total = jnp.zeros_like(values)
        for inside, size in parts:
            mean = jnp.sum(jnp.where(inside, values, 0.0), axis=1, keepdims=True) / size
            total = jnp.where(inside, mean, total)
        return total

    scale = lax.rsqrt(means(projected * projected) + EPS)
    normed = projected * scale
    scaled = stats * gains
    return scale * (scaled - normed * means(scaled * normed)), stats * normed


class PairScatter:
    def __init__(self, count, grads, given, came, scratch):
        place = lax.axis_index("seq")
        self.around = count // 2
        self.low, self.high = lax.rem(place, 2), place // 2
        self.grads, self.given, self.came = grads, given, came
        self.mine_buf, self.given_buf, self.sum_buf = scratch[:3]
        self.swap_send, self.swap_recv, self.hop_send, self.hop_recv, self.load_sem = scratch[3:]
        self.items = [(k, steps) for k in range(len(grads)) for steps in range(1, self.around)]
        self.turns = len(self.items) + 1

    def pair(self, steps):
        return lax.rem(self.high + steps, self.around)

    def swap(self, kind, steps):
        return pltpu.make_async_remote_copy(
            src_ref=self.grads[kind].at[self.pair(steps), 1 - self.low],
            dst_ref=self.given[kind].at[steps],
            send_sem=self.swap_send.at[kind, steps],
            recv_sem=self.swap_recv.at[kind, steps],
            device_id={"seq": self.high * 2 + 1 - self.low},
            device_id_type=pl.DeviceIdType.MESH,
        )

    def hop(self, item):
        kind, steps = self.items[item]
        wide = self.grads[kind].shape[-1]
        return pltpu.make_async_remote_copy(
            src_ref=self.sum_buf.at[item % 2, :, pl.ds(0, wide)],
            dst_ref=self.came[kind].at[steps - 1],
            send_sem=self.hop_send.at[kind, steps],
            recv_sem=self.hop_recv.at[kind, steps],
            device_id={"seq": self.pair(steps) * 2 + self.low},
            device_id_type=pl.DeviceIdType.MESH,
        )

    def loads(self, item):
        kind, steps = self.items[item]
        lanes = pl.ds(0, self.grads[kind].shape[-1])
        return [
            pltpu.make_async_copy(
                self.grads[kind].at[self.pair(steps), self.low],
                self.mine_buf.at[item % 2, :, lanes],
                self.load_sem.at[item % 2, 0],
            ),
            pltpu.make_async_copy(
                self.given[kind].at[steps],
                self.given_buf.at[item % 2, :, lanes],
                self.load_sem.at[item % 2, 1],
            ),
        ]

    def start(self):
        for kind, steps in self.items:
            self.swap(kind, steps).start()
        for kind in range(len(self.grads)):
            self.swap(kind, 0).start()

    def advance(self, turn):
        if turn < len(self.items):
            self.swap(*self.items[turn]).wait_recv()
            for load in self.loads(turn):
                load.start()
        item = turn - 1
        if 0 <= item < len(self.items):
            for load in self.loads(item):
                load.wait()
            if item >= 2:
                self.hop(item - 2).wait_send()
            wide = self.grads[self.items[item][0]].shape[-1]
            rows = self.mine_buf.shape[1]

            def add(row, carry):
                here = at_rows(row, 16)
                lanes = pl.ds(0, wide)
                total = self.mine_buf[item % 2, here, lanes].astype(F32) + self.given_buf[
                    item % 2, here, lanes
                ].astype(F32)
                self.sum_buf[item % 2, here, lanes] = total.astype(self.sum_buf.dtype)
                return carry

            lax.fori_loop(0, rows // 16, add, 0)
            self.hop(item).start()

    def finish(self):
        for item in range(max(0, len(self.items) - 2), len(self.items)):
            self.hop(item).wait_send()
        for item in range(len(self.items)):
            self.hop(item).wait_recv()
            self.swap(*self.items[item]).wait_send()
        for kind in range(len(self.grads)):
            self.swap(kind, 0).wait()


def scatter_scratch(count, grads):
    rows = grads[0].shape[2]
    wide = max(grad.shape[3] for grad in grads)
    sems = pltpu.SemaphoreType.DMA((len(grads), count // 2))
    buffer = pltpu.VMEM((2, rows, wide), grads[0].dtype)
    return [buffer] * 3 + [sems] * 4 + [pltpu.SemaphoreType.DMA((2, 2))]


def exchange_scratch(count, seqs, states, channels):
    sems = pltpu.SemaphoreType.DMA((2, count // 2, channels // LANES))
    return [
        pltpu.VMEM((count, states * seqs, channels), BF),
        pltpu.VMEM((count, seqs, channels), F32),
    ] + [sems] * 4


def state_call(body, ident, seqs, states, columns, ins, outs, scratch, ops, hosted):
    count = lax.axis_size("seq")
    rows, channels = ins[1].shape
    in_vmem = pl.BlockSpec(memory_space=pltpu.VMEM)
    anywhere = pl.BlockSpec(memory_space=pl.ANY)
    return pl.pallas_call(
        functools.partial(body, count, seqs, states),
        in_specs=[in_vmem] * (len(ins) - hosted[0]) + [anywhere] * hosted[0],
        out_specs=tuple([in_vmem] * (len(outs) - hosted[1]) + [anywhere] * hosted[1]),
        out_shape=tuple(outs),
        scratch_shapes=[pltpu.VMEM((rows, columns * LANES), F32)] + scratch,
        compiler_params=pltpu.CompilerParams(
            collective_id=ident, has_side_effects=True, vmem_limit_bytes=62 * 1024 * 1024
        ),
        cost_estimate=pl.CostEstimate(
            flops=ops * rows * channels * states,
            bytes_accessed=16 * 1024 * 1024,
            transcendentals=0,
        ),
    )(*ins)


class BlockGather:
    def __init__(self, count, source, target, sems):
        place = lax.axis_index("seq")
        self.around = count // 2
        self.low, self.high = lax.rem(place, 2), place // 2
        self.place = place
        self.source, self.target = source, target
        self.hop_send, self.hop_recv, self.swap_send, self.swap_recv, self.local_sem = sems
        self.mate = self.high * 2 + 1 - self.low
        self.pieces = pieces_of(source.shape[-1])

    def pair(self, steps):
        return lax.rem(self.high + steps + self.around, self.around) * 2 + self.low

    def lanes(self, piece):
        size = self.source.shape[-1] // self.pieces
        return pl.ds(piece * size, size)

    def local(self):
        return pltpu.make_async_copy(self.source, self.target.at[self.place], self.local_sem.at[0])

    def hop(self, piece, steps):
        return pltpu.make_async_remote_copy(
            src_ref=self.source.at[:, self.lanes(piece)],
            dst_ref=self.target.at[self.place, :, self.lanes(piece)],
            send_sem=self.hop_send.at[piece, steps],
            recv_sem=self.hop_recv.at[piece, steps],
            device_id={"seq": self.pair(steps)},
            device_id_type=pl.DeviceIdType.MESH,
        )

    def swap(self, piece, steps):
        block = self.target.at[self.pair(-steps), :, self.lanes(piece)]
        return pltpu.make_async_remote_copy(
            src_ref=block if steps else self.source.at[:, self.lanes(piece)],
            dst_ref=block,
            send_sem=self.swap_send.at[piece, steps],
            recv_sem=self.swap_recv.at[piece, steps],
            device_id={"seq": self.mate},
            device_id_type=pl.DeviceIdType.MESH,
        )

    def start(self):
        self.local().start()
        for piece in range(self.pieces):
            for steps in range(1, self.around):
                self.hop(piece, steps).start()
        for piece in range(self.pieces):
            self.swap(piece, 0).start()

    def relay(self, piece):
        for steps in range(1, self.around):
            self.hop(piece, steps).wait_recv()
            self.swap(piece, steps).start()

    def finish(self):
        self.local().wait()
        for piece in range(self.pieces):
            for steps in range(1, self.around):
                self.hop(piece, steps).wait_send()
            for steps in range(self.around):
                self.swap(piece, steps).wait()


def pieces_of(width):
    for size in (384, 256):
        if width % size == 0:
            return width // size
    return 1


def gather_sems(around, width):
    pieces = pieces_of(width)
    return [pltpu.SemaphoreType.DMA((pieces, around))] * 4 + [pltpu.SemaphoreType.DMA((1,))]


def greet_pairs(count, heads=False, ring=False):
    place = lax.axis_index("seq")
    around = count // 2
    low, high = lax.rem(place, 2), place // 2
    barrier = pltpu.get_barrier_semaphore()
    peers = [lax.rem(high + steps, around) * 2 + low for steps in range(1, around)]
    peers = [{"seq": device} for device in peers + [high * 2 + 1 - low]]
    if heads:
        head = lax.axis_index("head")
        low, high = lax.rem(head, 2), head // 2
        peers += [{"head": high * 2 + 1 - low}, {"head": 2 - 2 * high + low}]
    if ring:
        peers += [{"seq": lax.rem(place + 1, count)}, {"seq": lax.rem(place + count - 1, count)}]
    for device in peers:
        pl.semaphore_signal(barrier, inc=1, device_id=device, device_id_type=pl.DeviceIdType.MESH)
    pl.semaphore_wait(barrier, len(peers))


class HeadSum:
    def __init__(self, part, half, give, take, whole, sems):
        head = lax.axis_index("head")
        self.low, self.high = lax.rem(head, 2), head // 2
        self.near = {"head": self.high * 2 + 1 - self.low}
        self.far = {"head": 2 - 2 * self.high + self.low}
        self.part, self.half, self.give, self.take, self.whole = part, half, give, take, whole
        self.sems = sems
        self.size = half.shape[1]

    def copy(self, source, target, kind, chunk, device):
        return pltpu.make_async_remote_copy(
            src_ref=source,
            dst_ref=target,
            send_sem=self.sems.at[kind, 0, chunk],
            recv_sem=self.sems.at[kind, 1, chunk],
            device_id=device,
            device_id_type=pl.DeviceIdType.MESH,
        )

    def rows(self, chunk, bit):
        start = pl.multiple_of((chunk * 2 + bit) * self.size, self.size)
        return pl.ds(start, self.size)

    def own_rows(self, chunk):
        quarter = self.size // 2
        start = (chunk * 2 + self.low) * self.size + self.high * quarter
        return pl.ds(pl.multiple_of(start, quarter), quarter)

    def near_copy(self, chunk):
        return self.copy(
            self.part.at[self.rows(chunk, 1 - self.low)], self.half.at[chunk], 0, chunk, self.near
        )

    def far_copy(self, chunk):
        return self.copy(self.give.at[chunk], self.take.at[chunk], 1, chunk, self.far)

    def far_back(self, chunk):
        here = self.whole.at[self.own_rows(chunk)]
        return self.copy(here, here, 2, chunk, self.far)

    def near_back(self, chunk):
        here = self.whole.at[self.rows(chunk, self.low)]
        return self.copy(here, here, 3, chunk, self.near)

    def fold(self, chunk, kept):
        self.near_copy(chunk).wait_recv()
        quarter = self.size // 2
        base = (chunk * 2 + self.low) * self.size
        for mine in (False, True):
            bit = self.high if mine else 1 - self.high
            start = pl.multiple_of(bit * quarter, quarter)
            at = pl.multiple_of(base + bit * quarter, quarter)
            total = self.part[pl.ds(at, quarter), :].astype(F32)
            total = total + self.half[chunk, pl.ds(start, quarter), :].astype(F32)
            if mine:
                kept[chunk] = total
            else:
                self.give[chunk] = total.astype(BF)
                self.far_copy(chunk).start()

    def finish(self, chunk):
        for copy in (self.near_copy, self.far_copy, self.far_back, self.near_back):
            copy(chunk).wait_send()


def put_sequences(target, rows_ref, chunk, size, buffer):
    seqs = target.shape[0]
    span = size // seqs
    for m in range(buffer.shape[0]):
        lanes = pl.ds(m * LANES, LANES)
        buffer[m] = rows_ref[at_rows(chunk, size), lanes].astype(F32)
        for k in range(seqs):
            rows = buffer[m, pl.ds(k, span, stride=seqs), :]
            target[k, at_rows(chunk, span), lanes] = rows.astype(target.dtype)


def transposed_dot(left, right):
    return lax.dot_general(left, right, (((1,), (1,)), ((), ())), preferred_element_type=F32)


def ffn_kernel(count, chunks, *refs):
    g_ref, out_ref, x_ref, gain_ref, low_ref, gate_ref, up_shard, down_shard, *refs = refs
    hidden_ref, norm_ref, act_ref, dgate_ref, dup_ref, dnorm_gain_ref, part_out_ref, *refs = refs
    dhidden_ref, dmix_ref, *refs = refs
    up_ref, down_ref, *refs = refs
    part_a, half_a, give_a, take_a, part_b, half_b, give_b, take_b, kept, *refs = refs
    sems_a, sems_b, *refs = refs
    gathers = [
        BlockGather(count, up_shard, up_ref, refs[:5]),
        BlockGather(count, down_shard, down_ref, refs[5:]),
    ]
    mix = HeadSum(part_a, half_a, give_a, take_a, norm_ref, sems_a)
    back = HeadSum(part_b, half_b, give_b, take_b, dmix_ref, sems_b)
    size = g_ref.shape[0] // chunks
    quarter = size // 4
    width = x_ref.shape[1]
    shard, units = down_ref.shape[1:]
    channels = g_ref.shape[1]
    greet_pairs(count, True)
    for gather in gathers:
        gather.start()
    relays = [(gather, piece) for gather in gathers for piece in range(gather.pieces)]
    fourth = -(-len(relays) // chunks)

    def project(chunk, carry):
        here = at_rows(chunk, size)
        weights = out_ref[:, :, pl.ds(channels, channels)].reshape(width, channels)
        part_a[here, :] = transposed_dot(g_ref[here, :], weights).astype(BF)
        mix.near_copy(chunk).start()
        return carry

    lax.fori_loop(0, chunks, project, 0)

    def fold(chunk, carry):
        mix.fold(chunk, kept)
        return carry

    lax.fori_loop(0, chunks, fold, 0)

    def normalise(chunk, carry):
        mix.far_copy(chunk).wait_recv()
        here = at_rows(chunk, quarter)
        own = x_ref[mix.own_rows(chunk), :].astype(F32)
        hidden = own + kept[chunk] + take_a[chunk].astype(F32)
        hidden_ref[here, :] = hidden
        scale = lax.rsqrt(jnp.mean(hidden * hidden, axis=1, keepdims=True) + EPS)
        norm_ref[mix.own_rows(chunk), :] = (hidden * scale * gain_ref[...]).astype(BF)
        mix.far_back(chunk).start()
        for k in range(chunks):
            if relays[k * fourth : (k + 1) * fourth]:

                @pl.when(chunk == k)
                def _():
                    for gather, piece in relays[k * fourth : (k + 1) * fourth]:
                        gather.relay(piece)

        return carry

    lax.fori_loop(0, chunks, normalise, 0)
    mix.far_back(0).wait_recv()
    mix.near_back(0).start()
    for gather in gathers:
        gather.finish()
    per_block = max(1, count // 4)
    wide = per_block * shard
    lanes_block = 256 if units % 256 == 0 else units

    def feed(chunk, carry):
        here = at_rows(chunk, size)

        @pl.when(chunk + 1 < chunks)
        def _():
            mix.far_back(chunk + 1).wait_recv()
            mix.near_back(chunk + 1).start()

        mix.near_back(chunk).wait_recv()
        rows = norm_ref[here, :]
        grads = low_ref[here, :]
        for k in range(units // lanes_block):
            lanes = pl.ds(k * lanes_block, lanes_block)
            block = lambda ref: ref[:, :, lanes].reshape(width, lanes_block)
            gate = jnp.dot(rows, block(gate_ref), preferred_element_type=F32)
            up = jnp.dot(rows, block(up_ref), preferred_element_type=F32)
            d_act = jnp.dot(grads, block(down_ref), preferred_element_type=F32)
            logistic = 1.0 / (1.0 + jnp.exp(-gate))
            silu = gate * logistic
            act_ref[here, lanes] = (silu * up).astype(BF)
            slope = logistic * (1.0 + gate * (1.0 - logistic))
            dgate_ref[here, lanes] = (d_act * up * slope).astype(BF)
            dup_ref[here, lanes] = (d_act * silu).astype(BF)
        for k in range(count // per_block):
            lanes = pl.ds(k * wide, wide)
            block = lambda ref: ref[pl.ds(k * per_block, per_block)].reshape(wide, units)
            total = transposed_dot(dgate_ref[here, :], block(gate_ref))
            total = total + transposed_dot(dup_ref[here, :], block(up_ref))
            part_b[here, lanes] = total.astype(BF)
        back.near_copy(chunk).start()
        for k in range(count // per_block):
            lanes = pl.ds(k * wide, wide)
            block = down_ref[pl.ds(k * per_block, per_block)].reshape(wide, units)
            part_out_ref[here, lanes] = transposed_dot(act_ref[here, :], block).astype(BF)

        @pl.when(chunk >= 1)
        def _():
            back.fold(chunk - 1, kept)

        return carry

    lax.fori_loop(0, chunks, feed, 0)
    back.fold(chunks - 1, kept)
    dnorm_gain_ref[...] = jnp.zeros(dnorm_gain_ref.shape, F32)

    def turn(chunk, carry):
        back.far_copy(chunk).wait_recv()
        here = at_rows(chunk, quarter)
        hidden = hidden_ref[here, :]
        scale = lax.rsqrt(jnp.mean(hidden * hidden, axis=1, keepdims=True) + EPS)
        normed = hidden * scale
        d_norm = kept[chunk] + take_b[chunk].astype(F32)
        dnorm_gain_ref[...] += jnp.sum(d_norm * normed, axis=0, keepdims=True)
        scaled = d_norm * gain_ref[...]
        shift = jnp.mean(scaled * normed, axis=1, keepdims=True)
        own = low_ref[back.own_rows(chunk), :].astype(F32)
        d_hidden = own + scale * (scaled - normed * shift)
        dhidden_ref[here, :] = d_hidden
        dmix_ref[back.own_rows(chunk), :] = d_hidden.astype(BF)
        back.far_back(chunk).start()
        return carry

    lax.fori_loop(0, chunks, turn, 0)

    def spread_out(chunk, carry):
        back.far_back(chunk).wait_recv()
        back.near_back(chunk).start()
        return carry

    lax.fori_loop(0, chunks, spread_out, 0)

    def finish(chunk, carry):
        back.near_back(chunk).wait_recv()
        mix.finish(chunk)
        back.finish(chunk)
        return carry

    lax.fori_loop(0, chunks, finish, 0)


CHUNKS = 4


def sum_scratch(rows, width, part=True):
    chunk = rows // CHUNKS
    parts = [pltpu.VMEM((rows, width), BF)] if part else []
    return parts + [
        pltpu.VMEM((CHUNKS, chunk // 2, width), BF),
        pltpu.VMEM((CHUNKS, chunk // 4, width), BF),
        pltpu.VMEM((CHUNKS, chunk // 4, width), BF),
    ]


def kept_scratch(rows, width):
    return pltpu.VMEM((CHUNKS, rows // CHUNKS // 4, width), F32)


SUM_SEMS = pltpu.SemaphoreType.DMA((4, 2, CHUNKS))


def ffn_call(g_low, mix_blocks, x_low, gain, grad_low, gate_blocks, w_up, w_down_t):
    count = lax.axis_size("seq")
    rows, width = grad_low.shape
    units = w_down_t.shape[1]
    shape = jax.ShapeDtypeStruct
    in_vmem = pl.BlockSpec(memory_space=pltpu.VMEM)
    anywhere = pl.BlockSpec(memory_space=pl.ANY)
    outs = [
        shape((rows // 4, width), F32),
        shape((rows, width), BF),
        shape((rows, units), BF),
        shape((rows, units), BF),
        shape((rows, units), BF),
        shape((1, width), F32),
        shape((rows, width), BF),
        shape((rows // 4, width), F32),
        shape((rows, width), BF),
    ]
    return pl.pallas_call(
        functools.partial(ffn_kernel, count, CHUNKS),
        in_specs=[in_vmem] * 6 + [anywhere] * 2,
        out_specs=tuple([in_vmem] * len(outs)),
        out_shape=tuple(outs),
        scratch_shapes=[pltpu.VMEM((count,) + w_down_t.shape, BF)] * 2
        + sum_scratch(rows, width)
        + sum_scratch(rows, width)
        + [kept_scratch(rows, width)]
        + [SUM_SEMS] * 2
        + gather_sems(count // 2, units) * 2,
        compiler_params=pltpu.CompilerParams(
            collective_id=5, has_side_effects=True, vmem_limit_bytes=62 * 1024 * 1024
        ),
        cost_estimate=pl.CostEstimate(
            flops=14 * rows * width * units, bytes_accessed=40 * 1024 * 1024, transcendentals=0
        ),
    )(g_low, mix_blocks, x_low, gain, grad_low, gate_blocks, w_up, w_down_t)


def input_kernel(count, chunks, kinds, *refs):
    inner_ref, z_ref, in_x_ref, mix_ref, x_ref, norm_ref, gain_ref, dhidden_ref, *refs = refs
    pack_ref, refs = refs[0], refs[1:]
    olds, refs = [refs[k * kinds : (k + 1) * kinds] for k in range(3)], refs[3 * kinds :]
    out_ref, gain_out_ref, *refs = refs
    own_refs, refs = refs[: kinds + 1], refs[kinds + 1 :]
    pack_given, pack_came, *refs = refs
    part, half, give, take, kept, rows_ref, buffer, sems, *refs = refs
    sent, got, vector_sems, grad_ref, given, came, *refs = refs
    owned = OwnSum(count, olds, own_refs, refs[:3])
    refs = refs[3:]
    scatter = PairScatter(count, [grad_ref], [given], [came], refs[:8])
    pack = PairScatter(count, [pack_ref], [pack_given], [pack_came], refs[8:])
    back = HeadSum(part, half, give, take, rows_ref, sems)
    size = inner_ref.shape[0] // chunks
    quarter = size // 4
    shard, channels = in_x_ref.shape[1:]
    per_block = max(1, count // 4)
    wide = per_block * shard
    greet_pairs(count, True)
    pack.start()
    owned.load(0)
    around, _, shard_rows, _ = grad_ref.shape
    together = max(1, 384 // (2 * shard_rows))
    for block in range(around // together):
        lanes = pl.ds(block * together * 2 * shard_rows, together * 2 * shard_rows)
        grad = jnp.dot(norm_ref[:, lanes].T, inner_ref[...], preferred_element_type=F32)
        grad = grad.astype(BF).reshape(together, 2, shard_rows, channels)
        grad_ref[pl.ds(block * together, together)] = grad
    scatter.start()
    turns = [(scatter, turn) for turn in range(scatter.turns)]
    turns += [(pack, turn) for turn in range(pack.turns)]
    share = -(-len(turns) // (3 * chunks))
    early = 2 * chunks * share

    def move(chunk, stage):
        for k in range(chunks):
            todo = turns[(stage * chunks + k) * share :][:share]
            if todo:

                @pl.when(chunk == k)
                def _():
                    for moving, turn in todo:
                        moving.advance(turn)

    def own_step(chunk, first):
        for k in range(chunks):
            if first + k < kinds:

                @pl.when(chunk == k)
                def _():
                    owned.add(first + k)

    def project(chunk, carry):
        here = at_rows(chunk, size)
        for k in range(count // per_block):
            blocks = pl.ds(k * per_block, per_block)
            total = transposed_dot(inner_ref[here, :], in_x_ref[blocks].reshape(wide, channels))
            in_z = mix_ref[blocks, :, pl.ds(0, channels)].reshape(wide, channels)
            total = total + transposed_dot(z_ref[here, :], in_z)
            part[here, pl.ds(k * wide, wide)] = total.astype(BF)
        back.near_copy(chunk).start()
        return carry

    lax.fori_loop(0, chunks, project, 0)

    def fold(chunk, carry):
        back.fold(chunk, kept)
        own_step(chunk, 0)
        return carry

    lax.fori_loop(0, chunks, fold, 0)
    gain_out_ref[...] = jnp.zeros(gain_out_ref.shape, F32)
    around = scatter.around

    def vector(stage, slot, device):
        return pltpu.make_async_remote_copy(
            src_ref=sent.at[stage],
            dst_ref=got.at[slot],
            send_sem=vector_sems.at[0, slot],
            recv_sem=vector_sems.at[1, slot],
            device_id=device,
            device_id_type=pl.DeviceIdType.MESH,
        )

    stages = [
        [vector(0, 0, {"seq": scatter.high * 2 + 1 - scatter.low})],
        [
            vector(1, steps, {"seq": scatter.pair(steps) * 2 + scatter.low})
            for steps in range(1, around)
        ],
        [vector(2, around, back.near)],
        [vector(3, around + 1, back.far)],
    ]

    def pass_sum(stage):
        value = gain_out_ref[...]
        if stage > 0:
            for copy in stages[stage - 1]:
                copy.wait_recv()
            slots = [[0], list(range(1, around)), [around], [around + 1]][stage - 1]
            for slot in slots:
                value = value + got[slot]
            gain_out_ref[...] = value
        if stage < len(stages):
            sent[stage] = value
            for copy in stages[stage]:
                copy.start()

    def turn(chunk, carry):
        back.far_copy(chunk).wait_recv()
        here = at_rows(chunk, quarter)
        values = x_ref[back.own_rows(chunk), :].astype(F32)
        scale = lax.rsqrt(jnp.mean(values * values, axis=1, keepdims=True) + EPS)
        normed = values * scale
        d_norm = kept[chunk] + take[chunk].astype(F32)
        share_of_sum = jnp.sum(d_norm * normed, axis=0, keepdims=True)
        gain_out_ref[...] += jnp.broadcast_to(share_of_sum, gain_out_ref.shape)
        scaled = d_norm * gain_ref[...]
        shift = jnp.mean(scaled * normed, axis=1, keepdims=True)
        total = dhidden_ref[here, :] + scale * (scaled - normed * shift)
        rows_ref[back.own_rows(chunk), :] = total.astype(BF)
        back.far_back(chunk).start()
        move(chunk, 0)
        return carry

    lax.fori_loop(0, chunks, turn, 0)
    pass_sum(0)

    def spread_out(chunk, carry):
        back.far_back(chunk).wait_recv()
        back.near_back(chunk).start()
        move(chunk, 1)
        own_step(chunk, chunks)
        return carry

    lax.fori_loop(0, chunks, spread_out, 0)
    for stage in range(1, len(stages) + 1):
        pass_sum(stage)
    for old in range(2 * chunks, kinds):
        owned.add(old)
    for moving, turn in turns[early:]:
        moving.advance(turn)
    for copies in stages:
        for copy in copies:
            copy.wait_send()

    def finish(chunk, carry):
        back.near_back(chunk).wait_recv()
        put_sequences(out_ref, rows_ref, chunk, size, buffer)
        back.finish(chunk)
        return carry

    lax.fori_loop(0, chunks, finish, 0)
    scatter.finish()
    pack.finish()
    place = lax.axis_index("seq")
    total = grad_ref[place // 2, lax.rem(place, 2)].astype(F32) + given[0].astype(F32)
    for k in range(around - 1):
        total = total + came[k].astype(F32)
    own_refs[kinds][...] = total
    owned.finish()


class OwnSum:
    def __init__(self, count, olds, targets, scratch):
        self.place = lax.axis_index("seq")
        self.around = count // 2
        self.grads, self.given, self.came = olds
        self.targets = targets
        self.parts, self.total, self.sems = scratch

    def sources(self, kind):
        own = self.grads[kind].at[self.place // 2, lax.rem(self.place, 2)]
        came = [self.came[kind].at[k] for k in range(self.around - 1)]
        return [own, self.given[kind].at[0]] + came

    def loads(self, kind):
        lanes = pl.ds(0, self.targets[kind].shape[1])
        return [
            pltpu.make_async_copy(source, self.parts.at[k, :, lanes], self.sems.at[k])
            for k, source in enumerate(self.sources(kind))
        ]

    def store(self, kind):
        lanes = pl.ds(0, self.targets[kind].shape[1])
        return pltpu.make_async_copy(
            self.total.at[:, lanes], self.targets[kind], self.sems.at[self.around + 1]
        )

    def load(self, kind):
        for load in self.loads(kind):
            load.start()

    def add(self, kind):
        for load in self.loads(kind):
            load.wait()
        if kind:
            self.store(kind - 1).wait()
        lanes = pl.ds(0, self.targets[kind].shape[1])

        def one(row, carry):
            here = at_rows(row, 16)
            total = self.parts[0, here, lanes].astype(F32)
            for k in range(1, self.around + 1):
                total = total + self.parts[k, here, lanes].astype(F32)
            self.total[here, lanes] = total
            return carry

        lax.fori_loop(0, self.total.shape[0] // 16, one, 0)
        self.store(kind).start()
        if kind + 1 < len(self.grads):
            self.load(kind + 1)

    def finish(self):
        self.store(len(self.grads) - 1).wait()


def moved_shapes(grads):
    shape = jax.ShapeDtypeStruct
    around = grads[0].shape[0]
    given = [shape((around,) + grad.shape[2:], grad.dtype) for grad in grads]
    return given + [shape((around - 1,) + grad.shape[2:], grad.dtype) for grad in grads]


def input_call(d_inner, d_z, in_x_blocks, mix_blocks, x_low, x_norm, gain, d_hidden, pack, olds, dims):
    count = lax.axis_size("seq")
    around = count // 2
    rows, channels = d_inner.shape
    width = x_low.shape[1]
    shape = jax.ShapeDtypeStruct
    in_vmem = pl.BlockSpec(memory_space=pltpu.VMEM)
    anywhere = pl.BlockSpec(memory_space=pl.ANY)
    grads, given, came = olds
    shard = grads[0].shape[2]
    widest = max(grad.shape[3] for grad in grads)
    moved = moved_shapes([pack])
    late = shape((around, 2, shard, channels), BF)
    return pl.pallas_call(
        functools.partial(input_kernel, count, CHUNKS, len(grads)),
        in_specs=[in_vmem] * 8 + [anywhere] * (3 * len(grads) + 1),
        out_specs=tuple(
            [in_vmem] * 2 + [anywhere] * len(grads) + [in_vmem] + [anywhere] * len(moved)
        ),
        out_shape=tuple(
            [shape(dims, F32), shape((8, width), F32)]
            + [shape((shard, grad.shape[3]), F32) for grad in grads]
            + [shape((shard, channels), F32)]
            + moved
        ),
        scratch_shapes=sum_scratch(rows, width)
        + [kept_scratch(rows, width), pltpu.VMEM((rows, width), BF)]
        + [pltpu.VMEM((width // LANES, rows // CHUNKS, LANES), F32), SUM_SEMS]
        + [pltpu.VMEM((4, 8, width), F32), pltpu.VMEM((around + 2, 8, width), F32)]
        + [pltpu.SemaphoreType.DMA((2, around + 2))]
        + [pltpu.VMEM(late.shape, BF), pltpu.VMEM((around, shard, channels), BF)]
        + [pltpu.VMEM((around - 1, shard, channels), BF)]
        + [pltpu.VMEM((around + 1, shard, widest), BF), pltpu.VMEM((shard, widest), F32)]
        + [pltpu.SemaphoreType.DMA((around + 2,))]
        + scatter_scratch(count, [late])
        + scatter_scratch(count, [pack]),
        compiler_params=pltpu.CompilerParams(
            collective_id=6, has_side_effects=True, vmem_limit_bytes=62 * 1024 * 1024
        ),
        cost_estimate=pl.CostEstimate(
            flops=4 * rows * width * d_inner.shape[1],
            bytes_accessed=40 * 1024 * 1024,
            transcendentals=0,
        ),
    )(
        d_inner,
        d_z,
        in_x_blocks,
        mix_blocks,
        x_low,
        x_norm,
        gain,
        d_hidden,
        pack,
        *grads,
        *given,
        *came,
    )


def pairs_of(axis):
    return lax.axis_size(axis) // 2


def hop(value, steps):
    count = lax.axis_size("seq")
    return lax.ppermute(value, "seq", [(s, (s + 2 * steps) % count) for s in range(count)])


def swap(value, axis, bit):
    return lax.ppermute(value, axis, [(s, s ^ bit) for s in range(lax.axis_size(axis))])


def owner_blocks(value):
    return value.reshape((pairs_of("seq"), 2, -1) + value.shape[1:])


def scatter_half(blocks, theirs):
    place = lax.axis_index("seq")
    around = pairs_of("seq")
    low, high = place % 2, place // 2
    mine = lax.dynamic_index_in_dim(blocks, low, 1, False)
    half = mine.astype(F32) + theirs.astype(F32)
    total = lax.dynamic_index_in_dim(half, high, 0, False)
    half = half.astype(blocks.dtype)
    for steps in range(1, around):
        part = lax.dynamic_index_in_dim(half, (high + steps) % around, 0, False)
        total = total + hop(part, steps).astype(F32)
    return total


def scatter_rows(value, kind=BF):
    low = lax.axis_index("seq") % 2
    blocks = owner_blocks(value.astype(kind))
    theirs = lax.dynamic_index_in_dim(blocks, 1 - low, 1, False)
    return scatter_half(blocks, swap(theirs, "seq", 1))


def scatter_own(blocks, given, came):
    place = lax.axis_index("seq")
    own = blocks.reshape((-1,) + blocks.shape[2:])
    total = lax.dynamic_index_in_dim(own, place, 0, False).astype(F32) + given[0].astype(F32)
    for k in range(came.shape[0]):
        total = total + came[k].astype(F32)
    return total


def head_bits():
    return (lax.axis_size("head") - 1).bit_length()


def head_scatter(value):
    place = lax.axis_index("head")
    width = value.shape[1]
    value = value.reshape(CHUNKS, -1, width)
    for k in range(head_bits()):
        bit = place // 2**k % 2
        halves = value.astype(BF).reshape(CHUNKS, 2, -1, width)
        keep = lax.dynamic_index_in_dim(halves, bit, 1, False)
        send = lax.dynamic_index_in_dim(halves, 1 - bit, 1, False)
        value = keep.astype(F32) + swap(send, "head", 2**k).astype(F32)
    return value.reshape(-1, width)


def head_part(value):
    place = lax.axis_index("head")
    width = value.shape[1]
    value = value.reshape(CHUNKS, -1, width)
    for k in range(head_bits()):
        halves = value.reshape(CHUNKS, 2, -1, width)
        value = lax.dynamic_index_in_dim(halves, place // 2**k % 2, 1, False)
    return value.reshape(-1, width)


def head_gather(value):
    place = lax.axis_index("head")
    width = value.shape[1]
    value = value.reshape(CHUNKS, -1, width)
    for k in reversed(range(head_bits())):
        got = swap(value, "head", 2**k)
        first = place // 2**k % 2 == 0
        both = [jnp.where(first, value, got), jnp.where(first, got, value)]
        value = jnp.concatenate(both, axis=1)
    return value.reshape(-1, width)


def head_total(value, kind):
    for k in range(head_bits()):
        value = value.astype(kind)
        value = value.astype(F32) + swap(value, "head", 2**k).astype(F32)
    return value


def first_kernel(count, kinds, turned, *refs):
    sources, plain, refs = refs[:kinds], refs[kinds : kinds + turned], refs[kinds + turned :]
    targets, outs, refs = refs[:kinds], refs[kinds : kinds + turned], refs[kinds + turned :]
    buffer, *refs = refs
    gathers = [
        BlockGather(count, sources[k], targets[k], refs[5 * k : 5 * k + 5]) for k in range(kinds)
    ]
    greet_pairs(count)
    for gather in gathers:
        gather.start()
    for source, target in zip(plain, outs):
        seqs, tokens, _ = source.shape

        def widen(k, carry):
            for m in range(buffer.shape[0]):
                lanes = pl.ds(m * LANES, LANES)
                buffer[m, at_rows(k, tokens), :] = source[k, :, lanes].astype(F32)
            return carry

        lax.fori_loop(0, seqs, widen, 0)

        def turn(pair, carry):
            for m in range(buffer.shape[0]):
                both = [buffer[m, pl.ds(2 * pair + k, seqs, stride=tokens), :] for k in range(2)]
                both = jnp.concatenate(both, axis=0).astype(BF)
                target[at_rows(pair, 2 * seqs), pl.ds(m * LANES, LANES)] = both
            return carry

        lax.fori_loop(0, tokens // 2, turn, 0)
    for gather in gathers:
        for piece in range(gather.pieces):
            gather.relay(piece)
    for gather in gathers:
        gather.finish()


def first_gather(values, plain):
    count = lax.axis_size("seq")
    around = count // 2
    seqs, tokens, width = plain[0].shape
    shape = jax.ShapeDtypeStruct
    in_vmem = pl.BlockSpec(memory_space=pltpu.VMEM)
    anywhere = pl.BlockSpec(memory_space=pl.ANY)
    return pl.pallas_call(
        functools.partial(first_kernel, count, len(values), len(plain)),
        out_shape=tuple(
            [shape((count,) + v.shape, v.dtype) for v in values]
            + [shape((seqs * tokens, width), BF) for _ in plain]
        ),
        in_specs=[anywhere] * len(values) + [in_vmem] * len(plain),
        out_specs=tuple([anywhere] * len(values) + [in_vmem] * len(plain)),
        scratch_shapes=[pltpu.VMEM((width // LANES, seqs * tokens, LANES), F32)]
        + [sem for v in values for sem in gather_sems(around, v.shape[-1])],
        compiler_params=pltpu.CompilerParams(
            collective_id=0, has_side_effects=True, vmem_limit_bytes=40 * 1024 * 1024
        ),
    )(*values, *plain)


def shards(
    x_in,
    seg_ids,
    norm1_gain,
    w_in_x,
    w_in_z,
    conv_w,
    conv_b,
    w_xproj,
    ssm_gain,
    w_dt,
    dt_bias,
    a_log,
    d_skip,
    w_out,
    norm2_gain,
    w_gate,
    w_up,
    w_down,
    d_out,
):
    count = lax.axis_size("seq")
    place = lax.axis_index("seq")
    seqs, tokens, width = x_in.shape
    rows = seqs * tokens
    taps = conv_w.shape[0]
    rank = w_dt.shape[0]
    states = a_log.shape[1]
    channels = w_in_x.shape[1]
    halo = (taps - 1) * seqs

    per = channels // count
    fields = [w_xproj, w_dt.T, a_log, conv_w.T, conv_b[:, None], dt_bias[:, None], d_skip[:, None]]
    starts = [0]
    for field in fields:
        starts.append(starts[-1] + field.shape[1])
    pack_width = -(-starts[-1] // LANES) * LANES
    gains = [norm1_gain, norm2_gain, ssm_gain]
    gain_starts = [0]
    for gain in gains:
        gain_starts.append(gain_starts[-1] + gain.shape[0])
    pack_rows = -(-(per + -(-gain_starts[-1] // pack_width)) // 16) * 16

    def pack(channel_fields, gain_fields):
        table = jnp.concatenate([f.astype(F32) for f in channel_fields], axis=1)
        table = jnp.pad(table, ((0, 0), (0, pack_width - table.shape[1])))
        table = table.reshape(-1, per, pack_width)
        rest = jnp.concatenate([g.astype(F32).reshape(table.shape[0], -1) for g in gain_fields], 1)
        rest = jnp.pad(rest, ((0, 0), (0, (pack_rows - per) * pack_width - rest.shape[1])))
        return jnp.concatenate([table, rest.reshape(-1, pack_rows - per, pack_width)], axis=1)

    def unpack(block):
        table = block[:, :per].reshape(-1, pack_width)
        rest = block[:, per:].reshape(block.shape[0], -1)
        return (
            [table[:, starts[k] : starts[k + 1]] for k in range(len(fields))],
            [rest[:, gain_starts[k] : gain_starts[k + 1]].reshape(-1) for k in range(len(gains))],
        )

    in_x_blocks, pack_blocks, x_low, grad_low = first_gather(
        [w_in_x.astype(BF), pack(fields, gains)[0].astype(BF)], [x_in, d_out]
    )
    fulls, full_gains = unpack(pack_blocks)
    full_xproj, w_dt_cols, full_a_log, conv_cols, conv_b_col, bias_col, skip_col = fulls
    full_w_dt = w_dt_cols.T
    full_conv_w = conv_cols.T
    full_conv_b, full_dt_bias, full_d_skip = conv_b_col[:, 0], bias_col[:, 0], skip_col[:, 0]
    full_norm1, full_norm2, full_ssm_gain = full_gains

    w_mix = jnp.concatenate([w_in_z.astype(BF), w_out.astype(BF).T], axis=1)
    w_mix, in_x_blocks = lax.optimization_barrier((w_mix, in_x_blocks))
    full_in_x = in_x_blocks.reshape(width, channels)
    full_mix = lax.all_gather(w_mix, "seq", axis=0, tiled=True)

    norm1_vec = full_norm1.astype(F32)
    x_rows = x_low.astype(F32)
    ids = seg_ids.T.reshape(rows)
    normed1, scale_one = norm_rows(x_rows, norm1_vec)
    x_norm = normed1.astype(BF)
    x_inner = jnp.dot(x_norm, full_in_x, preferred_element_type=F32).astype(BF)
    prev_tail, prev_ids = shifted((x_inner[rows - halo :], ids[rows - halo :]), "seq", 1)
    extended = jnp.concatenate([prev_tail, x_inner], axis=0).astype(F32)
    ext_ids = jnp.concatenate([prev_ids, ids])
    conv_weight = full_conv_w.astype(F32)
    x_conv = full_conv_b.astype(F32)[None, :]
    same_docs = []
    for offset in range(taps):
        first = (taps - 1 - offset) * seqs
        same = (ext_ids[first : first + rows] == ids).astype(F32)[:, None]
        same_docs.append(same)
        x_conv = x_conv + conv_weight[offset] * extended[first : first + rows] * same
    u_low = jax.nn.silu(x_conv).astype(BF)
    projected = head_total(jnp.dot(u_low, full_xproj, preferred_element_type=F32), BF)
    ssm_vec = full_ssm_gain.astype(F32)
    b_end = rank + states
    dt_normed, dt_scale = norm_rows(projected[:, :rank], ssm_vec[:rank])
    b_normed, b_scale = norm_rows(projected[:, rank:b_end], ssm_vec[rank:b_end])
    c_normed, c_scale = norm_rows(projected[:, b_end:], ssm_vec[b_end:])
    dt_low = dt_normed.astype(BF)
    dt_pre = jnp.dot(dt_low, full_w_dt, preferred_element_type=F32) + full_dt_bias.astype(F32)
    step = jax.nn.softplus(dt_pre)
    rates = -jnp.exp(full_a_log.astype(F32))
    rate_rows = jnp.repeat((rates * LOG2E).T, seqs, axis=0)
    bc = jnp.concatenate([b_normed, c_normed], axis=1)
    part_one = bc.astype(BF)
    part_two = (bc - part_one.astype(F32)).astype(BF)
    part_three = (bc - part_one.astype(F32) - part_two.astype(F32)).astype(BF)
    stops = ((1.0 - same_docs[1]) * STOP).astype(BF)
    masks = [same.astype(BF) for same in same_docs[1:]]
    spare = jnp.zeros((rows, LANES - 6 * states - taps), BF)
    parts = jnp.concatenate([part_one, part_two, part_three, stops] + masks + [spare], axis=1)
    shape = jax.ShapeDtypeStruct
    state_rows = states * seqs
    start, step_sum = state_call(
        entry_kernel,
        1,
        seqs,
        states,
        2 * states + 2,
        [parts, step, u_low, rate_rows],
        [shape((state_rows, channels), F32), shape((seqs, channels), F32)],
        exchange_scratch(count, seqs, states, channels),
        6,
        (0, 0),
    )
    start, full_mix = lax.optimization_barrier((start, full_mix))
    mix_blocks = full_mix.reshape(count, -1, full_mix.shape[1])
    w_gate_low = w_gate.astype(BF)
    y_state, gate_blocks = state_call(
        forward_kernel,
        2,
        seqs,
        states,
        2 * states + 2,
        [parts, step, u_low, rate_rows, start, w_gate_low],
        [shape((rows, channels), F32), shape((count,) + w_gate.shape, BF)],
        gather_sems(count // 2, w_gate.shape[1]),
        8,
        (1, 1),
    )
    full_in_z = full_mix[:, :channels]
    z_gate = jnp.dot(x_norm, full_in_z, preferred_element_type=F32)
    skip_vec = full_d_skip.astype(F32)
    u_rows = u_low.astype(F32)
    y_full = y_state + skip_vec * u_rows
    silu_z = jax.nn.silu(z_gate)
    g_low = (y_full * silu_z).astype(BF)
    hidden, x_norm2, act_low, d_gate, d_up, norm2_sums, ffn_part, d_hidden, d_mix = ffn_call(
        g_low,
        mix_blocks,
        x_low,
        full_norm2.astype(F32)[None, :],
        grad_low,
        gate_blocks,
        w_up.astype(BF),
        w_down.astype(BF).T,
    )
    grad_norm2 = norm2_sums[0]
    grad_out_w = jnp.einsum("rd,re->de", d_mix, g_low, preferred_element_type=F32)
    full_out_t = full_mix[:, channels:]
    d_g = jnp.dot(d_mix, full_out_t, preferred_element_type=F32)
    d_y = d_g * silu_z
    d_z = (d_g * y_full * silu_slope(z_gate)).astype(BF)
    grad_skip = jnp.sum(d_y * u_rows, axis=0)
    grad_block = shape((count // 2, 2, width // count, w_gate.shape[1]), BF)
    last, grad_down, grad_gate, grad_up, block_out = state_call(
        adjoint_kernel,
        3,
        seqs,
        states,
        states + 2,
        [parts, step, d_y, rate_rows, step_sum, x_norm2, grad_low, act_low, d_gate, d_up]
        + [ffn_part, hidden],
        [shape((state_rows, channels), F32)] + [grad_block] * 3 + [shape(x_in.shape, BF)],
        exchange_scratch(count, seqs, states, channels)
        + sum_scratch(rows, width, False)
        + [kept_scratch(rows, width), pltpu.VMEM((rows, width), BF)]
        + [pltpu.VMEM((width // LANES, rows // CHUNKS, LANES), F32), SUM_SEMS],
        6,
        (0, 0),
    )
    grad_in_z = jnp.einsum("rd,re->de", x_norm, d_z, preferred_element_type=F32)
    big_grads = [grad_down, grad_gate, grad_up]
    big_grads += [owner_blocks(grad.astype(BF)) for grad in (grad_out_w, grad_in_z)]
    padded = lambda value: jnp.pad(value, ((0, 0), (0, LANES - value.shape[1])))
    taps_table = jnp.concatenate([conv_weight, skip_vec[None, :]], axis=0)
    taps_table = jnp.pad(taps_table, ((0, 2 * taps - taps_table.shape[0]), (0, 0)))
    big_ins = [x_conv, extended.reshape(-1, seqs, channels), projected] + big_grads
    block_rows_moved = moved_shapes(big_grads)
    bf_rows = pltpu.VMEM((4 * seqs, channels), BF)
    d_inner_low, ssm_sums, grad_xproj, grad_step_t, d_log, column_sums, *first_moved = state_call(
        backward_kernel,
        4,
        seqs,
        states,
        2 * states + 2,
        [parts, step, u_low, d_y, rate_rows, start, last, padded(dt_low)]
        + [padded(w_dt_cols), full_xproj, ssm_vec[None, :], taps_table]
        + big_ins,
        [
            shape((rows, channels), BF),
            shape((8, LANES), F32),
            shape((channels, LANES), F32),
            shape((channels, LANES), F32),
            shape((states, channels), F32),
            shape(((taps + 2) * seqs, channels), F32),
        ]
        + block_rows_moved,
        [
            pltpu.VMEM(((tokens + 1) * states, seqs, LANES), F32),
            pltpu.VMEM((rows, 2 * states * LANES), F32),
            pltpu.VMEM((rows, channels), F32),
            pltpu.VMEM((rows, channels), BF),
            pltpu.VMEM((2, rows, LANES), BF),
            pltpu.VMEM((2, rows, LANES), BF),
            pltpu.VMEM((4 * seqs, channels), F32),
            bf_rows,
            bf_rows,
            pltpu.SemaphoreType.DMA((2, 2)),
            pltpu.SemaphoreType.DMA((2,)),
            pltpu.SemaphoreType.DMA((channels // LANES + 2,)),
        ]
        + scatter_scratch(count, big_grads),
        30,
        (len(big_ins), len(block_rows_moved)),
    )
    grad_alog = d_log.T * rates
    columns = jnp.sum(column_sums.reshape(taps + 2, seqs, channels), axis=1)
    grad_ssm = ssm_sums[0]
    grad_ssm = grad_ssm * (lax.axis_index("head") == 0).astype(F32)
    small = pack(
        [
            grad_xproj,
            grad_step_t[:, :rank],
            grad_alog,
            columns[:taps].T,
            columns[taps][:, None],
            columns[taps + 1][:, None],
            grad_skip[:, None],
        ],
        [jnp.zeros_like(grad_norm2), grad_norm2, grad_ssm],
    )
    small = owner_blocks(small.reshape(-1, pack_width))
    kinds = len(big_grads)
    grad_input, norm1_sums, *owns, pack_given, pack_came = input_call(
        d_inner_low,
        d_z,
        in_x_blocks,
        mix_blocks,
        x_low,
        x_norm,
        norm1_vec[None, :],
        d_hidden,
        small,
        (big_grads, first_moved[:kinds], first_moved[kinds:]),
        x_in.shape,
    )
    own_down, own_gate, own_up, own_out, own_in_z, own_in_x = owns
    small = scatter_own(small, pack_given, pack_came)
    own_norm1 = lax.dynamic_slice_in_dim(norm1_sums[0], place * (width // count), width // count)
    small = jnp.concatenate([small[:per], head_total(small[per:], F32)])[None]
    small_fields, small_gains = unpack(small)
    return (
        block_out,
        grad_input,
        own_norm1,
        own_in_x,
        own_in_z,
        small_fields[3].T,
        small_fields[4][:, 0],
        small_fields[0],
        small_gains[2],
        small_fields[1].T,
        small_fields[5][:, 0],
        small_fields[2],
        small_fields[6][:, 0],
        own_out.T,
        small_gains[1],
        own_gate,
        own_up,
        own_down.T,
    )


def solution(mesh):
    placed = (
        P(None, "seq", None),
        P(None, "seq"),
        P("seq"),
        P("seq", "head"),
        P("seq", "head"),
        P(None, ("head", "seq")),
        P(("head", "seq")),
        P(("head", "seq"), None),
        P("seq"),
        P(None, ("head", "seq")),
        P(("head", "seq")),
        P(("head", "seq"), None),
        P(("head", "seq")),
        P("head", "seq"),
        P("seq"),
        P("seq", "head"),
        P("seq", "head"),
        P("head", "seq"),
        P(None, "seq", None),
    )
    return jax.shard_map(
        shards,
        mesh=mesh,
        in_specs=placed,
        out_specs=(
            P(None, "seq", None),
            P(None, "seq", None),
            P("seq"),
            P("seq", "head"),
            P("seq", "head"),
            P(None, ("head", "seq")),
            P(("head", "seq")),
            P(("head", "seq"), None),
            P("seq"),
            P(None, ("head", "seq")),
            P(("head", "seq")),
            P(("head", "seq"), None),
            P(("head", "seq")),
            P("head", "seq"),
            P("seq"),
            P("seq", "head"),
            P("seq", "head"),
            P("head", "seq"),
        ),
        check_vma=False,
    )
```

```python
import functools

import jax
import jax.numpy as jnp
from jax import lax
from jax.experimental import pallas as pl
from jax.experimental.pallas import tpu as pltpu
from jax.sharding import PartitionSpec as P

EPS = 1e-06
LOG2E = 1.4426950408889634
LN2 = 0.6931471805599453
STOP = 1e30
LANES = 128
BF = jnp.bfloat16
F32 = jnp.float32


def shifted(value, axis, steps):
    count = lax.axis_size(axis)
    initial, last = (max(0, -steps), min(count, count - steps))
    return lax.ppermute(value, axis, [(source, source + steps) for source in range(initial, last)])


def norm_rows(values, gain_vec):
    inv_rms = lax.rsqrt(jnp.mean(values * values, axis=-1, keepdims=True) + EPS)
    return (values * inv_rms * gain_vec, inv_rms)


def norm_back(values, inv_rms, gain_vec, grad_rows):
    normed = values * inv_rms
    gain_grad = jnp.sum(grad_rows * normed, axis=0)
    scaled = grad_rows * gain_vec
    value_grad = inv_rms * (scaled - normed * jnp.mean(scaled * normed, axis=-1, keepdims=True))
    return (value_grad, gain_grad)


def silu_slope(values):
    logistic = jax.nn.sigmoid(values)
    return logistic * (1.0 + values * (1.0 - logistic))


GROUP = 4


def at_rows(index, size):
    return pl.ds(pl.multiple_of(index * size, size), size)


def spread(parts_ref, states, target, first=0):
    rows = parts_ref.shape[0]
    wide = 2 * LANES
    chunk = 256 if rows % 256 == 0 else rows
    source = lax.broadcasted_iota(jnp.int32, (LANES, wide), 0)
    half = lax.broadcasted_iota(jnp.int32, (LANES, wide), 1) // LANES
    columns = 2 * states

    def one(pair, carry):
        column = pair * 2 + half
        third = source % columns == column
        hot = jnp.where((source < 3 * columns) & third, 1.0, 0.0)
        stop = (column == columns) & (source == 3 * columns)
        hot = jnp.where(stop, 1.0, hot).astype(BF)
        for k in range(rows // chunk):
            target[pl.ds(k * chunk, chunk), at_rows(pair - first, wide)] = jnp.dot(
                parts_ref[pl.ds(k * chunk, chunk), :], hot, preferred_element_type=F32
            )
        return carry

    lax.fori_loop(first, states + 1, one, 0)


def group_tokens(ref, group, lanes, seqs):
    both = ref[at_rows(group, GROUP * seqs), lanes].astype(F32)
    return [both[k * seqs : (k + 1) * seqs] for k in range(GROUP)]


class Exchange:
    def __init__(self, count, forward, arrays, sems):
        place = lax.axis_index("seq")
        self.around = count // 2
        self.low, self.high = lax.rem(place, 2), place // 2
        self.place = place
        self.forward = forward
        self.arrays = arrays
        self.sems = sems
        self.mate = self.high * 2 + 1 - self.low

    def copies(self, steps, tile, source, device, kind):
        send, recv = self.sems[2 * kind], self.sems[2 * kind + 1]
        lanes = at_rows(tile, LANES)
        return [
            pltpu.make_async_remote_copy(
                src_ref=array.at[source, :, lanes],
                dst_ref=array.at[source, :, lanes],
                send_sem=send.at[k, steps, tile],
                recv_sem=recv.at[k, steps, tile],
                device_id={"seq": device},
                device_id_type=pl.DeviceIdType.MESH,
            )
            for k, array in enumerate(self.arrays)
        ]

    def away(self, steps):
        return self.high + steps if self.forward else self.high - steps

    def inside(self, pair):
        return pair < self.around if self.forward else pair >= 0

    def behind(self, steps):
        return self.high - steps if self.forward else self.high + steps

    def has_behind(self, steps):
        pair = self.behind(steps)
        return pair >= 0 if self.forward else pair < self.around

    def gives(self):
        return self.low == (0 if self.forward else 1)

    def hop(self, steps, tile):
        pair = jnp.clip(self.away(steps), 0, self.around - 1)
        return self.copies(steps, tile, self.place, pair * 2 + self.low, 0)

    def relay(self, steps, tile):
        pair = jnp.clip(self.behind(steps), 0, self.around - 1)
        return self.copies(steps, tile, pair * 2 + self.low, self.mate, 1)

    def start(self, tile):
        for steps in range(1, self.around):

            @pl.when(self.inside(self.away(steps)))
            def _():
                for copy in self.hop(steps, tile):
                    copy.start()

        @pl.when(self.gives())
        def _():
            for copy in self.relay(0, tile):
                copy.start()

    def pass_on(self, tile):
        for steps in range(1, self.around):

            @pl.when(self.has_behind(steps))
            def _():
                for copy in self.hop(steps, tile):
                    copy.wait_recv()
                for copy in self.relay(steps, tile):
                    copy.start()

    def arrive(self, tile):
        @pl.when(jnp.logical_not(self.gives()))
        def _():
            for copy in self.relay(0, tile):
                copy.wait_recv()

        for steps in range(1, self.around):

            @pl.when(self.has_behind(steps))
            def _():
                for copy in self.relay(steps, tile):
                    copy.wait_recv()

    def finish(self, tile):
        @pl.when(self.gives())
        def _():
            for copy in self.relay(0, tile):
                copy.wait_send()

        for steps in range(1, self.around):

            @pl.when(self.inside(self.away(steps)))
            def _():
                for copy in self.hop(steps, tile):
                    copy.wait_send()

            @pl.when(self.has_behind(steps))
            def _():
                for copy in self.relay(steps, tile):
                    copy.wait_send()


def chained(state, block_ref, sums_ref, rate_ref, source, lanes, seqs):
    total = sums_ref[source, :, lanes]
    block = block_ref[source, :, lanes].astype(F32)
    after = []
    for n in range(len(state)):
        decay = jnp.exp2(total * rate_ref[pl.ds(n * seqs, seqs), lanes])
        after.append(decay * state[n] + block[n * seqs : (n + 1) * seqs])
    return tuple(after)


def state_blocks(ref, lanes, seqs, states):
    return tuple(ref[pl.ds(n * seqs, seqs), lanes] for n in range(states))


def put_blocks(ref, lead, lanes, blocks):
    stacked = jnp.concatenate(blocks, axis=0)
    if lead is None:
        ref[:, lanes] = stacked.astype(ref.dtype)
    else:
        ref[lead, :, lanes] = stacked.astype(ref.dtype)


def entry_kernel(
    count, seqs, states, parts_ref, step_ref, u_ref, rate_ref, start_ref, sum_ref, *scratch
):
    spread_ref, ends, sums, *sems = scratch
    rows, channels = step_ref.shape
    tokens, tiles = rows // seqs, channels // LANES
    stop_lanes = pl.ds(2 * states * LANES, LANES)
    exchange = Exchange(count, True, (ends, sums), sems)
    place = exchange.place
    zero = jnp.zeros((seqs, LANES), F32)
    greet_pairs(count)
    spread(parts_ref, states, spread_ref)

    def local(tile, carry):
        lanes = at_rows(tile, LANES)

        def one(group, carry):
            state, total = carry
            us = group_tokens(u_ref, group, lanes, seqs)
            for k in range(GROUP):
                here = at_rows(group * GROUP + k, seqs)
                step = step_ref[here, lanes]
                drive = step * us[k]
                stop = step + spread_ref[here, stop_lanes]
                total = total + stop
                fresh = []
                for n in range(states):
                    decay = jnp.exp2(stop * rate_ref[pl.ds(n * seqs, seqs), lanes])
                    b_one = spread_ref[here, pl.ds(n * LANES, LANES)]
                    fresh.append(decay * state[n] + drive * b_one)
                state = tuple(fresh)
            return state, total

        state, total = lax.fori_loop(0, tokens // GROUP, one, ((zero,) * states, zero))
        put_blocks(ends, place, lanes, state)
        sums[place, :, lanes] = total
        exchange.start(tile)
        return carry

    lax.fori_loop(0, tiles, local, 0)
    finish_exchange(exchange, tiles, lambda first, lanes: lax.fori_loop(
        0,
        place,
        lambda source, state: chained(state, ends, sums, rate_ref, source, lanes, seqs),
        first,
    ), start_ref, states, zero)
    sum_ref[...] = sums[place]


def finish_exchange(exchange, tiles, chain, target_ref, states, zero, relay=True):
    def pass_on(tile, carry):
        exchange.pass_on(tile)
        return carry

    if relay:
        lax.fori_loop(0, tiles, pass_on, 0)

    def take(tile, carry):
        lanes = at_rows(tile, LANES)
        exchange.arrive(tile)
        put_blocks(target_ref, None, lanes, chain((zero,) * states, lanes))
        return carry

    lax.fori_loop(0, tiles, take, 0)

    def finish(tile, carry):
        exchange.finish(tile)
        return carry

    lax.fori_loop(0, tiles, finish, 0)


def forward_kernel(
    count,
    seqs,
    states,
    parts_ref,
    step_ref,
    u_ref,
    rate_ref,
    start_ref,
    block_ref,
    y_ref,
    gathered_ref,
    *scratch,
):
    spread_ref, *sems = scratch
    gather = BlockGather(count, block_ref, gathered_ref, sems)
    rows, channels = step_ref.shape
    tokens, tiles = rows // seqs, channels // LANES
    stop_lanes = pl.ds(2 * states * LANES, LANES)
    zero = jnp.zeros((seqs, LANES), F32)
    greet_pairs(count)
    gather.start()
    spread(parts_ref, states, spread_ref)

    def whole(tile, carry):
        lanes = at_rows(tile, LANES)

        def one(group, state):
            us = group_tokens(u_ref, group, lanes, seqs)
            for k in range(GROUP):
                here = at_rows(group * GROUP + k, seqs)
                step = step_ref[here, lanes]
                drive = step * us[k]
                stop = step + spread_ref[here, stop_lanes]
                fresh = []
                out = zero
                for n in range(states):
                    decay = jnp.exp2(stop * rate_ref[pl.ds(n * seqs, seqs), lanes])
                    b_one = spread_ref[here, pl.ds(n * LANES, LANES)]
                    value = decay * state[n] + drive * b_one
                    out = out + value * spread_ref[here, pl.ds((states + n) * LANES, LANES)]
                    fresh.append(value)
                y_ref[here, lanes] = out
                state = tuple(fresh)
            return state

        lax.fori_loop(0, tokens // GROUP, one, state_blocks(start_ref, lanes, seqs, states))
        for piece in range(gather.pieces):
            if 3 * piece + 2 < tiles:

                @pl.when(tile == 3 * piece + 2)
                def _():
                    gather.relay(piece)

        return carry

    lax.fori_loop(0, tiles, whole, 0)
    for piece in range(gather.pieces):
        if 3 * piece + 2 >= tiles:
            gather.relay(piece)
    gather.finish()


def adjoint_kernel(
    count,
    seqs,
    states,
    parts_ref,
    step_ref,
    dy_ref,
    rate_ref,
    sum_ref,
    *refs,
):
    sources, refs = refs[:7], refs[7:]
    last_ref, gdown_ref, ggate_ref, gup_ref, out_ref, given_ref, came_ref, *scratch = refs
    spread_ref, ends, sums, *scratch = scratch
    sems, scratch = scratch[:4], scratch[4:]
    half, give, take, kept, block_ref, buffer, sum_sems, *scratch = scratch
    targets, fetch_sems, scratch = scratch[:7], scratch[7], scratch[8:]
    fetch = Fetch(sources, targets, fetch_sems)
    part_ref, low_ref, act_ref, norm_ref, dgate_ref, dup_ref, hidden_ref = targets
    fetch.start()
    scatter = PairScatter(count, [gdown_ref], [given_ref], [came_ref], scratch)
    total = HeadSum(part_ref, half, give, take, block_ref, sum_sems)
    chunks = kept.shape[0]
    quarter = kept.shape[1]
    rows, channels = step_ref.shape
    tokens, tiles = rows // seqs, channels // LANES
    groups = tokens // GROUP
    stop_lanes = pl.ds(states * LANES, LANES)
    exchange = Exchange(count, False, (ends, sums), sems)
    place = exchange.place
    zero = jnp.zeros((seqs, LANES), F32)
    greet_pairs(count, True)
    spread(parts_ref, states, spread_ref, states // 2)

    def own(tile, carry):
        lanes = at_rows(tile, LANES)

        def one(back, grads):
            group = groups - 1 - back
            for k in reversed(range(GROUP)):
                here = at_rows(group * GROUP + k, seqs)
                stop = step_ref[here, lanes] + spread_ref[here, stop_lanes]
                dy = dy_ref[here, lanes]
                fresh = []
                for n in range(states):
                    decay = jnp.exp2(stop * rate_ref[pl.ds(n * seqs, seqs), lanes])
                    c_one = spread_ref[here, pl.ds(n * LANES, LANES)]
                    fresh.append(decay * (grads[n] + dy * c_one))
                grads = tuple(fresh)
            return grads

        put_blocks(ends, place, lanes, lax.fori_loop(0, groups, one, (zero,) * states))
        sums[place, :, lanes] = sum_ref[:, lanes]
        exchange.start(tile)
        return carry

    lax.fori_loop(0, tiles, own, 0)
    fetch.wait(0, 1, 2, 3, 4, 5, 6)
    for chunk in range(chunks):
        total.near_copy(chunk).start()
    around, _, shard, units = gdown_ref.shape
    together = max(1, 384 // (2 * shard))
    wide = together * 2 * shard

    def place_of(block):
        return pl.ds(block * wide, wide), pl.ds(block * together, together)

    def multiply(block):
        lanes, pairs = place_of(block)
        mine = norm_ref[:, lanes].T
        for d_ref, grad_ref in ((dgate_ref, ggate_ref), (dup_ref, gup_ref)):
            grad = jnp.dot(mine, d_ref[...], preferred_element_type=F32).astype(BF)
            grad_ref[pairs] = grad.reshape(together, 2, shard, units)

    blocks = list(range(around // together))
    for block in blocks:
        lanes, pairs = place_of(block)
        grad = jnp.dot(low_ref[:, lanes].T, act_ref[...], preferred_element_type=F32).astype(BF)
        gdown_ref[pairs] = grad.reshape(together, 2, shard, units)

    for chunk in range(chunks):
        total.fold(chunk, kept)

    def pass_on(tile, carry):
        exchange.pass_on(tile)
        return carry

    lax.fori_loop(0, tiles, pass_on, 0)
    scatter.start()

    def bring(chunk, carry):
        total.far_copy(chunk).wait_recv()
        here = at_rows(chunk, quarter)
        rows_out = hidden_ref[here, :] + kept[chunk] + take[chunk].astype(F32)
        block_ref[total.own_rows(chunk), :] = rows_out.astype(BF)
        total.far_back(chunk).start()
        return carry

    lax.fori_loop(0, chunks, bring, 0)
    for block in blocks[:2]:
        multiply(block)
    scatter.advance(0)
    for block in blocks[2:]:
        multiply(block)
    scatter.advance(1)
    finish_exchange(exchange, tiles, lambda first, lanes: lax.fori_loop(
        0,
        count - 1 - place,
        lambda hop, state: chained(state, ends, sums, rate_ref, count - 1 - hop, lanes, seqs),
        first,
    ), last_ref, states, zero, False)
    scatter.advance(2)

    def spread_out(chunk, carry):
        total.far_back(chunk).wait_recv()
        total.near_back(chunk).start()
        return carry

    lax.fori_loop(0, chunks, spread_out, 0)
    for moment in range(3, scatter.turns):
        scatter.advance(moment)

    def finish(chunk, carry):
        total.near_back(chunk).wait_recv()
        put_sequences(out_ref, block_ref, chunk, 4 * quarter, buffer)
        total.finish(chunk)
        return carry

    lax.fori_loop(0, chunks, finish, 0)
    scatter.finish()


def backward_kernel(
    count,
    seqs,
    states,
    parts_ref,
    step_ref,
    u_ref,
    dy_ref,
    rate_ref,
    start_ref,
    last_ref,
    *refs,
):
    kinds = (len(refs) - 35) // 3
    dtlow_ref, wdt_ref, xproj_ref, gain_ref, taps_ref, *refs = refs
    xconv_ref, ext_ref, proj_ref, *refs = refs
    grad_refs, refs = refs[:kinds], refs[kinds:]
    inner_ref, ssm_ref, gx_ref, gw_ref, dlog_ref, sums_ref, *refs = refs
    given_refs, came_refs, scratch = refs[:kinds], refs[kinds : 2 * kinds], refs[2 * kinds :]
    spread_ref, held, acc, du_ref, dpre_ref, *scratch = scratch
    sent, got, tail, edge, from_next, head_sems, edge_sems, load_sems, *scratch = scratch
    rows, channels = step_ref.shape
    tokens, tiles = rows // seqs, channels // LANES
    groups = tokens // GROUP
    stop_lanes = pl.ds(2 * states * LANES, LANES)
    place = lax.axis_index("seq")
    low, high = lax.rem(place, 2), place // 2
    zero = jnp.zeros((seqs, LANES), F32)
    greet_pairs(count, True, True)
    scatter = PairScatter(count, grad_refs, given_refs, came_refs, scratch)
    scatter.start()
    spread(parts_ref, states, spread_ref)

    def clear(row, carry):
        acc[at_rows(row, seqs), :] = jnp.zeros((seqs, acc.shape[1]), F32)
        return carry

    lax.fori_loop(0, tokens, clear, 0)

    def whole(tile, carry):
        lanes = at_rows(tile, LANES)

        def again(group, state):
            us = group_tokens(u_ref, group, lanes, seqs)
            for k in range(GROUP):
                token = group * GROUP + k
                here = at_rows(token, seqs)
                step = step_ref[here, lanes]
                drive = step * us[k]
                stop = step + spread_ref[here, stop_lanes]
                fresh = []
                for n in range(states):
                    held[token * states + n] = state[n]
                    decay = jnp.exp2(stop * rate_ref[pl.ds(n * seqs, seqs), lanes])
                    b_one = spread_ref[here, pl.ds(n * LANES, LANES)]
                    fresh.append(decay * state[n] + drive * b_one)
                state = tuple(fresh)
            return state

        state = lax.fori_loop(0, groups, again, state_blocks(start_ref, lanes, seqs, states))
        for n in range(states):
            held[tokens * states + n] = state[n]
        grads = state_blocks(last_ref, lanes, seqs, states)

        def one(back, carry):
            grads, logs, bias = carry
            group = groups - 1 - back
            us = group_tokens(u_ref, group, lanes, seqs)
            pres = [None] * GROUP
            for k in reversed(range(GROUP)):
                token = group * GROUP + k
                here = at_rows(token, seqs)
                step = step_ref[here, lanes]
                dy = dy_ref[here, lanes]
                drive = step * us[k]
                stop = step + spread_ref[here, stop_lanes]
                fresh, fresh_logs = [], []
                on_b, on_rate = zero, zero
                for n in range(states):
                    at = token * states + n
                    on_lanes = pl.ds(n * LANES, LANES)
                    other_lanes = pl.ds((states + n) * LANES, LANES)
                    rate = rate_ref[pl.ds(n * seqs, seqs), lanes]
                    decay = jnp.exp2(stop * rate)
                    lam = grads[n] + dy * spread_ref[here, other_lanes]
                    carried = lam * decay
                    fresh.append(carried)
                    kept = carried * held[at]
                    on_b = on_b + lam * spread_ref[here, on_lanes]
                    on_rate = on_rate + kept * rate
                    fresh_logs.append(logs[n] + kept * step)
                    acc[here, on_lanes] = acc[here, on_lanes] + lam * drive
                    acc[here, other_lanes] = acc[here, other_lanes] + dy * held[at + states]
                du_ref[here, lanes] = step * on_b
                series = step * (1.0 - step * (0.5 - step * (1.0 / 6.0 - step * (1.0 / 24.0))))
                slope = jnp.where(step < 0.05, series, 1.0 - jnp.exp2(step * (-LOG2E)))
                pres[k] = (on_rate * LN2 + us[k] * on_b) * slope
                bias = bias + pres[k]
                grads, logs = tuple(fresh), tuple(fresh_logs)
            dpre_ref[at_rows(group, GROUP * seqs), lanes] = jnp.concatenate(pres, 0).astype(BF)
            return grads, logs, bias

        grads, logs, bias = lax.fori_loop(0, groups, one, (grads, (zero,) * states, zero))
        dlog_ref[:, lanes] = jnp.concatenate(
            [jnp.sum(log, axis=0, keepdims=True) for log in logs], axis=0
        )
        sums_ref[pl.ds(5 * seqs, seqs), lanes] = bias
        for k in range(tiles):

            @pl.when(tile == k)
            def _():
                scatter.advance(k)

        return carry

    lax.fori_loop(0, tiles, whole, 0)

    wide = 2 * LANES
    chunk = 256 if rows % 256 == 0 else rows
    target = lax.broadcasted_iota(jnp.int32, (wide, LANES), 1)
    half = lax.broadcasted_iota(jnp.int32, (wide, LANES), 0) // LANES
    past = taps_ref.shape[0] // 2 - 1
    dbc_ref = spread_ref.at[:, pl.ds((past + 2) * LANES, LANES)]
    dbc_ref[...] = jnp.zeros((rows, LANES), F32)

    def reduce(pair, carry):
        hot = jnp.where(target == LANES - 2 * states + pair * 2 + half, 1.0, 0.0).astype(BF)
        for k in range(rows // chunk):
            here = pl.ds(k * chunk, chunk)
            values = acc[here, at_rows(pair, wide)]
            main = values.astype(BF)
            rest = (values - main.astype(F32)).astype(BF)
            dbc_ref[here, :] += jnp.dot(main, hot, preferred_element_type=F32) + jnp.dot(
                rest, hot, preferred_element_type=F32
            )
        return carry

    lax.fori_loop(0, states, reduce, 0)

    scatter.advance(tiles)

    span = tokens + past
    value_at = tiles * span
    tap_at = [value_at + k * span for k in range(past + 1)]
    proj_lanes = pl.ds((past + 1) * LANES, LANES)
    loads = [
        pltpu.make_async_copy(xconv_ref, acc.at[:, pl.ds(0, channels)], load_sems.at[tiles]),
        pltpu.make_async_copy(proj_ref, spread_ref.at[:, proj_lanes], load_sems.at[tiles + 1]),
    ]
    for tile in range(tiles):
        source = ext_ref.at[:, :, pl.ds(tile * LANES, LANES)]
        target_tiles = held.at[pl.ds(tile * span, span)]
        loads.append(pltpu.make_async_copy(source, target_tiles, load_sems.at[tile]))
    for load in loads:
        load.start()
    head = lax.axis_index("head")
    near = {"head": head // 2 * 2 + 1 - lax.rem(head, 2)}
    far = {"head": lax.rem(head + 2, 4)}
    trade = [
        pltpu.make_async_remote_copy(
            src_ref=sent.at[k],
            dst_ref=got.at[k],
            send_sem=head_sems.at[0, k],
            recv_sem=head_sems.at[1, k],
            device_id=device,
            device_id_type=pl.DeviceIdType.MESH,
        )
        for k, device in enumerate((near, far))
    ]
    for k in range(rows // chunk):
        here = pl.ds(k * chunk, chunk)
        stats = jnp.dot(dpre_ref[here, :], wdt_ref[...], preferred_element_type=F32)
        sent[0, here, :] = (dbc_ref[here, :] + stats).astype(BF)
    trade[0].start()

    source = lax.broadcasted_iota(jnp.int32, (LANES, LANES), 0)
    for k in range(1, past + 1):
        hot = jnp.where(source == 6 * states + k, 1.0, 0.0).astype(BF)
        for m in range(rows // chunk):
            here = pl.ds(m * chunk, chunk)
            spread_ref[here, pl.ds(k * LANES, LANES)] = jnp.dot(
                parts_ref[here, :], hot, preferred_element_type=F32
            )
    scatter.advance(tiles + 1)
    trade[0].wait_recv()
    for k in range(rows // chunk):
        here = pl.ds(k * chunk, chunk)
        sent[1, here, :] = (sent[0, here, :].astype(F32) + got[0, here, :].astype(F32)).astype(BF)
    trade[1].start()

    def step_weights(tile, carry):
        lanes = at_rows(tile, LANES)
        gw_ref[lanes, :] = jnp.dot(
            dpre_ref[:, lanes].T, dtlow_ref[...], preferred_element_type=F32
        )
        return carry

    lax.fori_loop(0, tiles, step_weights, 0)
    scatter.advance(tiles + 2)
    trade[0].wait_send()
    for load in loads:
        load.wait()
    trade[1].wait_recv()
    ssm_ref[...] = jnp.zeros(ssm_ref.shape, F32)
    for k in range(rows // chunk):
        here = pl.ds(k * chunk, chunk)
        stats = sent[1, here, :].astype(F32) + got[1, here, :].astype(F32)
        d_proj, gain_rows = stats_back(stats, spread_ref[here, proj_lanes], gain_ref[...], states)
        sent[0, here, :] = d_proj.astype(BF)
        share = jnp.sum(gain_rows, axis=0, keepdims=True)
        ssm_ref[...] += jnp.broadcast_to(share, ssm_ref.shape)
    block = 16
    size = block * seqs
    edge[...] = jnp.zeros(edge.shape, BF)

    def convolve(tile, carry):
        lanes = at_rows(tile, LANES)
        gx_ref[lanes, :] = jnp.dot(u_ref[:, lanes].T, sent[0], preferred_element_type=F32)
        weights = xproj_ref[lanes, :]
        skip = taps_ref[pl.ds(past + 1, 1), lanes]
        ext_at = tile * span

        def one(part, sums):
            here = at_rows(part, size)
            token = part * block
            d_u = du_ref[here, lanes] + dy_ref[here, lanes] * skip
            d_u = d_u + transposed_dot(sent[0, here, :], weights)
            conv = acc[here, lanes]
            logistic = 1.0 / (1.0 + jnp.exp(-conv))
            d_conv = d_u * logistic * (1.0 + conv * (1.0 - logistic))
            fresh = []
            for k in range(past + 1):
                masked = d_conv
                if k:
                    masked = d_conv * spread_ref[here, pl.ds(k * LANES, LANES)]
                before = held[pl.ds(ext_at + token + past - k, block)]
                blocks = masked.reshape(block, seqs, LANES)
                fresh.append(sums[k] + jnp.sum(blocks * before, axis=0))
                tap = taps_ref[pl.ds(k, 1), lanes]
                held[pl.ds(tap_at[k] + token, block)] = blocks * tap[None]
            fresh.append(sums[past + 1] + jnp.sum(d_conv.reshape(block, seqs, LANES), axis=0))
            return tuple(fresh)

        sums = lax.fori_loop(0, rows // size, one, (zero,) * (past + 2))
        for k in range(past + 2):
            sums_ref[pl.ds(k * seqs, seqs), lanes] = sums[k]
        for k in range(1, past + 1):
            for later in range(past):
                held[tap_at[k] + tokens + later] = zero

        def gather(part, carry):
            token = part * block
            total = held[pl.ds(tap_at[0] + token, block)]
            for k in range(1, past + 1):
                total = total + held[pl.ds(tap_at[k] + token + k, block)]
            total = total.reshape(size, LANES)
            inner_ref[at_rows(part, size), lanes] = total.astype(BF)

            @pl.when(part == rows // size - 1)
            def _():
                tail[:, lanes] = total[size - tail.shape[0] :]

            return carry

        lax.fori_loop(0, rows // size, gather, 0)
        first = [zero] * (tail.shape[0] // seqs - past)
        for token in range(past):
            total = zero
            for k in range(past - token, past + 1):
                total = total + held[tap_at[k] + token - past + k]
            first.append(total)
        edge[:, lanes] = jnp.concatenate(first, axis=0).astype(BF)
        for k in range(tiles):

            @pl.when(tile == k)
            def _():
                scatter.advance(tiles + 3 + k)

        return carry

    lax.fori_loop(0, tiles, convolve, 0)
    hand = pltpu.make_async_remote_copy(
        src_ref=edge,
        dst_ref=from_next,
        send_sem=edge_sems.at[0],
        recv_sem=edge_sems.at[1],
        device_id={"seq": lax.rem(place + count - 1, count)},
        device_id_type=pl.DeviceIdType.MESH,
    )

    @pl.when(place > 0)
    def _():
        hand.start()

    @pl.when(place < count - 1)
    def _():
        hand.wait_recv()
        last_rows = pl.ds(rows - tail.shape[0], tail.shape[0])
        inner_ref[last_rows, :] = (tail[...] + from_next[...].astype(F32)).astype(BF)

    @pl.when(place > 0)
    def _():
        hand.wait_send()

    trade[1].wait_send()
    for turn in range(2 * tiles + 3, scatter.turns):
        scatter.advance(turn)
    scatter.finish()


def stats_back(stats, projected, gains, states):
    rank = LANES - 2 * states
    lane = lax.broadcasted_iota(jnp.int32, stats.shape, 1)
    parts = [
        (lane < rank, rank),
        ((lane >= rank) & (lane < rank + states), states),
        (lane >= rank + states, states),
    ]

    def means(values):
        total = jnp.zeros_like(values)
        for inside, size in parts:
            mean = jnp.sum(jnp.where(inside, values, 0.0), axis=1, keepdims=True) / size
            total = jnp.where(inside, mean, total)
        return total

    scale = lax.rsqrt(means(projected * projected) + EPS)
    normed = projected * scale
    scaled = stats * gains
    return scale * (scaled - normed * means(scaled * normed)), stats * normed


class PairScatter:
    def __init__(self, count, grads, given, came, scratch):
        place = lax.axis_index("seq")
        self.around = count // 2
        self.low, self.high = lax.rem(place, 2), place // 2
        self.grads, self.given, self.came = grads, given, came
        self.mine_buf, self.given_buf, self.sum_buf = scratch[:3]
        self.swap_send, self.swap_recv, self.hop_send, self.hop_recv, self.load_sem = scratch[3:]
        self.items = [(k, steps) for k in range(len(grads)) for steps in range(1, self.around)]
        self.turns = len(self.items) + 1

    def pair(self, steps):
        return lax.rem(self.high + steps, self.around)

    def swap(self, kind, steps):
        return pltpu.make_async_remote_copy(
            src_ref=self.grads[kind].at[self.pair(steps), 1 - self.low],
            dst_ref=self.given[kind].at[steps],
            send_sem=self.swap_send.at[kind, steps],
            recv_sem=self.swap_recv.at[kind, steps],
            device_id={"seq": self.high * 2 + 1 - self.low},
            device_id_type=pl.DeviceIdType.MESH,
        )

    def hop(self, item):
        kind, steps = self.items[item]
        wide = self.grads[kind].shape[-1]
        return pltpu.make_async_remote_copy(
            src_ref=self.sum_buf.at[item % 2, :, pl.ds(0, wide)],
            dst_ref=self.came[kind].at[steps - 1],
            send_sem=self.hop_send.at[kind, steps],
            recv_sem=self.hop_recv.at[kind, steps],
            device_id={"seq": self.pair(steps) * 2 + self.low},
            device_id_type=pl.DeviceIdType.MESH,
        )

    def loads(self, item):
        kind, steps = self.items[item]
        lanes = pl.ds(0, self.grads[kind].shape[-1])
        return [
            pltpu.make_async_copy(
                self.grads[kind].at[self.pair(steps), self.low],
                self.mine_buf.at[item % 2, :, lanes],
                self.load_sem.at[item % 2, 0],
            ),
            pltpu.make_async_copy(
                self.given[kind].at[steps],
                self.given_buf.at[item % 2, :, lanes],
                self.load_sem.at[item % 2, 1],
            ),
        ]

    def start(self):
        for kind, steps in self.items:
            self.swap(kind, steps).start()
        for kind in range(len(self.grads)):
            self.swap(kind, 0).start()

    def advance(self, turn):
        if turn < len(self.items):
            self.swap(*self.items[turn]).wait_recv()
            for load in self.loads(turn):
                load.start()
        item = turn - 1
        if 0 <= item < len(self.items):
            for load in self.loads(item):
                load.wait()
            if item >= 2:
                self.hop(item - 2).wait_send()
            wide = self.grads[self.items[item][0]].shape[-1]
            rows = self.mine_buf.shape[1]

            def add(row, carry):
                here = at_rows(row, 16)
                lanes = pl.ds(0, wide)
                total = self.mine_buf[item % 2, here, lanes].astype(F32) + self.given_buf[
                    item % 2, here, lanes
                ].astype(F32)
                self.sum_buf[item % 2, here, lanes] = total.astype(self.sum_buf.dtype)
                return carry

            lax.fori_loop(0, rows // 16, add, 0)
            self.hop(item).start()

    def finish(self):
        for item in range(max(0, len(self.items) - 2), len(self.items)):
            self.hop(item).wait_send()
        for item in range(len(self.items)):
            self.hop(item).wait_recv()
            self.swap(*self.items[item]).wait_send()
        for kind in range(len(self.grads)):
            self.swap(kind, 0).wait()


def scatter_scratch(count, grads):
    rows = grads[0].shape[2]
    wide = max(grad.shape[3] for grad in grads)
    sems = pltpu.SemaphoreType.DMA((len(grads), count // 2))
    buffer = pltpu.VMEM((2, rows, wide), grads[0].dtype)
    return [buffer] * 3 + [sems] * 4 + [pltpu.SemaphoreType.DMA((2, 2))]


def exchange_scratch(count, seqs, states, channels):
    sems = pltpu.SemaphoreType.DMA((2, count // 2, channels // LANES))
    return [
        pltpu.VMEM((count, states * seqs, channels), BF),
        pltpu.VMEM((count, seqs, channels), F32),
    ] + [sems] * 4


def state_call(body, ident, seqs, states, columns, ins, outs, scratch, ops, hosted):
    count = lax.axis_size("seq")
    rows, channels = ins[1].shape
    in_vmem = pl.BlockSpec(memory_space=pltpu.VMEM)
    anywhere = pl.BlockSpec(memory_space=pl.ANY)
    return pl.pallas_call(
        functools.partial(body, count, seqs, states),
        in_specs=[in_vmem] * (len(ins) - hosted[0]) + [anywhere] * hosted[0],
        out_specs=tuple([in_vmem] * (len(outs) - hosted[1]) + [anywhere] * hosted[1]),
        out_shape=tuple(outs),
        scratch_shapes=[pltpu.VMEM((rows, columns * LANES), F32)] + scratch,
        compiler_params=pltpu.CompilerParams(
            collective_id=ident, has_side_effects=True, vmem_limit_bytes=62 * 1024 * 1024
        ),
        cost_estimate=pl.CostEstimate(
            flops=ops * rows * channels * states,
            bytes_accessed=16 * 1024 * 1024,
            transcendentals=0,
        ),
    )(*ins)


class BlockGather:
    def __init__(self, count, source, target, sems):
        place = lax.axis_index("seq")
        self.around = count // 2
        self.low, self.high = lax.rem(place, 2), place // 2
        self.place = place
        self.source, self.target = source, target
        self.hop_send, self.hop_recv, self.swap_send, self.swap_recv, self.local_sem = sems
        self.mate = self.high * 2 + 1 - self.low
        self.pieces = pieces_of(source.shape[-1])

    def pair(self, steps):
        return lax.rem(self.high + steps + self.around, self.around) * 2 + self.low

    def lanes(self, piece):
        size = self.source.shape[-1] // self.pieces
        return pl.ds(piece * size, size)

    def local(self):
        return pltpu.make_async_copy(self.source, self.target.at[self.place], self.local_sem.at[0])

    def hop(self, piece, steps):
        return pltpu.make_async_remote_copy(
            src_ref=self.source.at[:, self.lanes(piece)],
            dst_ref=self.target.at[self.place, :, self.lanes(piece)],
            send_sem=self.hop_send.at[piece, steps],
            recv_sem=self.hop_recv.at[piece, steps],
            device_id={"seq": self.pair(steps)},
            device_id_type=pl.DeviceIdType.MESH,
        )

    def swap(self, piece, steps):
        block = self.target.at[self.pair(-steps), :, self.lanes(piece)]
        return pltpu.make_async_remote_copy(
            src_ref=block if steps else self.source.at[:, self.lanes(piece)],
            dst_ref=block,
            send_sem=self.swap_send.at[piece, steps],
            recv_sem=self.swap_recv.at[piece, steps],
            device_id={"seq": self.mate},
            device_id_type=pl.DeviceIdType.MESH,
        )

    def start(self):
        self.local().start()
        for piece in range(self.pieces):
            for steps in range(1, self.around):
                self.hop(piece, steps).start()
        for piece in range(self.pieces):
            self.swap(piece, 0).start()

    def relay(self, piece):
        for steps in range(1, self.around):
            self.hop(piece, steps).wait_recv()
            self.swap(piece, steps).start()

    def finish(self):
        self.local().wait()
        for piece in range(self.pieces):
            for steps in range(1, self.around):
                self.hop(piece, steps).wait_send()
            for steps in range(self.around):
                self.swap(piece, steps).wait()


def pieces_of(width):
    for size in (384, 256):
        if width % size == 0:
            return width // size
    return 1


def gather_sems(around, width):
    pieces = pieces_of(width)
    return [pltpu.SemaphoreType.DMA((pieces, around))] * 4 + [pltpu.SemaphoreType.DMA((1,))]


def greet_pairs(count, heads=False, ring=False):
    place = lax.axis_index("seq")
    around = count // 2
    low, high = lax.rem(place, 2), place // 2
    barrier = pltpu.get_barrier_semaphore()
    peers = [lax.rem(high + steps, around) * 2 + low for steps in range(1, around)]
    peers = [{"seq": device} for device in peers + [high * 2 + 1 - low]]
    if heads:
        head = lax.axis_index("head")
        low, high = lax.rem(head, 2), head // 2
        peers += [{"head": high * 2 + 1 - low}, {"head": 2 - 2 * high + low}]
    if ring:
        peers += [{"seq": lax.rem(place + 1, count)}, {"seq": lax.rem(place + count - 1, count)}]
    for device in peers:
        pl.semaphore_signal(barrier, inc=1, device_id=device, device_id_type=pl.DeviceIdType.MESH)
    pl.semaphore_wait(barrier, len(peers))


class HeadSum:
    def __init__(self, part, half, give, take, whole, sems):
        head = lax.axis_index("head")
        self.low, self.high = lax.rem(head, 2), head // 2
        self.near = {"head": self.high * 2 + 1 - self.low}
        self.far = {"head": 2 - 2 * self.high + self.low}
        self.part, self.half, self.give, self.take, self.whole = part, half, give, take, whole
        self.sems = sems
        self.size = half.shape[1]

    def copy(self, source, target, kind, chunk, device):
        return pltpu.make_async_remote_copy(
            src_ref=source,
            dst_ref=target,
            send_sem=self.sems.at[kind, 0, chunk],
            recv_sem=self.sems.at[kind, 1, chunk],
            device_id=device,
            device_id_type=pl.DeviceIdType.MESH,
        )

    def rows(self, chunk, bit):
        start = pl.multiple_of((chunk * 2 + bit) * self.size, self.size)
        return pl.ds(start, self.size)

    def own_rows(self, chunk):
        quarter = self.size // 2
        start = (chunk * 2 + self.low) * self.size + self.high * quarter
        return pl.ds(pl.multiple_of(start, quarter), quarter)

    def near_copy(self, chunk):
        return self.copy(
            self.part.at[self.rows(chunk, 1 - self.low)], self.half.at[chunk], 0, chunk, self.near
        )

    def far_copy(self, chunk):
        return self.copy(self.give.at[chunk], self.take.at[chunk], 1, chunk, self.far)

    def far_back(self, chunk):
        here = self.whole.at[self.own_rows(chunk)]
        return self.copy(here, here, 2, chunk, self.far)

    def near_back(self, chunk):
        here = self.whole.at[self.rows(chunk, self.low)]
        return self.copy(here, here, 3, chunk, self.near)

    def fold(self, chunk, kept):
        self.near_copy(chunk).wait_recv()
        quarter = self.size // 2
        base = (chunk * 2 + self.low) * self.size
        for mine in (False, True):
            bit = self.high if mine else 1 - self.high
            start = pl.multiple_of(bit * quarter, quarter)
            at = pl.multiple_of(base + bit * quarter, quarter)
            total = self.part[pl.ds(at, quarter), :].astype(F32)
            total = total + self.half[chunk, pl.ds(start, quarter), :].astype(F32)
            if mine:
                kept[chunk] = total
            else:
                self.give[chunk] = total.astype(BF)
                self.far_copy(chunk).start()

    def finish(self, chunk, near=True):
        copies = [self.far_copy, self.far_back, self.near_back]
        for copy in copies + [self.near_copy] * near:
            copy(chunk).wait_send()


def put_sequences(target, rows_ref, chunk, size, buffer):
    seqs = target.shape[0]
    span = size // seqs
    for m in range(buffer.shape[0]):
        lanes = pl.ds(m * LANES, LANES)
        buffer[m] = rows_ref[at_rows(chunk, size), lanes].astype(F32)
        for k in range(seqs):
            rows = buffer[m, pl.ds(k, span, stride=seqs), :]
            target[k, at_rows(chunk, span), lanes] = rows.astype(target.dtype)


def transposed_dot(left, right):
    return lax.dot_general(left, right, (((1,), (1,)), ((), ())), preferred_element_type=F32)


def ffn_kernel(count, chunks, *refs):
    g_ref, out_ref, gain_ref, *refs = refs
    sources, up_shard, down_shard, refs = refs[:3], refs[3], refs[4], refs[5:]
    hidden_ref, norm_ref, act_ref, dgate_ref, dup_ref, dnorm_gain_ref, part_out_ref, *refs = refs
    dhidden_ref, dmix_ref, *refs = refs
    up_ref, down_ref, *refs = refs
    part, half_a, give_a, take_a, half_b, give_b, take_b, kept, *refs = refs
    gate_buf, up_buf, sems_a, sems_b, *refs = refs
    x_ref, gate_ref, low_ref, fetch_sems, *refs = refs
    fetch = Fetch(sources, (x_ref, gate_ref, low_ref), fetch_sems)
    fetch.start()
    gathers = [
        BlockGather(count, up_shard, up_ref, refs[:5]),
        BlockGather(count, down_shard, down_ref, refs[5:]),
    ]
    mix = HeadSum(part, half_a, give_a, take_a, norm_ref, sems_a)
    back = HeadSum(part, half_b, give_b, take_b, dmix_ref, sems_b)
    size = g_ref.shape[0] // chunks
    quarter = size // 4
    width = x_ref.shape[1]
    shard, units = down_ref.shape[1:]
    channels = g_ref.shape[1]
    greet_pairs(count, True)
    for gather in gathers:
        gather.start()
    fourth = -(-gathers[0].pieces // chunks)

    def relay(gather, chunk):
        for k in range(chunks):
            pieces = range(gather.pieces)[k * fourth : (k + 1) * fourth]
            if pieces:

                @pl.when(chunk == k)
                def _():
                    for piece in pieces:
                        gather.relay(piece)


    def project(chunk, carry):
        here = at_rows(chunk, size)
        weights = out_ref[:, :, pl.ds(channels, channels)].reshape(width, channels)
        part[here, :] = transposed_dot(g_ref[here, :], weights).astype(BF)
        mix.near_copy(chunk).start()
        return carry

    lax.fori_loop(0, chunks, project, 0)

    def fold(chunk, carry):
        mix.fold(chunk, kept)
        return carry

    lax.fori_loop(0, chunks, fold, 0)

    def normalise(chunk, carry):
        mix.far_copy(chunk).wait_recv()
        here = at_rows(chunk, quarter)
        own = x_ref[mix.own_rows(chunk), :].astype(F32)
        hidden = own + kept[chunk] + take_a[chunk].astype(F32)
        hidden_ref[here, :] = hidden
        scale = lax.rsqrt(jnp.mean(hidden * hidden, axis=1, keepdims=True) + EPS)
        norm_ref[mix.own_rows(chunk), :] = (hidden * scale * gain_ref[...]).astype(BF)
        mix.far_back(chunk).start()
        relay(gathers[0], chunk)
        return carry

    fetch.wait(0)
    lax.fori_loop(0, chunks, normalise, 0)
    fetch.wait(1)
    mix.far_back(0).wait_recv()
    mix.near_back(0).start()
    gathers[0].finish()
    per_block = max(1, count // 4)
    wide = per_block * shard
    lanes_block = 256 if units % 256 == 0 else units

    def widen(chunk, carry):
        here = at_rows(chunk, size)

        @pl.when(chunk + 1 < chunks)
        def _():
            mix.far_back(chunk + 1).wait_recv()
            mix.near_back(chunk + 1).start()

        mix.near_back(chunk).wait_recv()
        rows = norm_ref[here, :]
        for k in range(units // lanes_block):
            lanes = pl.ds(k * lanes_block, lanes_block)
            block = lambda ref: ref[:, :, lanes].reshape(width, lanes_block)
            gate_buf[here, lanes] = jnp.dot(rows, block(gate_ref), preferred_element_type=F32)
            up_buf[here, lanes] = jnp.dot(rows, block(up_ref), preferred_element_type=F32)
        relay(gathers[1], chunk)
        return carry

    lax.fori_loop(0, chunks, widen, 0)
    gathers[1].finish()
    fetch.wait(2)

    def feed(chunk, carry):
        here = at_rows(chunk, size)
        mix.near_copy(chunk).wait_send()
        grads = low_ref[here, :]
        for k in range(units // lanes_block):
            lanes = pl.ds(k * lanes_block, lanes_block)
            block = lambda ref: ref[:, :, lanes].reshape(width, lanes_block)
            gate, up = gate_buf[here, lanes], up_buf[here, lanes]
            d_act = jnp.dot(grads, block(down_ref), preferred_element_type=F32)
            logistic = 1.0 / (1.0 + jnp.exp(-gate))
            silu = gate * logistic
            act_ref[here, lanes] = (silu * up).astype(BF)
            slope = logistic * (1.0 + gate * (1.0 - logistic))
            dgate_ref[here, lanes] = (d_act * up * slope).astype(BF)
            dup_ref[here, lanes] = (d_act * silu).astype(BF)
        for k in range(count // per_block):
            lanes = pl.ds(k * wide, wide)
            block = lambda ref: ref[pl.ds(k * per_block, per_block)].reshape(wide, units)
            total = transposed_dot(dgate_ref[here, :], block(gate_ref))
            total = total + transposed_dot(dup_ref[here, :], block(up_ref))
            part[here, lanes] = total.astype(BF)
        back.near_copy(chunk).start()
        for k in range(count // per_block):
            lanes = pl.ds(k * wide, wide)
            block = down_ref[pl.ds(k * per_block, per_block)].reshape(wide, units)
            part_out_ref[here, lanes] = transposed_dot(act_ref[here, :], block).astype(BF)

        @pl.when(chunk >= 1)
        def _():
            back.fold(chunk - 1, kept)

        return carry

    lax.fori_loop(0, chunks, feed, 0)
    back.fold(chunks - 1, kept)
    dnorm_gain_ref[...] = jnp.zeros(dnorm_gain_ref.shape, F32)

    def turn(chunk, carry):
        back.far_copy(chunk).wait_recv()
        here = at_rows(chunk, quarter)
        hidden = hidden_ref[here, :]
        scale = lax.rsqrt(jnp.mean(hidden * hidden, axis=1, keepdims=True) + EPS)
        normed = hidden * scale
        d_norm = kept[chunk] + take_b[chunk].astype(F32)
        dnorm_gain_ref[...] += jnp.sum(d_norm * normed, axis=0, keepdims=True)
        scaled = d_norm * gain_ref[...]
        shift = jnp.mean(scaled * normed, axis=1, keepdims=True)
        own = low_ref[back.own_rows(chunk), :].astype(F32)
        d_hidden = own + scale * (scaled - normed * shift)
        dhidden_ref[here, :] = d_hidden
        dmix_ref[back.own_rows(chunk), :] = d_hidden.astype(BF)
        back.far_back(chunk).start()
        return carry

    lax.fori_loop(0, chunks, turn, 0)

    def spread_out(chunk, carry):
        back.far_back(chunk).wait_recv()
        back.near_back(chunk).start()
        return carry

    lax.fori_loop(0, chunks, spread_out, 0)

    def finish(chunk, carry):
        back.near_back(chunk).wait_recv()
        mix.finish(chunk, False)
        back.finish(chunk)
        return carry

    lax.fori_loop(0, chunks, finish, 0)


CHUNKS = 4


def sum_scratch(rows, width, part=True):
    chunk = rows // CHUNKS
    parts = [pltpu.VMEM((rows, width), BF)] if part else []
    return parts + [
        pltpu.VMEM((CHUNKS, chunk // 2, width), BF),
        pltpu.VMEM((CHUNKS, chunk // 4, width), BF),
        pltpu.VMEM((CHUNKS, chunk // 4, width), BF),
    ]


def kept_scratch(rows, width):
    return pltpu.VMEM((CHUNKS, rows // CHUNKS // 4, width), F32)


SUM_SEMS = pltpu.SemaphoreType.DMA((4, 2, CHUNKS))


def ffn_call(g_low, mix_blocks, x_low, gain, grad_low, gate_blocks, w_up, w_down_t):
    count = lax.axis_size("seq")
    rows, width = grad_low.shape
    units = w_down_t.shape[1]
    shape = jax.ShapeDtypeStruct
    in_vmem = pl.BlockSpec(memory_space=pltpu.VMEM)
    anywhere = pl.BlockSpec(memory_space=pl.ANY)
    outs = [
        shape((rows // 4, width), F32),
        shape((rows, width), BF),
        shape((rows, units), BF),
        shape((rows, units), BF),
        shape((rows, units), BF),
        shape((1, width), F32),
        shape((rows, width), BF),
        shape((rows // 4, width), F32),
        shape((rows, width), BF),
    ]
    return pl.pallas_call(
        functools.partial(ffn_kernel, count, CHUNKS),
        in_specs=[in_vmem] * 3 + [anywhere] * 5,
        out_specs=tuple([in_vmem] * len(outs)),
        out_shape=tuple(outs),
        scratch_shapes=[pltpu.VMEM((count,) + w_down_t.shape, BF)] * 2
        + sum_scratch(rows, width)
        + sum_scratch(rows, width, False)
        + [kept_scratch(rows, width)]
        + [pltpu.VMEM((rows, units), F32)] * 2
        + [SUM_SEMS] * 2
        + fetch_scratch([x_low, gate_blocks, grad_low])
        + gather_sems(count // 2, units) * 2,
        compiler_params=pltpu.CompilerParams(
            collective_id=5, has_side_effects=True, vmem_limit_bytes=62 * 1024 * 1024
        ),
        cost_estimate=pl.CostEstimate(
            flops=14 * rows * width * units, bytes_accessed=40 * 1024 * 1024, transcendentals=0
        ),
    )(g_low, mix_blocks, gain, x_low, gate_blocks, grad_low, w_up, w_down_t)


def input_kernel(count, chunks, kinds, *refs):
    inner_ref, z_ref, in_x_ref, gain_ref, dhidden_ref, *refs = refs
    sources, pack_ref, refs = refs[:3], refs[3], refs[4:]
    olds, refs = [refs[k * kinds : (k + 1) * kinds] for k in range(3)], refs[3 * kinds :]
    out_ref, gain_out_ref, *refs = refs
    own_refs, refs = refs[: kinds + 1], refs[kinds + 1 :]
    pack_given, pack_came, *refs = refs
    part, half, give, take, kept, rows_ref, buffer, sems, *refs = refs
    sent, got, vector_sems, grad_ref, given, came, *refs = refs
    norm_ref, mix_ref, x_ref, fetch_sems, *refs = refs
    channels = inner_ref.shape[1]
    sources = [sources[0], sources[1].at[:, :, pl.ds(0, channels)], sources[2]]
    fetch = Fetch(sources, (norm_ref, mix_ref, x_ref), fetch_sems)
    fetch.start()
    owned = OwnSum(count, olds, own_refs, refs[:3])
    refs = refs[3:]
    scatter = PairScatter(count, [grad_ref], [given], [came], refs[:8])
    pack = PairScatter(count, [pack_ref], [pack_given], [pack_came], refs[8:])
    back = HeadSum(part, half, give, take, rows_ref, sems)
    size = inner_ref.shape[0] // chunks
    quarter = size // 4
    shard, channels = in_x_ref.shape[1:]
    per_block = max(1, count // 4)
    wide = per_block * shard
    greet_pairs(count, True)
    pack.start()
    owned.load(0)
    around, _, shard_rows, _ = grad_ref.shape
    together = max(1, 384 // (2 * shard_rows))
    fetch.wait(0)
    for block in range(around // together):
        lanes = pl.ds(block * together * 2 * shard_rows, together * 2 * shard_rows)
        grad = jnp.dot(norm_ref[:, lanes].T, inner_ref[...], preferred_element_type=F32)
        grad = grad.astype(BF).reshape(together, 2, shard_rows, channels)
        grad_ref[pl.ds(block * together, together)] = grad
    scatter.start()
    turns = [(scatter, turn) for turn in range(scatter.turns)]
    turns += [(pack, turn) for turn in range(pack.turns)]
    share = -(-len(turns) // (3 * chunks))
    early = 2 * chunks * share

    def move(chunk, stage):
        for k in range(chunks):
            todo = turns[(stage * chunks + k) * share :][:share]
            if todo:

                @pl.when(chunk == k)
                def _():
                    for moving, turn in todo:
                        moving.advance(turn)

    def own_step(chunk, first):
        for k in range(chunks):
            if first + k < kinds:

                @pl.when(chunk == k)
                def _():
                    owned.add(first + k)

    fetch.wait(1, 2)

    def project(chunk, carry):
        here = at_rows(chunk, size)
        for k in range(count // per_block):
            blocks = pl.ds(k * per_block, per_block)
            total = transposed_dot(inner_ref[here, :], in_x_ref[blocks].reshape(wide, channels))
            in_z = mix_ref[blocks].reshape(wide, channels)
            total = total + transposed_dot(z_ref[here, :], in_z)
            part[here, pl.ds(k * wide, wide)] = total.astype(BF)
        back.near_copy(chunk).start()
        return carry

    lax.fori_loop(0, chunks, project, 0)

    def fold(chunk, carry):
        back.fold(chunk, kept)
        own_step(chunk, 0)
        return carry

    lax.fori_loop(0, chunks, fold, 0)
    gain_out_ref[...] = jnp.zeros(gain_out_ref.shape, F32)
    around = scatter.around

    def vector(stage, slot, device):
        return pltpu.make_async_remote_copy(
            src_ref=sent.at[stage],
            dst_ref=got.at[slot],
            send_sem=vector_sems.at[0, slot],
            recv_sem=vector_sems.at[1, slot],
            device_id=device,
            device_id_type=pl.DeviceIdType.MESH,
        )

    stages = [
        [vector(0, 0, {"seq": scatter.high * 2 + 1 - scatter.low})],
        [
            vector(1, steps, {"seq": scatter.pair(steps) * 2 + scatter.low})
            for steps in range(1, around)
        ],
        [vector(2, around, back.near)],
        [vector(3, around + 1, back.far)],
    ]

    def pass_sum(stage):
        value = gain_out_ref[...]
        if stage > 0:
            for copy in stages[stage - 1]:
                copy.wait_recv()
            slots = [[0], list(range(1, around)), [around], [around + 1]][stage - 1]
            for slot in slots:
                value = value + got[slot]
            gain_out_ref[...] = value
        if stage < len(stages):
            sent[stage] = value
            for copy in stages[stage]:
                copy.start()

    def turn(chunk, carry):
        back.far_copy(chunk).wait_recv()
        here = at_rows(chunk, quarter)
        values = x_ref[back.own_rows(chunk), :].astype(F32)
        scale = lax.rsqrt(jnp.mean(values * values, axis=1, keepdims=True) + EPS)
        normed = values * scale
        d_norm = kept[chunk] + take[chunk].astype(F32)
        share_of_sum = jnp.sum(d_norm * normed, axis=0, keepdims=True)
        gain_out_ref[...] += jnp.broadcast_to(share_of_sum, gain_out_ref.shape)
        scaled = d_norm * gain_ref[...]
        shift = jnp.mean(scaled * normed, axis=1, keepdims=True)
        total = dhidden_ref[here, :] + scale * (scaled - normed * shift)
        rows_ref[back.own_rows(chunk), :] = total.astype(BF)
        back.far_back(chunk).start()
        move(chunk, 0)
        return carry

    lax.fori_loop(0, chunks, turn, 0)
    pass_sum(0)

    def spread_out(chunk, carry):
        back.far_back(chunk).wait_recv()
        back.near_back(chunk).start()
        move(chunk, 1)
        own_step(chunk, chunks)
        return carry

    lax.fori_loop(0, chunks, spread_out, 0)
    for stage in range(1, len(stages) + 1):
        pass_sum(stage)
    for old in range(2 * chunks, kinds):
        owned.add(old)
    for moving, turn in turns[early:]:
        moving.advance(turn)
    for copies in stages:
        for copy in copies:
            copy.wait_send()

    def finish(chunk, carry):
        back.near_back(chunk).wait_recv()
        put_sequences(out_ref, rows_ref, chunk, size, buffer)
        back.finish(chunk)
        return carry

    lax.fori_loop(0, chunks, finish, 0)
    scatter.finish()
    pack.finish()
    place = lax.axis_index("seq")
    total = grad_ref[place // 2, lax.rem(place, 2)].astype(F32) + given[0].astype(F32)
    for k in range(around - 1):
        total = total + came[k].astype(F32)
    own_refs[kinds][...] = total
    owned.finish()


class OwnSum:
    def __init__(self, count, olds, targets, scratch):
        self.place = lax.axis_index("seq")
        self.around = count // 2
        self.grads, self.given, self.came = olds
        self.targets = targets
        self.parts, self.total, self.sems = scratch

    def sources(self, kind):
        own = self.grads[kind].at[self.place // 2, lax.rem(self.place, 2)]
        came = [self.came[kind].at[k] for k in range(self.around - 1)]
        return [own, self.given[kind].at[0]] + came

    def loads(self, kind):
        lanes = pl.ds(0, self.targets[kind].shape[1])
        return [
            pltpu.make_async_copy(source, self.parts.at[k, :, lanes], self.sems.at[k])
            for k, source in enumerate(self.sources(kind))
        ]

    def store(self, kind):
        lanes = pl.ds(0, self.targets[kind].shape[1])
        return pltpu.make_async_copy(
            self.total.at[:, lanes], self.targets[kind], self.sems.at[self.around + 1]
        )

    def load(self, kind):
        for load in self.loads(kind):
            load.start()

    def add(self, kind):
        for load in self.loads(kind):
            load.wait()
        if kind:
            self.store(kind - 1).wait()
        lanes = pl.ds(0, self.targets[kind].shape[1])

        def one(row, carry):
            here = at_rows(row, 16)
            total = self.parts[0, here, lanes].astype(F32)
            for k in range(1, self.around + 1):
                total = total + self.parts[k, here, lanes].astype(F32)
            self.total[here, lanes] = total
            return carry

        lax.fori_loop(0, self.total.shape[0] // 16, one, 0)
        self.store(kind).start()
        if kind + 1 < len(self.grads):
            self.load(kind + 1)

    def finish(self):
        self.store(len(self.grads) - 1).wait()


def moved_shapes(grads):
    shape = jax.ShapeDtypeStruct
    around = grads[0].shape[0]
    given = [shape((around,) + grad.shape[2:], grad.dtype) for grad in grads]
    return given + [shape((around - 1,) + grad.shape[2:], grad.dtype) for grad in grads]


def input_call(d_inner, d_z, in_x_blocks, mix_blocks, x_low, x_norm, gain, d_hidden, pack, olds, dims):
    count = lax.axis_size("seq")
    around = count // 2
    rows, channels = d_inner.shape
    width = x_low.shape[1]
    shape = jax.ShapeDtypeStruct
    in_vmem = pl.BlockSpec(memory_space=pltpu.VMEM)
    anywhere = pl.BlockSpec(memory_space=pl.ANY)
    grads, given, came = olds
    shard = grads[0].shape[2]
    widest = max(grad.shape[3] for grad in grads)
    moved = moved_shapes([pack])
    late = shape((around, 2, shard, channels), BF)
    return pl.pallas_call(
        functools.partial(input_kernel, count, CHUNKS, len(grads)),
        in_specs=[in_vmem] * 5 + [anywhere] * (3 * len(grads) + 4),
        out_specs=tuple(
            [in_vmem] * 2 + [anywhere] * len(grads) + [in_vmem] + [anywhere] * len(moved)
        ),
        out_shape=tuple(
            [shape(dims, F32), shape((8, width), F32)]
            + [shape((shard, grad.shape[3]), F32) for grad in grads]
            + [shape((shard, channels), F32)]
            + moved
        ),
        scratch_shapes=sum_scratch(rows, width)
        + [kept_scratch(rows, width), pltpu.VMEM((rows, width), BF)]
        + [pltpu.VMEM((width // LANES, rows // CHUNKS, LANES), F32), SUM_SEMS]
        + [pltpu.VMEM((4, 8, width), F32), pltpu.VMEM((around + 2, 8, width), F32)]
        + [pltpu.SemaphoreType.DMA((2, around + 2))]
        + [pltpu.VMEM(late.shape, BF), pltpu.VMEM((around, shard, channels), BF)]
        + [pltpu.VMEM((around - 1, shard, channels), BF)]
        + fetch_scratch([x_norm, in_x_blocks, x_low])
        + [pltpu.VMEM((around + 1, shard, widest), BF), pltpu.VMEM((shard, widest), F32)]
        + [pltpu.SemaphoreType.DMA((around + 2,))]
        + scatter_scratch(count, [late])
        + scatter_scratch(count, [pack]),
        compiler_params=pltpu.CompilerParams(
            collective_id=6, has_side_effects=True, vmem_limit_bytes=62 * 1024 * 1024
        ),
        cost_estimate=pl.CostEstimate(
            flops=4 * rows * width * d_inner.shape[1],
            bytes_accessed=40 * 1024 * 1024,
            transcendentals=0,
        ),
    )(
        d_inner,
        d_z,
        in_x_blocks,
        gain,
        d_hidden,
        x_norm,
        mix_blocks,
        x_low,
        pack,
        *grads,
        *given,
        *came,
    )


class Fetch:
    def __init__(self, sources, targets, sems):
        self.copies = [
            pltpu.make_async_copy(source, target, sems.at[k])
            for k, (source, target) in enumerate(zip(sources, targets))
        ]

    def start(self):
        for copy in self.copies:
            copy.start()

    def wait(self, *which):
        for k in which:
            self.copies[k].wait()


def fetch_scratch(values):
    buffers = [pltpu.VMEM(value.shape, value.dtype) for value in values]
    return buffers + [pltpu.SemaphoreType.DMA((len(values),))]


def pairs_of(axis):
    return lax.axis_size(axis) // 2


def hop(value, steps):
    count = lax.axis_size("seq")
    return lax.ppermute(value, "seq", [(s, (s + 2 * steps) % count) for s in range(count)])


def swap(value, axis, bit):
    return lax.ppermute(value, axis, [(s, s ^ bit) for s in range(lax.axis_size(axis))])


def owner_blocks(value):
    return value.reshape((pairs_of("seq"), 2, -1) + value.shape[1:])


def scatter_half(blocks, theirs):
    place = lax.axis_index("seq")
    around = pairs_of("seq")
    low, high = place % 2, place // 2
    mine = lax.dynamic_index_in_dim(blocks, low, 1, False)
    half = mine.astype(F32) + theirs.astype(F32)
    total = lax.dynamic_index_in_dim(half, high, 0, False)
    half = half.astype(blocks.dtype)
    for steps in range(1, around):
        part = lax.dynamic_index_in_dim(half, (high + steps) % around, 0, False)
        total = total + hop(part, steps).astype(F32)
    return total


def scatter_rows(value, kind=BF):
    low = lax.axis_index("seq") % 2
    blocks = owner_blocks(value.astype(kind))
    theirs = lax.dynamic_index_in_dim(blocks, 1 - low, 1, False)
    return scatter_half(blocks, swap(theirs, "seq", 1))


def scatter_own(blocks, given, came):
    place = lax.axis_index("seq")
    own = blocks.reshape((-1,) + blocks.shape[2:])
    total = lax.dynamic_index_in_dim(own, place, 0, False).astype(F32) + given[0].astype(F32)
    for k in range(came.shape[0]):
        total = total + came[k].astype(F32)
    return total


def head_bits():
    return (lax.axis_size("head") - 1).bit_length()


def head_scatter(value):
    place = lax.axis_index("head")
    width = value.shape[1]
    value = value.reshape(CHUNKS, -1, width)
    for k in range(head_bits()):
        bit = place // 2**k % 2
        halves = value.astype(BF).reshape(CHUNKS, 2, -1, width)
        keep = lax.dynamic_index_in_dim(halves, bit, 1, False)
        send = lax.dynamic_index_in_dim(halves, 1 - bit, 1, False)
        value = keep.astype(F32) + swap(send, "head", 2**k).astype(F32)
    return value.reshape(-1, width)


def head_part(value):
    place = lax.axis_index("head")
    width = value.shape[1]
    value = value.reshape(CHUNKS, -1, width)
    for k in range(head_bits()):
        halves = value.reshape(CHUNKS, 2, -1, width)
        value = lax.dynamic_index_in_dim(halves, place // 2**k % 2, 1, False)
    return value.reshape(-1, width)


def head_gather(value):
    place = lax.axis_index("head")
    width = value.shape[1]
    value = value.reshape(CHUNKS, -1, width)
    for k in reversed(range(head_bits())):
        got = swap(value, "head", 2**k)
        first = place // 2**k % 2 == 0
        both = [jnp.where(first, value, got), jnp.where(first, got, value)]
        value = jnp.concatenate(both, axis=1)
    return value.reshape(-1, width)


def head_total(value, kind):
    for k in range(head_bits()):
        value = value.astype(kind)
        value = value.astype(F32) + swap(value, "head", 2**k).astype(F32)
    return value


def first_kernel(count, kinds, turned, *refs):
    sources, plain, refs = refs[:kinds], refs[kinds : kinds + turned], refs[kinds + turned :]
    targets, outs, refs = refs[:kinds], refs[kinds : kinds + turned], refs[kinds + turned :]
    buffer, *refs = refs
    gathers = [
        BlockGather(count, sources[k], targets[k], refs[5 * k : 5 * k + 5]) for k in range(kinds)
    ]
    greet_pairs(count)
    for gather in gathers:
        gather.start()
    for source, target in zip(plain, outs):
        seqs, tokens, _ = source.shape

        def widen(k, carry):
            for m in range(buffer.shape[0]):
                lanes = pl.ds(m * LANES, LANES)
                buffer[m, at_rows(k, tokens), :] = source[k, :, lanes].astype(F32)
            return carry

        lax.fori_loop(0, seqs, widen, 0)

        def turn(pair, carry):
            for m in range(buffer.shape[0]):
                both = [buffer[m, pl.ds(2 * pair + k, seqs, stride=tokens), :] for k in range(2)]
                both = jnp.concatenate(both, axis=0).astype(BF)
                target[at_rows(pair, 2 * seqs), pl.ds(m * LANES, LANES)] = both
            return carry

        lax.fori_loop(0, tokens // 2, turn, 0)
    for gather in gathers:
        for piece in range(gather.pieces):
            gather.relay(piece)
    for gather in gathers:
        gather.finish()


def first_gather(values, plain):
    count = lax.axis_size("seq")
    around = count // 2
    seqs, tokens, width = plain[0].shape
    shape = jax.ShapeDtypeStruct
    in_vmem = pl.BlockSpec(memory_space=pltpu.VMEM)
    anywhere = pl.BlockSpec(memory_space=pl.ANY)
    return pl.pallas_call(
        functools.partial(first_kernel, count, len(values), len(plain)),
        out_shape=tuple(
            [shape((count,) + v.shape, v.dtype) for v in values]
            + [shape((seqs * tokens, width), BF) for _ in plain]
        ),
        in_specs=[anywhere] * len(values) + [in_vmem] * len(plain),
        out_specs=tuple([anywhere] * len(values) + [in_vmem] * len(plain)),
        scratch_shapes=[pltpu.VMEM((width // LANES, seqs * tokens, LANES), F32)]
        + [sem for v in values for sem in gather_sems(around, v.shape[-1])],
        compiler_params=pltpu.CompilerParams(
            collective_id=0, has_side_effects=True, vmem_limit_bytes=40 * 1024 * 1024
        ),
    )(*values, *plain)


def shards(
    x_in,
    seg_ids,
    norm1_gain,
    w_in_x,
    w_in_z,
    conv_w,
    conv_b,
    w_xproj,
    ssm_gain,
    w_dt,
    dt_bias,
    a_log,
    d_skip,
    w_out,
    norm2_gain,
    w_gate,
    w_up,
    w_down,
    d_out,
):
    count = lax.axis_size("seq")
    place = lax.axis_index("seq")
    seqs, tokens, width = x_in.shape
    rows = seqs * tokens
    taps = conv_w.shape[0]
    rank = w_dt.shape[0]
    states = a_log.shape[1]
    channels = w_in_x.shape[1]
    halo = (taps - 1) * seqs

    per = channels // count
    fields = [w_xproj, w_dt.T, a_log, conv_w.T, conv_b[:, None], dt_bias[:, None], d_skip[:, None]]
    starts = [0]
    for field in fields:
        starts.append(starts[-1] + field.shape[1])
    pack_width = -(-starts[-1] // LANES) * LANES
    gains = [norm1_gain, norm2_gain, ssm_gain]
    gain_starts = [0]
    for gain in gains:
        gain_starts.append(gain_starts[-1] + gain.shape[0])
    pack_rows = -(-(per + -(-gain_starts[-1] // pack_width)) // 16) * 16

    def pack(channel_fields, gain_fields):
        table = jnp.concatenate([f.astype(F32) for f in channel_fields], axis=1)
        table = jnp.pad(table, ((0, 0), (0, pack_width - table.shape[1])))
        table = table.reshape(-1, per, pack_width)
        rest = jnp.concatenate([g.astype(F32).reshape(table.shape[0], -1) for g in gain_fields], 1)
        rest = jnp.pad(rest, ((0, 0), (0, (pack_rows - per) * pack_width - rest.shape[1])))
        return jnp.concatenate([table, rest.reshape(-1, pack_rows - per, pack_width)], axis=1)

    def unpack(block):
        table = block[:, :per].reshape(-1, pack_width)
        rest = block[:, per:].reshape(block.shape[0], -1)
        return (
            [table[:, starts[k] : starts[k + 1]] for k in range(len(fields))],
            [rest[:, gain_starts[k] : gain_starts[k + 1]].reshape(-1) for k in range(len(gains))],
        )

    in_x_blocks, pack_blocks, x_low, grad_low = first_gather(
        [w_in_x.astype(BF), pack(fields, gains)[0].astype(BF)], [x_in, d_out]
    )
    fulls, full_gains = unpack(pack_blocks)
    full_xproj, w_dt_cols, full_a_log, conv_cols, conv_b_col, bias_col, skip_col = fulls
    full_w_dt = w_dt_cols.T
    full_conv_w = conv_cols.T
    full_conv_b, full_dt_bias, full_d_skip = conv_b_col[:, 0], bias_col[:, 0], skip_col[:, 0]
    full_norm1, full_norm2, full_ssm_gain = full_gains

    w_mix = jnp.concatenate([w_in_z.astype(BF), w_out.astype(BF).T], axis=1)
    w_mix, in_x_blocks = lax.optimization_barrier((w_mix, in_x_blocks))
    full_in_x = in_x_blocks.reshape(width, channels)
    full_mix = lax.all_gather(w_mix, "seq", axis=0, tiled=True)

    norm1_vec = full_norm1.astype(F32)
    x_rows = x_low.astype(F32)
    ids = seg_ids.T.reshape(rows)
    normed1, scale_one = norm_rows(x_rows, norm1_vec)
    x_norm = normed1.astype(BF)
    x_inner = jnp.dot(x_norm, full_in_x, preferred_element_type=F32).astype(BF)
    prev_tail, prev_ids = shifted((x_inner[rows - halo :], ids[rows - halo :]), "seq", 1)
    extended = jnp.concatenate([prev_tail, x_inner], axis=0).astype(F32)
    ext_ids = jnp.concatenate([prev_ids, ids])
    conv_weight = full_conv_w.astype(F32)
    x_conv = full_conv_b.astype(F32)[None, :]
    same_docs = []
    for offset in range(taps):
        first = (taps - 1 - offset) * seqs
        same = (ext_ids[first : first + rows] == ids).astype(F32)[:, None]
        same_docs.append(same)
        x_conv = x_conv + conv_weight[offset] * extended[first : first + rows] * same
    u_low = jax.nn.silu(x_conv).astype(BF)
    projected = head_total(jnp.dot(u_low, full_xproj, preferred_element_type=F32), BF)
    ssm_vec = full_ssm_gain.astype(F32)
    b_end = rank + states
    dt_normed, dt_scale = norm_rows(projected[:, :rank], ssm_vec[:rank])
    b_normed, b_scale = norm_rows(projected[:, rank:b_end], ssm_vec[rank:b_end])
    c_normed, c_scale = norm_rows(projected[:, b_end:], ssm_vec[b_end:])
    dt_low = dt_normed.astype(BF)
    dt_pre = jnp.dot(dt_low, full_w_dt, preferred_element_type=F32) + full_dt_bias.astype(F32)
    step = jax.nn.softplus(dt_pre)
    rates = -jnp.exp(full_a_log.astype(F32))
    rate_rows = jnp.repeat((rates * LOG2E).T, seqs, axis=0)
    bc = jnp.concatenate([b_normed, c_normed], axis=1)
    part_one = bc.astype(BF)
    part_two = (bc - part_one.astype(F32)).astype(BF)
    part_three = (bc - part_one.astype(F32) - part_two.astype(F32)).astype(BF)
    stops = ((1.0 - same_docs[1]) * STOP).astype(BF)
    masks = [same.astype(BF) for same in same_docs[1:]]
    spare = jnp.zeros((rows, LANES - 6 * states - taps), BF)
    parts = jnp.concatenate([part_one, part_two, part_three, stops] + masks + [spare], axis=1)
    shape = jax.ShapeDtypeStruct
    state_rows = states * seqs
    start, step_sum = state_call(
        entry_kernel,
        1,
        seqs,
        states,
        2 * states + 2,
        [parts, step, u_low, rate_rows],
        [shape((state_rows, channels), F32), shape((seqs, channels), F32)],
        exchange_scratch(count, seqs, states, channels),
        6,
        (0, 0),
    )
    start, full_mix = lax.optimization_barrier((start, full_mix))
    mix_blocks = full_mix.reshape(count, -1, full_mix.shape[1])
    w_gate_low = w_gate.astype(BF)
    y_state, gate_blocks = state_call(
        forward_kernel,
        2,
        seqs,
        states,
        2 * states + 2,
        [parts, step, u_low, rate_rows, start, w_gate_low],
        [shape((rows, channels), F32), shape((count,) + w_gate.shape, BF)],
        gather_sems(count // 2, w_gate.shape[1]),
        8,
        (1, 1),
    )
    full_in_z = full_mix[:, :channels]
    z_gate = jnp.dot(x_norm, full_in_z, preferred_element_type=F32)
    skip_vec = full_d_skip.astype(F32)
    u_rows = u_low.astype(F32)
    y_full = y_state + skip_vec * u_rows
    silu_z = jax.nn.silu(z_gate)
    g_low = (y_full * silu_z).astype(BF)
    hidden, x_norm2, act_low, d_gate, d_up, norm2_sums, ffn_part, d_hidden, d_mix = ffn_call(
        g_low,
        mix_blocks,
        x_low,
        full_norm2.astype(F32)[None, :],
        grad_low,
        gate_blocks,
        w_up.astype(BF),
        w_down.astype(BF).T,
    )
    grad_norm2 = norm2_sums[0]
    grad_out_w = jnp.einsum("rd,re->de", d_mix, g_low, preferred_element_type=F32)
    full_out_t = full_mix[:, channels:]
    d_g = jnp.dot(d_mix, full_out_t, preferred_element_type=F32)
    d_y = d_g * silu_z
    d_z = (d_g * y_full * silu_slope(z_gate)).astype(BF)
    grad_skip = jnp.sum(d_y * u_rows, axis=0)
    grad_block = shape((count // 2, 2, width // count, w_gate.shape[1]), BF)
    down_moved = moved_shapes([grad_block])
    fetched = [ffn_part, grad_low, act_low, x_norm2, d_gate, d_up, hidden]
    last, grad_down, grad_gate, grad_up, block_out, *down_moved = state_call(
        adjoint_kernel,
        3,
        seqs,
        states,
        states + 2,
        [parts, step, d_y, rate_rows, step_sum] + fetched,
        [shape((state_rows, channels), F32)]
        + [grad_block] * 3
        + [shape(x_in.shape, BF)]
        + down_moved,
        exchange_scratch(count, seqs, states, channels)
        + sum_scratch(rows, width, False)
        + [kept_scratch(rows, width), pltpu.VMEM((rows, width), BF)]
        + [pltpu.VMEM((width // LANES, rows // CHUNKS, LANES), F32), SUM_SEMS]
        + fetch_scratch(fetched)
        + scatter_scratch(count, [grad_block]),
        6,
        (7, 2),
    )
    grad_in_z = jnp.einsum("rd,re->de", x_norm, d_z, preferred_element_type=F32)
    big_grads = [grad_gate, grad_up]
    big_grads += [owner_blocks(grad.astype(BF)) for grad in (grad_out_w, grad_in_z)]
    padded = lambda value: jnp.pad(value, ((0, 0), (0, LANES - value.shape[1])))
    taps_table = jnp.concatenate([conv_weight, skip_vec[None, :]], axis=0)
    taps_table = jnp.pad(taps_table, ((0, 2 * taps - taps_table.shape[0]), (0, 0)))
    big_ins = [x_conv, extended.reshape(-1, seqs, channels), projected] + big_grads
    block_rows_moved = moved_shapes(big_grads)
    bf_rows = pltpu.VMEM((4 * seqs, channels), BF)
    d_inner_low, ssm_sums, grad_xproj, grad_step_t, d_log, column_sums, *first_moved = state_call(
        backward_kernel,
        4,
        seqs,
        states,
        2 * states + 2,
        [parts, step, u_low, d_y, rate_rows, start, last, padded(dt_low)]
        + [padded(w_dt_cols), full_xproj, ssm_vec[None, :], taps_table]
        + big_ins,
        [
            shape((rows, channels), BF),
            shape((8, LANES), F32),
            shape((channels, LANES), F32),
            shape((channels, LANES), F32),
            shape((states, channels), F32),
            shape(((taps + 2) * seqs, channels), F32),
        ]
        + block_rows_moved,
        [
            pltpu.VMEM(((tokens + 1) * states, seqs, LANES), F32),
            pltpu.VMEM((rows, 2 * states * LANES), F32),
            pltpu.VMEM((rows, channels), F32),
            pltpu.VMEM((rows, channels), BF),
            pltpu.VMEM((2, rows, LANES), BF),
            pltpu.VMEM((2, rows, LANES), BF),
            pltpu.VMEM((4 * seqs, channels), F32),
            bf_rows,
            bf_rows,
            pltpu.SemaphoreType.DMA((2, 2)),
            pltpu.SemaphoreType.DMA((2,)),
            pltpu.SemaphoreType.DMA((channels // LANES + 2,)),
        ]
        + scatter_scratch(count, big_grads),
        30,
        (len(big_ins), len(block_rows_moved)),
    )
    grad_alog = d_log.T * rates
    columns = jnp.sum(column_sums.reshape(taps + 2, seqs, channels), axis=1)
    grad_ssm = ssm_sums[0]
    grad_ssm = grad_ssm * (lax.axis_index("head") == 0).astype(F32)
    small = pack(
        [
            grad_xproj,
            grad_step_t[:, :rank],
            grad_alog,
            columns[:taps].T,
            columns[taps][:, None],
            columns[taps + 1][:, None],
            grad_skip[:, None],
        ],
        [jnp.zeros_like(grad_norm2), grad_norm2, grad_ssm],
    )
    small = owner_blocks(small.reshape(-1, pack_width))
    kinds = len(big_grads)
    grad_input, norm1_sums, *owns, pack_given, pack_came = input_call(
        d_inner_low,
        d_z,
        in_x_blocks,
        mix_blocks,
        x_low,
        x_norm,
        norm1_vec[None, :],
        d_hidden,
        small,
        (
            [grad_down] + big_grads,
            down_moved[:1] + first_moved[:kinds],
            down_moved[1:] + first_moved[kinds:],
        ),
        x_in.shape,
    )
    own_down, own_gate, own_up, own_out, own_in_z, own_in_x = owns
    small = scatter_own(small, pack_given, pack_came)
    own_norm1 = lax.dynamic_slice_in_dim(norm1_sums[0], place * (width // count), width // count)
    small = jnp.concatenate([small[:per], head_total(small[per:], F32)])[None]
    small_fields, small_gains = unpack(small)
    return (
        block_out,
        grad_input,
        own_norm1,
        own_in_x,
        own_in_z,
        small_fields[3].T,
        small_fields[4][:, 0],
        small_fields[0],
        small_gains[2],
        small_fields[1].T,
        small_fields[5][:, 0],
        small_fields[2],
        small_fields[6][:, 0],
        own_out.T,
        small_gains[1],
        own_gate,
        own_up,
        own_down.T,
    )


def solution(mesh):
    placed = (
        P(None, "seq", None),
        P(None, "seq"),
        P("seq"),
        P("seq", "head"),
        P("seq", "head"),
        P(None, ("head", "seq")),
        P(("head", "seq")),
        P(("head", "seq"), None),
        P("seq"),
        P(None, ("head", "seq")),
        P(("head", "seq")),
        P(("head", "seq"), None),
        P(("head", "seq")),
        P("head", "seq"),
        P("seq"),
        P("seq", "head"),
        P("seq", "head"),
        P("head", "seq"),
        P(None, "seq", None),
    )
    return jax.shard_map(
        shards,
        mesh=mesh,
        in_specs=placed,
        out_specs=(
            P(None, "seq", None),
            P(None, "seq", None),
            P("seq"),
            P("seq", "head"),
            P("seq", "head"),
            P(None, ("head", "seq")),
            P(("head", "seq")),
            P(("head", "seq"), None),
            P("seq"),
            P(None, ("head", "seq")),
            P(("head", "seq")),
            P(("head", "seq"), None),
            P(("head", "seq")),
            P("head", "seq"),
            P("seq"),
            P("seq", "head"),
            P("seq", "head"),
            P("head", "seq"),
        ),
        check_vma=False,
    )
```

```python
import functools

import jax
import jax.numpy as jnp
from jax import lax
from jax.experimental import pallas as pl
from jax.experimental.pallas import tpu as pltpu
from jax.sharding import PartitionSpec as P

EPS = 1e-06
LOG2E = 1.4426950408889634
LN2 = 0.6931471805599453
STOP = 1e30
LANES = 128
BF = jnp.bfloat16
F32 = jnp.float32


def shifted(value, axis, steps):
    count = lax.axis_size(axis)
    initial, last = (max(0, -steps), min(count, count - steps))
    return lax.ppermute(value, axis, [(source, source + steps) for source in range(initial, last)])


def norm_rows(values, gain_vec):
    inv_rms = lax.rsqrt(jnp.mean(values * values, axis=-1, keepdims=True) + EPS)
    return (values * inv_rms * gain_vec, inv_rms)


def norm_back(values, inv_rms, gain_vec, grad_rows):
    normed = values * inv_rms
    gain_grad = jnp.sum(grad_rows * normed, axis=0)
    scaled = grad_rows * gain_vec
    value_grad = inv_rms * (scaled - normed * jnp.mean(scaled * normed, axis=-1, keepdims=True))
    return (value_grad, gain_grad)


def silu_slope(values):
    logistic = jax.nn.sigmoid(values)
    return logistic * (1.0 + values * (1.0 - logistic))


GROUP = 4


def at_rows(index, size):
    return pl.ds(pl.multiple_of(index * size, size), size)


def spread(parts_ref, states, target, first=0):
    rows = parts_ref.shape[0]
    wide = 2 * LANES
    chunk = 256 if rows % 256 == 0 else rows
    source = lax.broadcasted_iota(jnp.int32, (LANES, wide), 0)
    half = lax.broadcasted_iota(jnp.int32, (LANES, wide), 1) // LANES
    columns = 2 * states

    def one(pair, carry):
        column = pair * 2 + half
        third = source % columns == column
        hot = jnp.where((source < 3 * columns) & third, 1.0, 0.0)
        stop = (column == columns) & (source == 3 * columns)
        hot = jnp.where(stop, 1.0, hot).astype(BF)
        for k in range(rows // chunk):
            target[pl.ds(k * chunk, chunk), at_rows(pair - first, wide)] = jnp.dot(
                parts_ref[pl.ds(k * chunk, chunk), :], hot, preferred_element_type=F32
            )
        return carry

    lax.fori_loop(first, states + 1, one, 0)


def group_tokens(ref, group, lanes, seqs):
    both = ref[at_rows(group, GROUP * seqs), lanes].astype(F32)
    return [both[k * seqs : (k + 1) * seqs] for k in range(GROUP)]


class Exchange:
    def __init__(self, count, forward, arrays, sems):
        place = lax.axis_index("seq")
        self.around = count // 2
        self.low, self.high = lax.rem(place, 2), place // 2
        self.place = place
        self.forward = forward
        self.arrays = arrays
        self.sems = sems
        self.mate = self.high * 2 + 1 - self.low

    def copies(self, steps, tile, source, device, kind):
        send, recv = self.sems[2 * kind], self.sems[2 * kind + 1]
        lanes = at_rows(tile, LANES)
        return [
            pltpu.make_async_remote_copy(
                src_ref=array.at[source, :, lanes],
                dst_ref=array.at[source, :, lanes],
                send_sem=send.at[k, steps, tile],
                recv_sem=recv.at[k, steps, tile],
                device_id={"seq": device},
                device_id_type=pl.DeviceIdType.MESH,
            )
            for k, array in enumerate(self.arrays)
        ]

    def away(self, steps):
        return self.high + steps if self.forward else self.high - steps

    def inside(self, pair):
        return pair < self.around if self.forward else pair >= 0

    def behind(self, steps):
        return self.high - steps if self.forward else self.high + steps

    def has_behind(self, steps):
        pair = self.behind(steps)
        return pair >= 0 if self.forward else pair < self.around

    def gives(self):
        return self.low == (0 if self.forward else 1)

    def hop(self, steps, tile):
        pair = jnp.clip(self.away(steps), 0, self.around - 1)
        return self.copies(steps, tile, self.place, pair * 2 + self.low, 0)

    def relay(self, steps, tile):
        pair = jnp.clip(self.behind(steps), 0, self.around - 1)
        return self.copies(steps, tile, pair * 2 + self.low, self.mate, 1)

    def start(self, tile):
        for steps in range(1, self.around):

            @pl.when(self.inside(self.away(steps)))
            def _():
                for copy in self.hop(steps, tile):
                    copy.start()

        @pl.when(self.gives())
        def _():
            for copy in self.relay(0, tile):
                copy.start()

    def pass_on(self, tile):
        for steps in range(1, self.around):

            @pl.when(self.has_behind(steps))
            def _():
                for copy in self.hop(steps, tile):
                    copy.wait_recv()
                for copy in self.relay(steps, tile):
                    copy.start()

    def arrive(self, tile):
        @pl.when(jnp.logical_not(self.gives()))
        def _():
            for copy in self.relay(0, tile):
                copy.wait_recv()

        for steps in range(1, self.around):

            @pl.when(self.has_behind(steps))
            def _():
                for copy in self.relay(steps, tile):
                    copy.wait_recv()

    def finish(self, tile):
        @pl.when(self.gives())
        def _():
            for copy in self.relay(0, tile):
                copy.wait_send()

        for steps in range(1, self.around):

            @pl.when(self.inside(self.away(steps)))
            def _():
                for copy in self.hop(steps, tile):
                    copy.wait_send()

            @pl.when(self.has_behind(steps))
            def _():
                for copy in self.relay(steps, tile):
                    copy.wait_send()


def chained(state, block_ref, sums_ref, rate_ref, source, lanes, seqs):
    total = sums_ref[source, :, lanes]
    block = block_ref[source, :, lanes].astype(F32)
    after = []
    for n in range(len(state)):
        decay = jnp.exp2(total * rate_ref[pl.ds(n * seqs, seqs), lanes])
        after.append(decay * state[n] + block[n * seqs : (n + 1) * seqs])
    return tuple(after)


def state_blocks(ref, lanes, seqs, states):
    return tuple(ref[pl.ds(n * seqs, seqs), lanes] for n in range(states))


def put_blocks(ref, lead, lanes, blocks):
    stacked = jnp.concatenate(blocks, axis=0)
    if lead is None:
        ref[:, lanes] = stacked.astype(ref.dtype)
    else:
        ref[lead, :, lanes] = stacked.astype(ref.dtype)


def entry_kernel(
    count, seqs, states, parts_ref, step_ref, u_ref, rate_ref, start_ref, sum_ref, *scratch
):
    spread_ref, ends, sums, *sems = scratch
    rows, channels = step_ref.shape
    tokens, tiles = rows // seqs, channels // LANES
    stop_lanes = pl.ds(2 * states * LANES, LANES)
    exchange = Exchange(count, True, (ends, sums), sems)
    place = exchange.place
    zero = jnp.zeros((seqs, LANES), F32)
    greet_pairs(count)
    spread(parts_ref, states, spread_ref)

    def local(tile, carry):
        lanes = at_rows(tile, LANES)

        def one(group, carry):
            state, total = carry
            us = group_tokens(u_ref, group, lanes, seqs)
            for k in range(GROUP):
                here = at_rows(group * GROUP + k, seqs)
                step = step_ref[here, lanes]
                drive = step * us[k]
                stop = step + spread_ref[here, stop_lanes]
                total = total + stop
                fresh = []
                for n in range(states):
                    decay = jnp.exp2(stop * rate_ref[pl.ds(n * seqs, seqs), lanes])
                    b_one = spread_ref[here, pl.ds(n * LANES, LANES)]
                    fresh.append(decay * state[n] + drive * b_one)
                state = tuple(fresh)
            return state, total

        state, total = lax.fori_loop(0, tokens // GROUP, one, ((zero,) * states, zero))
        put_blocks(ends, place, lanes, state)
        sums[place, :, lanes] = total
        exchange.start(tile)
        return carry

    lax.fori_loop(0, tiles, local, 0)
    finish_exchange(exchange, tiles, lambda first, lanes: lax.fori_loop(
        0,
        place,
        lambda source, state: chained(state, ends, sums, rate_ref, source, lanes, seqs),
        first,
    ), start_ref, states, zero)
    sum_ref[...] = sums[place]


def finish_exchange(exchange, tiles, chain, target_ref, states, zero, relay=True):
    def pass_on(tile, carry):
        exchange.pass_on(tile)
        return carry

    if relay:
        lax.fori_loop(0, tiles, pass_on, 0)

    def take(tile, carry):
        lanes = at_rows(tile, LANES)
        exchange.arrive(tile)
        put_blocks(target_ref, None, lanes, chain((zero,) * states, lanes))
        return carry

    lax.fori_loop(0, tiles, take, 0)

    def finish(tile, carry):
        exchange.finish(tile)
        return carry

    lax.fori_loop(0, tiles, finish, 0)


def forward_kernel(
    count,
    seqs,
    states,
    parts_ref,
    step_ref,
    u_ref,
    rate_ref,
    start_ref,
    block_ref,
    y_ref,
    gathered_ref,
    *scratch,
):
    spread_ref, *sems = scratch
    gather = BlockGather(count, block_ref, gathered_ref, sems)
    rows, channels = step_ref.shape
    tokens, tiles = rows // seqs, channels // LANES
    stop_lanes = pl.ds(2 * states * LANES, LANES)
    zero = jnp.zeros((seqs, LANES), F32)
    greet_pairs(count)
    gather.start()
    spread(parts_ref, states, spread_ref)

    def whole(tile, carry):
        lanes = at_rows(tile, LANES)

        def one(group, state):
            us = group_tokens(u_ref, group, lanes, seqs)
            for k in range(GROUP):
                here = at_rows(group * GROUP + k, seqs)
                step = step_ref[here, lanes]
                drive = step * us[k]
                stop = step + spread_ref[here, stop_lanes]
                fresh = []
                out = zero
                for n in range(states):
                    decay = jnp.exp2(stop * rate_ref[pl.ds(n * seqs, seqs), lanes])
                    b_one = spread_ref[here, pl.ds(n * LANES, LANES)]
                    value = decay * state[n] + drive * b_one
                    out = out + value * spread_ref[here, pl.ds((states + n) * LANES, LANES)]
                    fresh.append(value)
                y_ref[here, lanes] = out
                state = tuple(fresh)
            return state

        lax.fori_loop(0, tokens // GROUP, one, state_blocks(start_ref, lanes, seqs, states))
        for piece in range(gather.pieces):
            if 2 * piece + 1 < tiles:

                @pl.when(tile == 2 * piece + 1)
                def _():
                    gather.relay(piece)

        return carry

    lax.fori_loop(0, tiles, whole, 0)
    for piece in range(gather.pieces):
        if 2 * piece + 1 >= tiles:
            gather.relay(piece)
    gather.finish()


def adjoint_kernel(
    count,
    seqs,
    states,
    parts_ref,
    step_ref,
    dy_ref,
    rate_ref,
    sum_ref,
    *refs,
):
    sources, refs = refs[:7], refs[7:]
    last_ref, gdown_ref, ggate_ref, gup_ref, out_ref, given_ref, came_ref, *scratch = refs
    spread_ref, ends, sums, *scratch = scratch
    sems, scratch = scratch[:4], scratch[4:]
    half, give, take, kept, block_ref, buffer, sum_sems, *scratch = scratch
    targets, fetch_sems, scratch = scratch[:7], scratch[7], scratch[8:]
    fetch = Fetch(sources, targets, fetch_sems)
    part_ref, low_ref, act_ref, norm_ref, dgate_ref, dup_ref, hidden_ref = targets
    fetch.start()
    scatter = PairScatter(count, [gdown_ref], [given_ref], [came_ref], scratch)
    total = HeadSum(part_ref, half, give, take, block_ref, sum_sems)
    chunks = kept.shape[0]
    quarter = kept.shape[1]
    rows, channels = step_ref.shape
    tokens, tiles = rows // seqs, channels // LANES
    groups = tokens // GROUP
    stop_lanes = pl.ds(states * LANES, LANES)
    exchange = Exchange(count, False, (ends, sums), sems)
    place = exchange.place
    zero = jnp.zeros((seqs, LANES), F32)
    greet_pairs(count, True)
    spread(parts_ref, states, spread_ref, states // 2)

    def own(tile, carry):
        lanes = at_rows(tile, LANES)

        def one(back, grads):
            group = groups - 1 - back
            for k in reversed(range(GROUP)):
                here = at_rows(group * GROUP + k, seqs)
                stop = step_ref[here, lanes] + spread_ref[here, stop_lanes]
                dy = dy_ref[here, lanes]
                fresh = []
                for n in range(states):
                    decay = jnp.exp2(stop * rate_ref[pl.ds(n * seqs, seqs), lanes])
                    c_one = spread_ref[here, pl.ds(n * LANES, LANES)]
                    fresh.append(decay * (grads[n] + dy * c_one))
                grads = tuple(fresh)
            return grads

        put_blocks(ends, place, lanes, lax.fori_loop(0, groups, one, (zero,) * states))
        sums[place, :, lanes] = sum_ref[:, lanes]
        exchange.start(tile)
        return carry

    lax.fori_loop(0, tiles, own, 0)
    fetch.wait(0, 1, 2, 3, 4, 5, 6)
    for chunk in range(chunks):
        total.near_copy(chunk).start()
    around, _, shard, units = gdown_ref.shape
    together = max(1, 384 // (2 * shard))
    wide = together * 2 * shard

    def place_of(block):
        return pl.ds(block * wide, wide), pl.ds(block * together, together)

    def multiply(block):
        lanes, pairs = place_of(block)
        mine = norm_ref[:, lanes].T
        for d_ref, grad_ref in ((dgate_ref, ggate_ref), (dup_ref, gup_ref)):
            grad = jnp.dot(mine, d_ref[...], preferred_element_type=F32).astype(BF)
            grad_ref[pairs] = grad.reshape(together, 2, shard, units)

    blocks = list(range(around // together))
    for block in blocks:
        lanes, pairs = place_of(block)
        grad = jnp.dot(low_ref[:, lanes].T, act_ref[...], preferred_element_type=F32).astype(BF)
        gdown_ref[pairs] = grad.reshape(together, 2, shard, units)

    for chunk in range(chunks):
        total.fold(chunk, kept)

    def pass_on(tile, carry):
        exchange.pass_on(tile)
        return carry

    lax.fori_loop(0, tiles, pass_on, 0)
    scatter.start()

    def bring(chunk, carry):
        total.far_copy(chunk).wait_recv()
        here = at_rows(chunk, quarter)
        rows_out = hidden_ref[here, :] + kept[chunk] + take[chunk].astype(F32)
        block_ref[total.own_rows(chunk), :] = rows_out.astype(BF)
        total.far_back(chunk).start()
        return carry

    lax.fori_loop(0, chunks, bring, 0)
    for block in blocks[:2]:
        multiply(block)
    scatter.advance(0)
    for block in blocks[2:]:
        multiply(block)
    scatter.advance(1)
    finish_exchange(exchange, tiles, lambda first, lanes: lax.fori_loop(
        0,
        count - 1 - place,
        lambda hop, state: chained(state, ends, sums, rate_ref, count - 1 - hop, lanes, seqs),
        first,
    ), last_ref, states, zero, False)
    scatter.advance(2)

    def spread_out(chunk, carry):
        total.far_back(chunk).wait_recv()
        total.near_back(chunk).start()
        return carry

    lax.fori_loop(0, chunks, spread_out, 0)
    for moment in range(3, scatter.turns):
        scatter.advance(moment)

    def finish(chunk, carry):
        total.near_back(chunk).wait_recv()
        put_sequences(out_ref, block_ref, chunk, 4 * quarter, buffer)
        total.finish(chunk)
        return carry

    lax.fori_loop(0, chunks, finish, 0)
    scatter.finish()


def backward_kernel(
    count,
    seqs,
    states,
    parts_ref,
    step_ref,
    u_ref,
    dy_ref,
    rate_ref,
    start_ref,
    last_ref,
    *refs,
):
    kinds = (len(refs) - 35) // 3
    dtlow_ref, wdt_ref, xproj_ref, gain_ref, taps_ref, *refs = refs
    xconv_ref, ext_ref, proj_ref, *refs = refs
    grad_refs, refs = refs[:kinds], refs[kinds:]
    inner_ref, ssm_ref, gx_ref, gw_ref, dlog_ref, sums_ref, *refs = refs
    given_refs, came_refs, scratch = refs[:kinds], refs[kinds : 2 * kinds], refs[2 * kinds :]
    spread_ref, held, acc, du_ref, dpre_ref, *scratch = scratch
    sent, got, tail, edge, from_next, head_sems, edge_sems, load_sems, *scratch = scratch
    rows, channels = step_ref.shape
    tokens, tiles = rows // seqs, channels // LANES
    groups = tokens // GROUP
    stop_lanes = pl.ds(2 * states * LANES, LANES)
    place = lax.axis_index("seq")
    low, high = lax.rem(place, 2), place // 2
    zero = jnp.zeros((seqs, LANES), F32)
    greet_pairs(count, True, True)
    scatter = PairScatter(count, grad_refs, given_refs, came_refs, scratch)
    scatter.start()
    spread(parts_ref, states, spread_ref)

    def clear(row, carry):
        acc[at_rows(row, seqs), :] = jnp.zeros((seqs, acc.shape[1]), F32)
        return carry

    lax.fori_loop(0, tokens, clear, 0)

    def whole(tile, carry):
        lanes = at_rows(tile, LANES)

        def again(group, state):
            us = group_tokens(u_ref, group, lanes, seqs)
            for k in range(GROUP):
                token = group * GROUP + k
                here = at_rows(token, seqs)
                step = step_ref[here, lanes]
                drive = step * us[k]
                stop = step + spread_ref[here, stop_lanes]
                fresh = []
                for n in range(states):
                    held[token * states + n] = state[n]
                    decay = jnp.exp2(stop * rate_ref[pl.ds(n * seqs, seqs), lanes])
                    b_one = spread_ref[here, pl.ds(n * LANES, LANES)]
                    fresh.append(decay * state[n] + drive * b_one)
                state = tuple(fresh)
            return state

        state = lax.fori_loop(0, groups, again, state_blocks(start_ref, lanes, seqs, states))
        for n in range(states):
            held[tokens * states + n] = state[n]
        grads = state_blocks(last_ref, lanes, seqs, states)

        def one(back, carry):
            grads, logs, bias = carry
            group = groups - 1 - back
            us = group_tokens(u_ref, group, lanes, seqs)
            pres = [None] * GROUP
            for k in reversed(range(GROUP)):
                token = group * GROUP + k
                here = at_rows(token, seqs)
                step = step_ref[here, lanes]
                dy = dy_ref[here, lanes]
                drive = step * us[k]
                stop = step + spread_ref[here, stop_lanes]
                fresh, fresh_logs = [], []
                on_b, on_rate = zero, zero
                for n in range(states):
                    at = token * states + n
                    on_lanes = pl.ds(n * LANES, LANES)
                    other_lanes = pl.ds((states + n) * LANES, LANES)
                    rate = rate_ref[pl.ds(n * seqs, seqs), lanes]
                    decay = jnp.exp2(stop * rate)
                    lam = grads[n] + dy * spread_ref[here, other_lanes]
                    carried = lam * decay
                    fresh.append(carried)
                    kept = carried * held[at]
                    on_b = on_b + lam * spread_ref[here, on_lanes]
                    on_rate = on_rate + kept * rate
                    fresh_logs.append(logs[n] + kept * step)
                    acc[here, on_lanes] = acc[here, on_lanes] + lam * drive
                    acc[here, other_lanes] = acc[here, other_lanes] + dy * held[at + states]
                du_ref[here, lanes] = step * on_b
                series = step * (1.0 - step * (0.5 - step * (1.0 / 6.0 - step * (1.0 / 24.0))))
                slope = jnp.where(step < 0.05, series, 1.0 - jnp.exp2(step * (-LOG2E)))
                pres[k] = (on_rate * LN2 + us[k] * on_b) * slope
                bias = bias + pres[k]
                grads, logs = tuple(fresh), tuple(fresh_logs)
            dpre_ref[at_rows(group, GROUP * seqs), lanes] = jnp.concatenate(pres, 0).astype(BF)
            return grads, logs, bias

        grads, logs, bias = lax.fori_loop(0, groups, one, (grads, (zero,) * states, zero))
        dlog_ref[:, lanes] = jnp.concatenate(
            [jnp.sum(log, axis=0, keepdims=True) for log in logs], axis=0
        )
        sums_ref[pl.ds(5 * seqs, seqs), lanes] = bias
        for k in range(tiles):

            @pl.when(tile == k)
            def _():
                scatter.advance(k)

        return carry

    lax.fori_loop(0, tiles, whole, 0)

    wide = 2 * LANES
    chunk = 256 if rows % 256 == 0 else rows
    target = lax.broadcasted_iota(jnp.int32, (wide, LANES), 1)
    half = lax.broadcasted_iota(jnp.int32, (wide, LANES), 0) // LANES
    past = taps_ref.shape[0] // 2 - 1
    dbc_ref = spread_ref.at[:, pl.ds((past + 2) * LANES, LANES)]
    dbc_ref[...] = jnp.zeros((rows, LANES), F32)

    def reduce(pair, carry):
        hot = jnp.where(target == LANES - 2 * states + pair * 2 + half, 1.0, 0.0).astype(BF)
        for k in range(rows // chunk):
            here = pl.ds(k * chunk, chunk)
            values = acc[here, at_rows(pair, wide)]
            main = values.astype(BF)
            rest = (values - main.astype(F32)).astype(BF)
            dbc_ref[here, :] += jnp.dot(main, hot, preferred_element_type=F32) + jnp.dot(
                rest, hot, preferred_element_type=F32
            )
        return carry

    lax.fori_loop(0, states, reduce, 0)

    scatter.advance(tiles)

    span = tokens + past
    value_at = tiles * span
    tap_at = [value_at + k * span for k in range(past + 1)]
    proj_lanes = pl.ds((past + 1) * LANES, LANES)
    loads = [
        pltpu.make_async_copy(xconv_ref, acc.at[:, pl.ds(0, channels)], load_sems.at[tiles]),
        pltpu.make_async_copy(proj_ref, spread_ref.at[:, proj_lanes], load_sems.at[tiles + 1]),
    ]
    for tile in range(tiles):
        source = ext_ref.at[:, :, pl.ds(tile * LANES, LANES)]
        target_tiles = held.at[pl.ds(tile * span, span)]
        loads.append(pltpu.make_async_copy(source, target_tiles, load_sems.at[tile]))
    for load in loads:
        load.start()
    head = lax.axis_index("head")
    near = {"head": head // 2 * 2 + 1 - lax.rem(head, 2)}
    far = {"head": lax.rem(head + 2, 4)}
    trade = [
        pltpu.make_async_remote_copy(
            src_ref=sent.at[k],
            dst_ref=got.at[k],
            send_sem=head_sems.at[0, k],
            recv_sem=head_sems.at[1, k],
            device_id=device,
            device_id_type=pl.DeviceIdType.MESH,
        )
        for k, device in enumerate((near, far))
    ]
    for k in range(rows // chunk):
        here = pl.ds(k * chunk, chunk)
        stats = jnp.dot(dpre_ref[here, :], wdt_ref[...], preferred_element_type=F32)
        sent[0, here, :] = (dbc_ref[here, :] + stats).astype(BF)
    trade[0].start()

    source = lax.broadcasted_iota(jnp.int32, (LANES, LANES), 0)
    for k in range(1, past + 1):
        hot = jnp.where(source == 6 * states + k, 1.0, 0.0).astype(BF)
        for m in range(rows // chunk):
            here = pl.ds(m * chunk, chunk)
            spread_ref[here, pl.ds(k * LANES, LANES)] = jnp.dot(
                parts_ref[here, :], hot, preferred_element_type=F32
            )
    scatter.advance(tiles + 1)
    trade[0].wait_recv()
    for k in range(rows // chunk):
        here = pl.ds(k * chunk, chunk)
        sent[1, here, :] = (sent[0, here, :].astype(F32) + got[0, here, :].astype(F32)).astype(BF)
    trade[1].start()

    def step_weights(tile, carry):
        lanes = at_rows(tile, LANES)
        gw_ref[lanes, :] = jnp.dot(
            dpre_ref[:, lanes].T, dtlow_ref[...], preferred_element_type=F32
        )
        return carry

    lax.fori_loop(0, tiles, step_weights, 0)
    scatter.advance(tiles + 2)
    trade[0].wait_send()
    for load in loads:
        load.wait()
    trade[1].wait_recv()
    ssm_ref[...] = jnp.zeros(ssm_ref.shape, F32)
    for k in range(rows // chunk):
        here = pl.ds(k * chunk, chunk)
        stats = sent[1, here, :].astype(F32) + got[1, here, :].astype(F32)
        d_proj, gain_rows = stats_back(stats, spread_ref[here, proj_lanes], gain_ref[...], states)
        sent[0, here, :] = d_proj.astype(BF)
        share = jnp.sum(gain_rows, axis=0, keepdims=True)
        ssm_ref[...] += jnp.broadcast_to(share, ssm_ref.shape)
    block = 16
    size = block * seqs
    edge[...] = jnp.zeros(edge.shape, BF)

    def convolve(tile, carry):
        lanes = at_rows(tile, LANES)
        gx_ref[lanes, :] = jnp.dot(u_ref[:, lanes].T, sent[0], preferred_element_type=F32)
        weights = xproj_ref[lanes, :]
        skip = taps_ref[pl.ds(past + 1, 1), lanes]
        ext_at = tile * span

        def one(part, sums):
            here = at_rows(part, size)
            token = part * block
            d_u = du_ref[here, lanes] + dy_ref[here, lanes] * skip
            d_u = d_u + transposed_dot(sent[0, here, :], weights)
            conv = acc[here, lanes]
            logistic = 1.0 / (1.0 + jnp.exp(-conv))
            d_conv = d_u * logistic * (1.0 + conv * (1.0 - logistic))
            fresh = []
            for k in range(past + 1):
                masked = d_conv
                if k:
                    masked = d_conv * spread_ref[here, pl.ds(k * LANES, LANES)]
                before = held[pl.ds(ext_at + token + past - k, block)]
                blocks = masked.reshape(block, seqs, LANES)
                fresh.append(sums[k] + jnp.sum(blocks * before, axis=0))
                tap = taps_ref[pl.ds(k, 1), lanes]
                held[pl.ds(tap_at[k] + token, block)] = blocks * tap[None]
            fresh.append(sums[past + 1] + jnp.sum(d_conv.reshape(block, seqs, LANES), axis=0))
            return tuple(fresh)

        sums = lax.fori_loop(0, rows // size, one, (zero,) * (past + 2))
        for k in range(past + 2):
            sums_ref[pl.ds(k * seqs, seqs), lanes] = sums[k]
        for k in range(1, past + 1):
            for later in range(past):
                held[tap_at[k] + tokens + later] = zero

        def gather(part, carry):
            token = part * block
            total = held[pl.ds(tap_at[0] + token, block)]
            for k in range(1, past + 1):
                total = total + held[pl.ds(tap_at[k] + token + k, block)]
            total = total.reshape(size, LANES)
            inner_ref[at_rows(part, size), lanes] = total.astype(BF)

            @pl.when(part == rows // size - 1)
            def _():
                tail[:, lanes] = total[size - tail.shape[0] :]

            return carry

        lax.fori_loop(0, rows // size, gather, 0)
        first = [zero] * (tail.shape[0] // seqs - past)
        for token in range(past):
            total = zero
            for k in range(past - token, past + 1):
                total = total + held[tap_at[k] + token - past + k]
            first.append(total)
        edge[:, lanes] = jnp.concatenate(first, axis=0).astype(BF)
        for k in range(tiles):

            @pl.when(tile == k)
            def _():
                scatter.advance(tiles + 3 + k)

        return carry

    lax.fori_loop(0, tiles, convolve, 0)
    hand = pltpu.make_async_remote_copy(
        src_ref=edge,
        dst_ref=from_next,
        send_sem=edge_sems.at[0],
        recv_sem=edge_sems.at[1],
        device_id={"seq": lax.rem(place + count - 1, count)},
        device_id_type=pl.DeviceIdType.MESH,
    )

    @pl.when(place > 0)
    def _():
        hand.start()

    @pl.when(place < count - 1)
    def _():
        hand.wait_recv()
        last_rows = pl.ds(rows - tail.shape[0], tail.shape[0])
        inner_ref[last_rows, :] = (tail[...] + from_next[...].astype(F32)).astype(BF)

    @pl.when(place > 0)
    def _():
        hand.wait_send()

    trade[1].wait_send()
    for turn in range(2 * tiles + 3, scatter.turns):
        scatter.advance(turn)
    scatter.finish()


def stats_back(stats, projected, gains, states):
    rank = LANES - 2 * states
    lane = lax.broadcasted_iota(jnp.int32, stats.shape, 1)
    parts = [
        (lane < rank, rank),
        ((lane >= rank) & (lane < rank + states), states),
        (lane >= rank + states, states),
    ]

    def means(values):
        total = jnp.zeros_like(values)
        for inside, size in parts:
            mean = jnp.sum(jnp.where(inside, values, 0.0), axis=1, keepdims=True) / size
            total = jnp.where(inside, mean, total)
        return total

    scale = lax.rsqrt(means(projected * projected) + EPS)
    normed = projected * scale
    scaled = stats * gains
    return scale * (scaled - normed * means(scaled * normed)), stats * normed


class PairScatter:
    def __init__(self, count, grads, given, came, scratch):
        place = lax.axis_index("seq")
        self.around = count // 2
        self.low, self.high = lax.rem(place, 2), place // 2
        self.grads, self.given, self.came = grads, given, came
        self.mine_buf, self.given_buf, self.sum_buf = scratch[:3]
        self.swap_send, self.swap_recv, self.hop_send, self.hop_recv, self.load_sem = scratch[3:]
        self.items = [(k, steps) for k in range(len(grads)) for steps in range(1, self.around)]
        self.turns = len(self.items) + 1

    def pair(self, steps):
        return lax.rem(self.high + steps, self.around)

    def swap(self, kind, steps):
        return pltpu.make_async_remote_copy(
            src_ref=self.grads[kind].at[self.pair(steps), 1 - self.low],
            dst_ref=self.given[kind].at[steps],
            send_sem=self.swap_send.at[kind, steps],
            recv_sem=self.swap_recv.at[kind, steps],
            device_id={"seq": self.high * 2 + 1 - self.low},
            device_id_type=pl.DeviceIdType.MESH,
        )

    def hop(self, item):
        kind, steps = self.items[item]
        wide = self.grads[kind].shape[-1]
        return pltpu.make_async_remote_copy(
            src_ref=self.sum_buf.at[item % 2, :, pl.ds(0, wide)],
            dst_ref=self.came[kind].at[steps - 1],
            send_sem=self.hop_send.at[kind, steps],
            recv_sem=self.hop_recv.at[kind, steps],
            device_id={"seq": self.pair(steps) * 2 + self.low},
            device_id_type=pl.DeviceIdType.MESH,
        )

    def loads(self, item):
        kind, steps = self.items[item]
        lanes = pl.ds(0, self.grads[kind].shape[-1])
        return [
            pltpu.make_async_copy(
                self.grads[kind].at[self.pair(steps), self.low],
                self.mine_buf.at[item % 2, :, lanes],
                self.load_sem.at[item % 2, 0],
            ),
            pltpu.make_async_copy(
                self.given[kind].at[steps],
                self.given_buf.at[item % 2, :, lanes],
                self.load_sem.at[item % 2, 1],
            ),
        ]

    def start(self):
        for kind, steps in self.items:
            self.swap(kind, steps).start()
        for kind in range(len(self.grads)):
            self.swap(kind, 0).start()

    def advance(self, turn):
        if turn < len(self.items):
            self.swap(*self.items[turn]).wait_recv()
            for load in self.loads(turn):
                load.start()
        item = turn - 1
        if 0 <= item < len(self.items):
            for load in self.loads(item):
                load.wait()
            if item >= 2:
                self.hop(item - 2).wait_send()
            wide = self.grads[self.items[item][0]].shape[-1]
            rows = self.mine_buf.shape[1]

            def add(row, carry):
                here = at_rows(row, 16)
                lanes = pl.ds(0, wide)
                total = self.mine_buf[item % 2, here, lanes].astype(F32) + self.given_buf[
                    item % 2, here, lanes
                ].astype(F32)
                self.sum_buf[item % 2, here, lanes] = total.astype(self.sum_buf.dtype)
                return carry

            lax.fori_loop(0, rows // 16, add, 0)
            self.hop(item).start()

    def finish(self):
        for item in range(max(0, len(self.items) - 2), len(self.items)):
            self.hop(item).wait_send()
        for item in range(len(self.items)):
            self.hop(item).wait_recv()
            self.swap(*self.items[item]).wait_send()
        for kind in range(len(self.grads)):
            self.swap(kind, 0).wait()


def scatter_scratch(count, grads):
    rows = grads[0].shape[2]
    wide = max(grad.shape[3] for grad in grads)
    sems = pltpu.SemaphoreType.DMA((len(grads), count // 2))
    buffer = pltpu.VMEM((2, rows, wide), grads[0].dtype)
    return [buffer] * 3 + [sems] * 4 + [pltpu.SemaphoreType.DMA((2, 2))]


def exchange_scratch(count, seqs, states, channels):
    sems = pltpu.SemaphoreType.DMA((2, count // 2, channels // LANES))
    return [
        pltpu.VMEM((count, states * seqs, channels), BF),
        pltpu.VMEM((count, seqs, channels), F32),
    ] + [sems] * 4


def state_call(body, ident, seqs, states, columns, ins, outs, scratch, ops, hosted):
    count = lax.axis_size("seq")
    rows, channels = ins[1].shape
    in_vmem = pl.BlockSpec(memory_space=pltpu.VMEM)
    anywhere = pl.BlockSpec(memory_space=pl.ANY)
    return pl.pallas_call(
        functools.partial(body, count, seqs, states),
        in_specs=[in_vmem] * (len(ins) - hosted[0]) + [anywhere] * hosted[0],
        out_specs=tuple([in_vmem] * (len(outs) - hosted[1]) + [anywhere] * hosted[1]),
        out_shape=tuple(outs),
        scratch_shapes=[pltpu.VMEM((rows, columns * LANES), F32)] + scratch,
        compiler_params=pltpu.CompilerParams(
            collective_id=ident, has_side_effects=True, vmem_limit_bytes=62 * 1024 * 1024
        ),
        cost_estimate=pl.CostEstimate(
            flops=ops * rows * channels * states,
            bytes_accessed=16 * 1024 * 1024,
            transcendentals=0,
        ),
    )(*ins)


class BlockGather:
    def __init__(self, count, source, target, sems):
        place = lax.axis_index("seq")
        self.around = count // 2
        self.low, self.high = lax.rem(place, 2), place // 2
        self.place = place
        self.source, self.target = source, target
        self.hop_send, self.hop_recv, self.swap_send, self.swap_recv, self.local_sem = sems
        self.mate = self.high * 2 + 1 - self.low
        self.pieces = pieces_of(source.shape[-1])

    def pair(self, steps):
        return lax.rem(self.high + steps + self.around, self.around) * 2 + self.low

    def lanes(self, piece):
        size = self.source.shape[-1] // self.pieces
        return pl.ds(piece * size, size)

    def local(self):
        return pltpu.make_async_copy(self.source, self.target.at[self.place], self.local_sem.at[0])

    def hop(self, piece, steps):
        return pltpu.make_async_remote_copy(
            src_ref=self.source.at[:, self.lanes(piece)],
            dst_ref=self.target.at[self.place, :, self.lanes(piece)],
            send_sem=self.hop_send.at[piece, steps],
            recv_sem=self.hop_recv.at[piece, steps],
            device_id={"seq": self.pair(steps)},
            device_id_type=pl.DeviceIdType.MESH,
        )

    def swap(self, piece, steps):
        block = self.target.at[self.pair(-steps), :, self.lanes(piece)]
        return pltpu.make_async_remote_copy(
            src_ref=block if steps else self.source.at[:, self.lanes(piece)],
            dst_ref=block,
            send_sem=self.swap_send.at[piece, steps],
            recv_sem=self.swap_recv.at[piece, steps],
            device_id={"seq": self.mate},
            device_id_type=pl.DeviceIdType.MESH,
        )

    def start(self):
        self.local().start()
        for piece in range(self.pieces):
            for steps in range(1, self.around):
                self.hop(piece, steps).start()
        for piece in range(self.pieces):
            self.swap(piece, 0).start()

    def relay(self, piece):
        for steps in range(1, self.around):
            self.hop(piece, steps).wait_recv()
            self.swap(piece, steps).start()

    def finish(self):
        self.local().wait()
        for piece in range(self.pieces):
            for steps in range(1, self.around):
                self.hop(piece, steps).wait_send()
            for steps in range(self.around):
                self.swap(piece, steps).wait()


def pieces_of(width):
    for size in (256, 384):
        if width % size == 0:
            return width // size
    return 1


def gather_sems(around, width):
    pieces = pieces_of(width)
    return [pltpu.SemaphoreType.DMA((pieces, around))] * 4 + [pltpu.SemaphoreType.DMA((1,))]


def greet_pairs(count, heads=False, ring=False):
    place = lax.axis_index("seq")
    around = count // 2
    low, high = lax.rem(place, 2), place // 2
    barrier = pltpu.get_barrier_semaphore()
    peers = [lax.rem(high + steps, around) * 2 + low for steps in range(1, around)]
    peers = [{"seq": device} for device in peers + [high * 2 + 1 - low]]
    if heads:
        head = lax.axis_index("head")
        low, high = lax.rem(head, 2), head // 2
        peers += [{"head": high * 2 + 1 - low}, {"head": 2 - 2 * high + low}]
    if ring:
        peers += [{"seq": lax.rem(place + 1, count)}, {"seq": lax.rem(place + count - 1, count)}]
    for device in peers:
        pl.semaphore_signal(barrier, inc=1, device_id=device, device_id_type=pl.DeviceIdType.MESH)
    pl.semaphore_wait(barrier, len(peers))


class HeadSum:
    def __init__(self, part, half, give, take, whole, sems):
        head = lax.axis_index("head")
        self.low, self.high = lax.rem(head, 2), head // 2
        self.near = {"head": self.high * 2 + 1 - self.low}
        self.far = {"head": 2 - 2 * self.high + self.low}
        self.part, self.half, self.give, self.take, self.whole = part, half, give, take, whole
        self.sems = sems
        self.size = half.shape[1]

    def copy(self, source, target, kind, chunk, device):
        return pltpu.make_async_remote_copy(
            src_ref=source,
            dst_ref=target,
            send_sem=self.sems.at[kind, 0, chunk],
            recv_sem=self.sems.at[kind, 1, chunk],
            device_id=device,
            device_id_type=pl.DeviceIdType.MESH,
        )

    def rows(self, chunk, bit):
        start = pl.multiple_of((chunk * 2 + bit) * self.size, self.size)
        return pl.ds(start, self.size)

    def own_rows(self, chunk):
        quarter = self.size // 2
        start = (chunk * 2 + self.low) * self.size + self.high * quarter
        return pl.ds(pl.multiple_of(start, quarter), quarter)

    def near_copy(self, chunk):
        return self.copy(
            self.part.at[self.rows(chunk, 1 - self.low)], self.half.at[chunk], 0, chunk, self.near
        )

    def far_copy(self, chunk):
        return self.copy(self.give.at[chunk], self.take.at[chunk], 1, chunk, self.far)

    def far_back(self, chunk):
        here = self.whole.at[self.own_rows(chunk)]
        return self.copy(here, here, 2, chunk, self.far)

    def near_back(self, chunk):
        here = self.whole.at[self.rows(chunk, self.low)]
        return self.copy(here, here, 3, chunk, self.near)

    def fold(self, chunk, kept):
        self.near_copy(chunk).wait_recv()
        quarter = self.size // 2
        base = (chunk * 2 + self.low) * self.size
        for mine in (False, True):
            bit = self.high if mine else 1 - self.high
            start = pl.multiple_of(bit * quarter, quarter)
            at = pl.multiple_of(base + bit * quarter, quarter)
            total = self.part[pl.ds(at, quarter), :].astype(F32)
            total = total + self.half[chunk, pl.ds(start, quarter), :].astype(F32)
            if mine:
                kept[chunk] = total
            else:
                self.give[chunk] = total.astype(BF)
                self.far_copy(chunk).start()

    def finish(self, chunk, near=True):
        copies = [self.far_copy, self.far_back, self.near_back]
        for copy in copies + [self.near_copy] * near:
            copy(chunk).wait_send()


def put_sequences(target, rows_ref, chunk, size, buffer):
    seqs = target.shape[0]
    span = size // seqs
    for m in range(buffer.shape[0]):
        lanes = pl.ds(m * LANES, LANES)
        buffer[m] = rows_ref[at_rows(chunk, size), lanes].astype(F32)
        for k in range(seqs):
            rows = buffer[m, pl.ds(k, span, stride=seqs), :]
            target[k, at_rows(chunk, span), lanes] = rows.astype(target.dtype)


def transposed_dot(left, right):
    return lax.dot_general(left, right, (((1,), (1,)), ((), ())), preferred_element_type=F32)


def ffn_kernel(count, chunks, *refs):
    g_ref, out_ref, gain_ref, *refs = refs
    sources, up_shard, down_shard, refs = refs[:3], refs[3], refs[4], refs[5:]
    hidden_ref, norm_ref, act_ref, dgate_ref, dup_ref, dnorm_gain_ref, part_out_ref, *refs = refs
    dhidden_ref, dmix_ref, *refs = refs
    up_ref, down_ref, *refs = refs
    part, half_a, give_a, take_a, half_b, give_b, take_b, kept, *refs = refs
    gate_buf, up_buf, sems_a, sems_b, *refs = refs
    x_ref, gate_ref, low_ref, fetch_sems, *refs = refs
    fetch = Fetch(sources, (x_ref, gate_ref, low_ref), fetch_sems)
    fetch.start()
    gathers = [
        BlockGather(count, up_shard, up_ref, refs[:5]),
        BlockGather(count, down_shard, down_ref, refs[5:]),
    ]
    mix = HeadSum(part, half_a, give_a, take_a, norm_ref, sems_a)
    back = HeadSum(part, half_b, give_b, take_b, dmix_ref, sems_b)
    size = g_ref.shape[0] // chunks
    quarter = size // 4
    width = x_ref.shape[1]
    shard, units = down_ref.shape[1:]
    channels = g_ref.shape[1]
    greet_pairs(count, True)
    for gather in gathers:
        gather.start()
    fourth = -(-gathers[0].pieces // chunks)

    def relay(gather, chunk):
        for k in range(chunks):
            pieces = range(gather.pieces)[k * fourth : (k + 1) * fourth]
            if pieces:

                @pl.when(chunk == k)
                def _():
                    for piece in pieces:
                        gather.relay(piece)


    def project(chunk, carry):
        here = at_rows(chunk, size)
        weights = out_ref[:, :, pl.ds(channels, channels)].reshape(width, channels)
        part[here, :] = transposed_dot(g_ref[here, :], weights).astype(BF)
        mix.near_copy(chunk).start()
        return carry

    lax.fori_loop(0, chunks, project, 0)

    def fold(chunk, carry):
        mix.fold(chunk, kept)
        return carry

    lax.fori_loop(0, chunks, fold, 0)

    def normalise(chunk, carry):
        mix.far_copy(chunk).wait_recv()
        here = at_rows(chunk, quarter)
        own = x_ref[mix.own_rows(chunk), :].astype(F32)
        hidden = own + kept[chunk] + take_a[chunk].astype(F32)
        hidden_ref[here, :] = hidden
        scale = lax.rsqrt(jnp.mean(hidden * hidden, axis=1, keepdims=True) + EPS)
        norm_ref[mix.own_rows(chunk), :] = (hidden * scale * gain_ref[...]).astype(BF)
        mix.far_back(chunk).start()
        relay(gathers[0], chunk)
        return carry

    fetch.wait(0)
    lax.fori_loop(0, chunks, normalise, 0)
    fetch.wait(1)
    mix.far_back(0).wait_recv()
    mix.near_back(0).start()
    gathers[0].finish()
    per_block = max(1, count // 4)
    wide = per_block * shard
    lanes_block = 256 if units % 256 == 0 else units

    def widen(chunk, carry):
        here = at_rows(chunk, size)

        @pl.when(chunk + 1 < chunks)
        def _():
            mix.far_back(chunk + 1).wait_recv()
            mix.near_back(chunk + 1).start()

        mix.near_back(chunk).wait_recv()
        rows = norm_ref[here, :]
        for k in range(units // lanes_block):
            lanes = pl.ds(k * lanes_block, lanes_block)
            block = lambda ref: ref[:, :, lanes].reshape(width, lanes_block)
            gate_buf[here, lanes] = jnp.dot(rows, block(gate_ref), preferred_element_type=F32)
            up_buf[here, lanes] = jnp.dot(rows, block(up_ref), preferred_element_type=F32)
        relay(gathers[1], chunk)
        return carry

    lax.fori_loop(0, chunks, widen, 0)
    gathers[1].finish()
    fetch.wait(2)

    def feed(chunk, carry):
        here = at_rows(chunk, size)
        mix.near_copy(chunk).wait_send()
        grads = low_ref[here, :]
        for k in range(units // lanes_block):
            lanes = pl.ds(k * lanes_block, lanes_block)
            block = lambda ref: ref[:, :, lanes].reshape(width, lanes_block)
            gate, up = gate_buf[here, lanes], up_buf[here, lanes]
            d_act = jnp.dot(grads, block(down_ref), preferred_element_type=F32)
            logistic = 1.0 / (1.0 + jnp.exp(-gate))
            silu = gate * logistic
            act_ref[here, lanes] = (silu * up).astype(BF)
            slope = logistic * (1.0 + gate * (1.0 - logistic))
            dgate_ref[here, lanes] = (d_act * up * slope).astype(BF)
            dup_ref[here, lanes] = (d_act * silu).astype(BF)
        for k in range(count // per_block):
            lanes = pl.ds(k * wide, wide)
            block = lambda ref: ref[pl.ds(k * per_block, per_block)].reshape(wide, units)
            total = transposed_dot(dgate_ref[here, :], block(gate_ref))
            total = total + transposed_dot(dup_ref[here, :], block(up_ref))
            part[here, lanes] = total.astype(BF)
        back.near_copy(chunk).start()
        for k in range(count // per_block):
            lanes = pl.ds(k * wide, wide)
            block = down_ref[pl.ds(k * per_block, per_block)].reshape(wide, units)
            part_out_ref[here, lanes] = transposed_dot(act_ref[here, :], block).astype(BF)

        @pl.when(chunk >= 1)
        def _():
            back.fold(chunk - 1, kept)

        return carry

    lax.fori_loop(0, chunks, feed, 0)
    back.fold(chunks - 1, kept)
    dnorm_gain_ref[...] = jnp.zeros(dnorm_gain_ref.shape, F32)

    def turn(chunk, carry):
        back.far_copy(chunk).wait_recv()
        here = at_rows(chunk, quarter)
        hidden = hidden_ref[here, :]
        scale = lax.rsqrt(jnp.mean(hidden * hidden, axis=1, keepdims=True) + EPS)
        normed = hidden * scale
        d_norm = kept[chunk] + take_b[chunk].astype(F32)
        dnorm_gain_ref[...] += jnp.sum(d_norm * normed, axis=0, keepdims=True)
        scaled = d_norm * gain_ref[...]
        shift = jnp.mean(scaled * normed, axis=1, keepdims=True)
        own = low_ref[back.own_rows(chunk), :].astype(F32)
        d_hidden = own + scale * (scaled - normed * shift)
        dhidden_ref[here, :] = d_hidden
        dmix_ref[back.own_rows(chunk), :] = d_hidden.astype(BF)
        back.far_back(chunk).start()
        return carry

    lax.fori_loop(0, chunks, turn, 0)

    def spread_out(chunk, carry):
        back.far_back(chunk).wait_recv()
        back.near_back(chunk).start()
        return carry

    lax.fori_loop(0, chunks, spread_out, 0)

    def finish(chunk, carry):
        back.near_back(chunk).wait_recv()
        mix.finish(chunk, False)
        back.finish(chunk)
        return carry

    lax.fori_loop(0, chunks, finish, 0)


CHUNKS = 4


def sum_scratch(rows, width, part=True):
    chunk = rows // CHUNKS
    parts = [pltpu.VMEM((rows, width), BF)] if part else []
    return parts + [
        pltpu.VMEM((CHUNKS, chunk // 2, width), BF),
        pltpu.VMEM((CHUNKS, chunk // 4, width), BF),
        pltpu.VMEM((CHUNKS, chunk // 4, width), BF),
    ]


def kept_scratch(rows, width):
    return pltpu.VMEM((CHUNKS, rows // CHUNKS // 4, width), F32)


SUM_SEMS = pltpu.SemaphoreType.DMA((4, 2, CHUNKS))


def ffn_call(g_low, mix_blocks, x_low, gain, grad_low, gate_blocks, w_up, w_down_t):
    count = lax.axis_size("seq")
    rows, width = grad_low.shape
    units = w_down_t.shape[1]
    shape = jax.ShapeDtypeStruct
    in_vmem = pl.BlockSpec(memory_space=pltpu.VMEM)
    anywhere = pl.BlockSpec(memory_space=pl.ANY)
    outs = [
        shape((rows // 4, width), F32),
        shape((rows, width), BF),
        shape((rows, units), BF),
        shape((rows, units), BF),
        shape((rows, units), BF),
        shape((1, width), F32),
        shape((rows, width), BF),
        shape((rows // 4, width), F32),
        shape((rows, width), BF),
    ]
    return pl.pallas_call(
        functools.partial(ffn_kernel, count, CHUNKS),
        in_specs=[in_vmem] * 3 + [anywhere] * 5,
        out_specs=tuple([in_vmem] * len(outs)),
        out_shape=tuple(outs),
        scratch_shapes=[pltpu.VMEM((count,) + w_down_t.shape, BF)] * 2
        + sum_scratch(rows, width)
        + sum_scratch(rows, width, False)
        + [kept_scratch(rows, width)]
        + [pltpu.VMEM((rows, units), F32)] * 2
        + [SUM_SEMS] * 2
        + fetch_scratch([x_low, gate_blocks, grad_low])
        + gather_sems(count // 2, units) * 2,
        compiler_params=pltpu.CompilerParams(
            collective_id=5, has_side_effects=True, vmem_limit_bytes=62 * 1024 * 1024
        ),
        cost_estimate=pl.CostEstimate(
            flops=14 * rows * width * units, bytes_accessed=40 * 1024 * 1024, transcendentals=0
        ),
    )(g_low, mix_blocks, gain, x_low, gate_blocks, grad_low, w_up, w_down_t)


def input_kernel(count, chunks, kinds, *refs):
    inner_ref, z_ref, in_x_ref, gain_ref, dhidden_ref, *refs = refs
    sources, pack_ref, refs = refs[:3], refs[3], refs[4:]
    olds, refs = [refs[k * kinds : (k + 1) * kinds] for k in range(3)], refs[3 * kinds :]
    out_ref, gain_out_ref, *refs = refs
    own_refs, refs = refs[: kinds + 1], refs[kinds + 1 :]
    pack_given, pack_came, *refs = refs
    part, half, give, take, kept, rows_ref, buffer, sems, *refs = refs
    sent, got, vector_sems, grad_ref, given, came, *refs = refs
    norm_ref, mix_ref, x_ref, fetch_sems, *refs = refs
    channels = inner_ref.shape[1]
    sources = [sources[0], sources[1].at[:, :, pl.ds(0, channels)], sources[2]]
    fetch = Fetch(sources, (norm_ref, mix_ref, x_ref), fetch_sems)
    fetch.start()
    owned = OwnSum(count, olds, own_refs, refs[:3])
    refs = refs[3:]
    scatter = PairScatter(count, [grad_ref], [given], [came], refs[:8])
    pack = PairScatter(count, [pack_ref], [pack_given], [pack_came], refs[8:])
    back = HeadSum(part, half, give, take, rows_ref, sems)
    size = inner_ref.shape[0] // chunks
    quarter = size // 4
    shard, channels = in_x_ref.shape[1:]
    per_block = max(1, count // 4)
    wide = per_block * shard
    greet_pairs(count, True)
    pack.start()
    owned.load(0)
    around, _, shard_rows, _ = grad_ref.shape
    together = max(1, 384 // (2 * shard_rows))
    fetch.wait(0)
    for block in range(around // together):
        lanes = pl.ds(block * together * 2 * shard_rows, together * 2 * shard_rows)
        grad = jnp.dot(norm_ref[:, lanes].T, inner_ref[...], preferred_element_type=F32)
        grad = grad.astype(BF).reshape(together, 2, shard_rows, channels)
        grad_ref[pl.ds(block * together, together)] = grad
    scatter.start()
    turns = [(scatter, turn) for turn in range(scatter.turns)]
    turns += [(pack, turn) for turn in range(pack.turns)]
    share = -(-len(turns) // (3 * chunks))
    early = 2 * chunks * share

    def move(chunk, stage):
        for k in range(chunks):
            todo = turns[(stage * chunks + k) * share :][:share]
            if todo:

                @pl.when(chunk == k)
                def _():
                    for moving, turn in todo:
                        moving.advance(turn)

    def own_step(chunk, first):
        for k in range(chunks):
            if first + k < kinds:

                @pl.when(chunk == k)
                def _():
                    owned.add(first + k)

    fetch.wait(1, 2)

    def project(chunk, carry):
        here = at_rows(chunk, size)
        for k in range(count // per_block):
            blocks = pl.ds(k * per_block, per_block)
            total = transposed_dot(inner_ref[here, :], in_x_ref[blocks].reshape(wide, channels))
            in_z = mix_ref[blocks].reshape(wide, channels)
            total = total + transposed_dot(z_ref[here, :], in_z)
            part[here, pl.ds(k * wide, wide)] = total.astype(BF)
        back.near_copy(chunk).start()
        return carry

    lax.fori_loop(0, chunks, project, 0)

    def fold(chunk, carry):
        back.fold(chunk, kept)
        own_step(chunk, 0)
        return carry

    lax.fori_loop(0, chunks, fold, 0)
    gain_out_ref[...] = jnp.zeros(gain_out_ref.shape, F32)
    around = scatter.around

    def vector(stage, slot, device):
        return pltpu.make_async_remote_copy(
            src_ref=sent.at[stage],
            dst_ref=got.at[slot],
            send_sem=vector_sems.at[0, slot],
            recv_sem=vector_sems.at[1, slot],
            device_id=device,
            device_id_type=pl.DeviceIdType.MESH,
        )

    stages = [
        [vector(0, 0, {"seq": scatter.high * 2 + 1 - scatter.low})],
        [
            vector(1, steps, {"seq": scatter.pair(steps) * 2 + scatter.low})
            for steps in range(1, around)
        ],
        [vector(2, around, back.near)],
        [vector(3, around + 1, back.far)],
    ]

    def pass_sum(stage):
        value = gain_out_ref[...]
        if stage > 0:
            for copy in stages[stage - 1]:
                copy.wait_recv()
            slots = [[0], list(range(1, around)), [around], [around + 1]][stage - 1]
            for slot in slots:
                value = value + got[slot]
            gain_out_ref[...] = value
        if stage < len(stages):
            sent[stage] = value
            for copy in stages[stage]:
                copy.start()

    def turn(chunk, carry):
        back.far_copy(chunk).wait_recv()
        here = at_rows(chunk, quarter)
        values = x_ref[back.own_rows(chunk), :].astype(F32)
        scale = lax.rsqrt(jnp.mean(values * values, axis=1, keepdims=True) + EPS)
        normed = values * scale
        d_norm = kept[chunk] + take[chunk].astype(F32)
        share_of_sum = jnp.sum(d_norm * normed, axis=0, keepdims=True)
        gain_out_ref[...] += jnp.broadcast_to(share_of_sum, gain_out_ref.shape)
        scaled = d_norm * gain_ref[...]
        shift = jnp.mean(scaled * normed, axis=1, keepdims=True)
        total = dhidden_ref[here, :] + scale * (scaled - normed * shift)
        rows_ref[back.own_rows(chunk), :] = total.astype(BF)
        back.far_back(chunk).start()
        move(chunk, 0)
        return carry

    lax.fori_loop(0, chunks, turn, 0)
    pass_sum(0)

    def spread_out(chunk, carry):
        back.far_back(chunk).wait_recv()
        back.near_back(chunk).start()
        move(chunk, 1)
        own_step(chunk, chunks)
        return carry

    lax.fori_loop(0, chunks, spread_out, 0)
    for stage in range(1, len(stages) + 1):
        pass_sum(stage)
    for old in range(2 * chunks, kinds):
        owned.add(old)
    for moving, turn in turns[early:]:
        moving.advance(turn)
    for copies in stages:
        for copy in copies:
            copy.wait_send()

    def finish(chunk, carry):
        back.near_back(chunk).wait_recv()
        put_sequences(out_ref, rows_ref, chunk, size, buffer)
        back.finish(chunk)
        return carry

    lax.fori_loop(0, chunks, finish, 0)
    scatter.finish()
    pack.finish()
    place = lax.axis_index("seq")
    total = grad_ref[place // 2, lax.rem(place, 2)].astype(F32) + given[0].astype(F32)
    for k in range(around - 1):
        total = total + came[k].astype(F32)
    own_refs[kinds][...] = total
    owned.finish()


class OwnSum:
    def __init__(self, count, olds, targets, scratch):
        self.place = lax.axis_index("seq")
        self.around = count // 2
        self.grads, self.given, self.came = olds
        self.targets = targets
        self.parts, self.total, self.sems = scratch

    def sources(self, kind):
        own = self.grads[kind].at[self.place // 2, lax.rem(self.place, 2)]
        came = [self.came[kind].at[k] for k in range(self.around - 1)]
        return [own, self.given[kind].at[0]] + came

    def loads(self, kind):
        lanes = pl.ds(0, self.targets[kind].shape[1])
        return [
            pltpu.make_async_copy(source, self.parts.at[k, :, lanes], self.sems.at[k])
            for k, source in enumerate(self.sources(kind))
        ]

    def store(self, kind):
        lanes = pl.ds(0, self.targets[kind].shape[1])
        return pltpu.make_async_copy(
            self.total.at[:, lanes], self.targets[kind], self.sems.at[self.around + 1]
        )

    def load(self, kind):
        for load in self.loads(kind):
            load.start()

    def add(self, kind):
        for load in self.loads(kind):
            load.wait()
        if kind:
            self.store(kind - 1).wait()
        lanes = pl.ds(0, self.targets[kind].shape[1])

        def one(row, carry):
            here = at_rows(row, 16)
            total = self.parts[0, here, lanes].astype(F32)
            for k in range(1, self.around + 1):
                total = total + self.parts[k, here, lanes].astype(F32)
            self.total[here, lanes] = total
            return carry

        lax.fori_loop(0, self.total.shape[0] // 16, one, 0)
        self.store(kind).start()
        if kind + 1 < len(self.grads):
            self.load(kind + 1)

    def finish(self):
        self.store(len(self.grads) - 1).wait()


def moved_shapes(grads):
    shape = jax.ShapeDtypeStruct
    around = grads[0].shape[0]
    given = [shape((around,) + grad.shape[2:], grad.dtype) for grad in grads]
    return given + [shape((around - 1,) + grad.shape[2:], grad.dtype) for grad in grads]


def input_call(d_inner, d_z, in_x_blocks, mix_blocks, x_low, x_norm, gain, d_hidden, pack, olds, dims):
    count = lax.axis_size("seq")
    around = count // 2
    rows, channels = d_inner.shape
    width = x_low.shape[1]
    shape = jax.ShapeDtypeStruct
    in_vmem = pl.BlockSpec(memory_space=pltpu.VMEM)
    anywhere = pl.BlockSpec(memory_space=pl.ANY)
    grads, given, came = olds
    shard = grads[0].shape[2]
    widest = max(grad.shape[3] for grad in grads)
    moved = moved_shapes([pack])
    late = shape((around, 2, shard, channels), BF)
    return pl.pallas_call(
        functools.partial(input_kernel, count, CHUNKS, len(grads)),
        in_specs=[in_vmem] * 5 + [anywhere] * (3 * len(grads) + 4),
        out_specs=tuple(
            [in_vmem] * 2 + [anywhere] * len(grads) + [in_vmem] + [anywhere] * len(moved)
        ),
        out_shape=tuple(
            [shape(dims, F32), shape((8, width), F32)]
            + [shape((shard, grad.shape[3]), F32) for grad in grads]
            + [shape((shard, channels), F32)]
            + moved
        ),
        scratch_shapes=sum_scratch(rows, width)
        + [kept_scratch(rows, width), pltpu.VMEM((rows, width), BF)]
        + [pltpu.VMEM((width // LANES, rows // CHUNKS, LANES), F32), SUM_SEMS]
        + [pltpu.VMEM((4, 8, width), F32), pltpu.VMEM((around + 2, 8, width), F32)]
        + [pltpu.SemaphoreType.DMA((2, around + 2))]
        + [pltpu.VMEM(late.shape, BF), pltpu.VMEM((around, shard, channels), BF)]
        + [pltpu.VMEM((around - 1, shard, channels), BF)]
        + fetch_scratch([x_norm, in_x_blocks, x_low])
        + [pltpu.VMEM((around + 1, shard, widest), BF), pltpu.VMEM((shard, widest), F32)]
        + [pltpu.SemaphoreType.DMA((around + 2,))]
        + scatter_scratch(count, [late])
        + scatter_scratch(count, [pack]),
        compiler_params=pltpu.CompilerParams(
            collective_id=6, has_side_effects=True, vmem_limit_bytes=62 * 1024 * 1024
        ),
        cost_estimate=pl.CostEstimate(
            flops=4 * rows * width * d_inner.shape[1],
            bytes_accessed=40 * 1024 * 1024,
            transcendentals=0,
        ),
    )(
        d_inner,
        d_z,
        in_x_blocks,
        gain,
        d_hidden,
        x_norm,
        mix_blocks,
        x_low,
        pack,
        *grads,
        *given,
        *came,
    )


class Fetch:
    def __init__(self, sources, targets, sems):
        self.copies = [
            pltpu.make_async_copy(source, target, sems.at[k])
            for k, (source, target) in enumerate(zip(sources, targets))
        ]

    def start(self):
        for copy in self.copies:
            copy.start()

    def wait(self, *which):
        for k in which:
            self.copies[k].wait()


def fetch_scratch(values):
    buffers = [pltpu.VMEM(value.shape, value.dtype) for value in values]
    return buffers + [pltpu.SemaphoreType.DMA((len(values),))]


def pairs_of(axis):
    return lax.axis_size(axis) // 2


def hop(value, steps):
    count = lax.axis_size("seq")
    return lax.ppermute(value, "seq", [(s, (s + 2 * steps) % count) for s in range(count)])


def swap(value, axis, bit):
    return lax.ppermute(value, axis, [(s, s ^ bit) for s in range(lax.axis_size(axis))])


def owner_blocks(value):
    return value.reshape((pairs_of("seq"), 2, -1) + value.shape[1:])


def scatter_half(blocks, theirs):
    place = lax.axis_index("seq")
    around = pairs_of("seq")
    low, high = place % 2, place // 2
    mine = lax.dynamic_index_in_dim(blocks, low, 1, False)
    half = mine.astype(F32) + theirs.astype(F32)
    total = lax.dynamic_index_in_dim(half, high, 0, False)
    half = half.astype(blocks.dtype)
    for steps in range(1, around):
        part = lax.dynamic_index_in_dim(half, (high + steps) % around, 0, False)
        total = total + hop(part, steps).astype(F32)
    return total


def scatter_rows(value, kind=BF):
    low = lax.axis_index("seq") % 2
    blocks = owner_blocks(value.astype(kind))
    theirs = lax.dynamic_index_in_dim(blocks, 1 - low, 1, False)
    return scatter_half(blocks, swap(theirs, "seq", 1))


def scatter_own(blocks, given, came):
    place = lax.axis_index("seq")
    own = blocks.reshape((-1,) + blocks.shape[2:])
    total = lax.dynamic_index_in_dim(own, place, 0, False).astype(F32) + given[0].astype(F32)
    for k in range(came.shape[0]):
        total = total + came[k].astype(F32)
    return total


def head_bits():
    return (lax.axis_size("head") - 1).bit_length()


def head_scatter(value):
    place = lax.axis_index("head")
    width = value.shape[1]
    value = value.reshape(CHUNKS, -1, width)
    for k in range(head_bits()):
        bit = place // 2**k % 2
        halves = value.astype(BF).reshape(CHUNKS, 2, -1, width)
        keep = lax.dynamic_index_in_dim(halves, bit, 1, False)
        send = lax.dynamic_index_in_dim(halves, 1 - bit, 1, False)
        value = keep.astype(F32) + swap(send, "head", 2**k).astype(F32)
    return value.reshape(-1, width)


def head_part(value):
    place = lax.axis_index("head")
    width = value.shape[1]
    value = value.reshape(CHUNKS, -1, width)
    for k in range(head_bits()):
        halves = value.reshape(CHUNKS, 2, -1, width)
        value = lax.dynamic_index_in_dim(halves, place // 2**k % 2, 1, False)
    return value.reshape(-1, width)


def head_gather(value):
    place = lax.axis_index("head")
    width = value.shape[1]
    value = value.reshape(CHUNKS, -1, width)
    for k in reversed(range(head_bits())):
        got = swap(value, "head", 2**k)
        first = place // 2**k % 2 == 0
        both = [jnp.where(first, value, got), jnp.where(first, got, value)]
        value = jnp.concatenate(both, axis=1)
    return value.reshape(-1, width)


def head_total(value, kind):
    for k in range(head_bits()):
        value = value.astype(kind)
        value = value.astype(F32) + swap(value, "head", 2**k).astype(F32)
    return value


def first_kernel(count, kinds, turned, *refs):
    sources, plain, refs = refs[:kinds], refs[kinds : kinds + turned], refs[kinds + turned :]
    targets, outs, refs = refs[:kinds], refs[kinds : kinds + turned], refs[kinds + turned :]
    buffer, *refs = refs
    gathers = [
        BlockGather(count, sources[k], targets[k], refs[5 * k : 5 * k + 5]) for k in range(kinds)
    ]
    greet_pairs(count)
    for gather in gathers:
        gather.start()
    for source, target in zip(plain, outs):
        seqs, tokens, _ = source.shape

        def widen(k, carry):
            for m in range(buffer.shape[0]):
                lanes = pl.ds(m * LANES, LANES)
                buffer[m, at_rows(k, tokens), :] = source[k, :, lanes].astype(F32)
            return carry

        lax.fori_loop(0, seqs, widen, 0)

        def turn(pair, carry):
            for m in range(buffer.shape[0]):
                both = [buffer[m, pl.ds(2 * pair + k, seqs, stride=tokens), :] for k in range(2)]
                both = jnp.concatenate(both, axis=0).astype(BF)
                target[at_rows(pair, 2 * seqs), pl.ds(m * LANES, LANES)] = both
            return carry

        lax.fori_loop(0, tokens // 2, turn, 0)
    for gather in gathers:
        for piece in range(gather.pieces):
            gather.relay(piece)
    for gather in gathers:
        gather.finish()


def first_gather(values, plain):
    count = lax.axis_size("seq")
    around = count // 2
    seqs, tokens, width = plain[0].shape
    shape = jax.ShapeDtypeStruct
    in_vmem = pl.BlockSpec(memory_space=pltpu.VMEM)
    anywhere = pl.BlockSpec(memory_space=pl.ANY)
    return pl.pallas_call(
        functools.partial(first_kernel, count, len(values), len(plain)),
        out_shape=tuple(
            [shape((count,) + v.shape, v.dtype) for v in values]
            + [shape((seqs * tokens, width), BF) for _ in plain]
        ),
        in_specs=[anywhere] * len(values) + [in_vmem] * len(plain),
        out_specs=tuple([anywhere] * len(values) + [in_vmem] * len(plain)),
        scratch_shapes=[pltpu.VMEM((width // LANES, seqs * tokens, LANES), F32)]
        + [sem for v in values for sem in gather_sems(around, v.shape[-1])],
        compiler_params=pltpu.CompilerParams(
            collective_id=0, has_side_effects=True, vmem_limit_bytes=40 * 1024 * 1024
        ),
    )(*values, *plain)


def shards(
    x_in,
    seg_ids,
    norm1_gain,
    w_in_x,
    w_in_z,
    conv_w,
    conv_b,
    w_xproj,
    ssm_gain,
    w_dt,
    dt_bias,
    a_log,
    d_skip,
    w_out,
    norm2_gain,
    w_gate,
    w_up,
    w_down,
    d_out,
):
    count = lax.axis_size("seq")
    place = lax.axis_index("seq")
    seqs, tokens, width = x_in.shape
    rows = seqs * tokens
    taps = conv_w.shape[0]
    rank = w_dt.shape[0]
    states = a_log.shape[1]
    channels = w_in_x.shape[1]
    halo = (taps - 1) * seqs

    per = channels // count
    fields = [w_xproj, w_dt.T, a_log, conv_w.T, conv_b[:, None], dt_bias[:, None], d_skip[:, None]]
    starts = [0]
    for field in fields:
        starts.append(starts[-1] + field.shape[1])
    pack_width = -(-starts[-1] // LANES) * LANES
    gains = [norm1_gain, norm2_gain, ssm_gain]
    gain_starts = [0]
    for gain in gains:
        gain_starts.append(gain_starts[-1] + gain.shape[0])
    pack_rows = -(-(per + -(-gain_starts[-1] // pack_width)) // 16) * 16

    def pack(channel_fields, gain_fields):
        table = jnp.concatenate([f.astype(F32) for f in channel_fields], axis=1)
        table = jnp.pad(table, ((0, 0), (0, pack_width - table.shape[1])))
        table = table.reshape(-1, per, pack_width)
        rest = jnp.concatenate([g.astype(F32).reshape(table.shape[0], -1) for g in gain_fields], 1)
        rest = jnp.pad(rest, ((0, 0), (0, (pack_rows - per) * pack_width - rest.shape[1])))
        return jnp.concatenate([table, rest.reshape(-1, pack_rows - per, pack_width)], axis=1)

    def unpack(block):
        table = block[:, :per].reshape(-1, pack_width)
        rest = block[:, per:].reshape(block.shape[0], -1)
        return (
            [table[:, starts[k] : starts[k + 1]] for k in range(len(fields))],
            [rest[:, gain_starts[k] : gain_starts[k + 1]].reshape(-1) for k in range(len(gains))],
        )

    in_x_blocks, pack_blocks, x_low, grad_low = first_gather(
        [w_in_x.astype(BF), pack(fields, gains)[0].astype(BF)], [x_in, d_out]
    )
    fulls, full_gains = unpack(pack_blocks)
    full_xproj, w_dt_cols, full_a_log, conv_cols, conv_b_col, bias_col, skip_col = fulls
    full_w_dt = w_dt_cols.T
    full_conv_w = conv_cols.T
    full_conv_b, full_dt_bias, full_d_skip = conv_b_col[:, 0], bias_col[:, 0], skip_col[:, 0]
    full_norm1, full_norm2, full_ssm_gain = full_gains

    w_mix = jnp.concatenate([w_in_z.astype(BF), w_out.astype(BF).T], axis=1)
    w_mix, in_x_blocks = lax.optimization_barrier((w_mix, in_x_blocks))
    full_in_x = in_x_blocks.reshape(width, channels)
    full_mix = lax.all_gather(w_mix, "seq", axis=0, tiled=True)

    norm1_vec = full_norm1.astype(F32)
    x_rows = x_low.astype(F32)
    ids = seg_ids.T.reshape(rows)
    normed1, scale_one = norm_rows(x_rows, norm1_vec)
    x_norm = normed1.astype(BF)
    x_inner = jnp.dot(x_norm, full_in_x, preferred_element_type=F32).astype(BF)
    prev_tail, prev_ids = shifted((x_inner[rows - halo :], ids[rows - halo :]), "seq", 1)
    extended = jnp.concatenate([prev_tail, x_inner], axis=0).astype(F32)
    ext_ids = jnp.concatenate([prev_ids, ids])
    conv_weight = full_conv_w.astype(F32)
    x_conv = full_conv_b.astype(F32)[None, :]
    same_docs = []
    for offset in range(taps):
        first = (taps - 1 - offset) * seqs
        same = (ext_ids[first : first + rows] == ids).astype(F32)[:, None]
        same_docs.append(same)
        x_conv = x_conv + conv_weight[offset] * extended[first : first + rows] * same
    u_low = jax.nn.silu(x_conv).astype(BF)
    projected = head_total(jnp.dot(u_low, full_xproj, preferred_element_type=F32), BF)
    ssm_vec = full_ssm_gain.astype(F32)
    b_end = rank + states
    dt_normed, dt_scale = norm_rows(projected[:, :rank], ssm_vec[:rank])
    b_normed, b_scale = norm_rows(projected[:, rank:b_end], ssm_vec[rank:b_end])
    c_normed, c_scale = norm_rows(projected[:, b_end:], ssm_vec[b_end:])
    dt_low = dt_normed.astype(BF)
    dt_pre = jnp.dot(dt_low, full_w_dt, preferred_element_type=F32) + full_dt_bias.astype(F32)
    step = jax.nn.softplus(dt_pre)
    rates = -jnp.exp(full_a_log.astype(F32))
    rate_rows = jnp.repeat((rates * LOG2E).T, seqs, axis=0)
    bc = jnp.concatenate([b_normed, c_normed], axis=1)
    part_one = bc.astype(BF)
    part_two = (bc - part_one.astype(F32)).astype(BF)
    part_three = (bc - part_one.astype(F32) - part_two.astype(F32)).astype(BF)
    stops = ((1.0 - same_docs[1]) * STOP).astype(BF)
    masks = [same.astype(BF) for same in same_docs[1:]]
    spare = jnp.zeros((rows, LANES - 6 * states - taps), BF)
    parts = jnp.concatenate([part_one, part_two, part_three, stops] + masks + [spare], axis=1)
    shape = jax.ShapeDtypeStruct
    state_rows = states * seqs
    start, step_sum = state_call(
        entry_kernel,
        1,
        seqs,
        states,
        2 * states + 2,
        [parts, step, u_low, rate_rows],
        [shape((state_rows, channels), F32), shape((seqs, channels), F32)],
        exchange_scratch(count, seqs, states, channels),
        6,
        (0, 0),
    )
    start, full_mix = lax.optimization_barrier((start, full_mix))
    mix_blocks = full_mix.reshape(count, -1, full_mix.shape[1])
    w_gate_low = w_gate.astype(BF)
    y_state, gate_blocks = state_call(
        forward_kernel,
        2,
        seqs,
        states,
        2 * states + 2,
        [parts, step, u_low, rate_rows, start, w_gate_low],
        [shape((rows, channels), F32), shape((count,) + w_gate.shape, BF)],
        gather_sems(count // 2, w_gate.shape[1]),
        8,
        (1, 1),
    )
    full_in_z = full_mix[:, :channels]
    z_gate = jnp.dot(x_norm, full_in_z, preferred_element_type=F32)
    skip_vec = full_d_skip.astype(F32)
    u_rows = u_low.astype(F32)
    y_full = y_state + skip_vec * u_rows
    silu_z = jax.nn.silu(z_gate)
    g_low = (y_full * silu_z).astype(BF)
    hidden, x_norm2, act_low, d_gate, d_up, norm2_sums, ffn_part, d_hidden, d_mix = ffn_call(
        g_low,
        mix_blocks,
        x_low,
        full_norm2.astype(F32)[None, :],
        grad_low,
        gate_blocks,
        w_up.astype(BF),
        w_down.astype(BF).T,
    )
    grad_norm2 = norm2_sums[0]
    grad_out_w = jnp.einsum("rd,re->de", d_mix, g_low, preferred_element_type=F32)
    full_out_t = full_mix[:, channels:]
    d_g = jnp.dot(d_mix, full_out_t, preferred_element_type=F32)
    d_y = d_g * silu_z
    d_z = (d_g * y_full * silu_slope(z_gate)).astype(BF)
    grad_skip = jnp.sum(d_y * u_rows, axis=0)
    grad_block = shape((count // 2, 2, width // count, w_gate.shape[1]), BF)
    down_moved = moved_shapes([grad_block])
    fetched = [ffn_part, grad_low, act_low, x_norm2, d_gate, d_up, hidden]
    last, grad_down, grad_gate, grad_up, block_out, *down_moved = state_call(
        adjoint_kernel,
        3,
        seqs,
        states,
        states + 2,
        [parts, step, d_y, rate_rows, step_sum] + fetched,
        [shape((state_rows, channels), F32)]
        + [grad_block] * 3
        + [shape(x_in.shape, BF)]
        + down_moved,
        exchange_scratch(count, seqs, states, channels)
        + sum_scratch(rows, width, False)
        + [kept_scratch(rows, width), pltpu.VMEM((rows, width), BF)]
        + [pltpu.VMEM((width // LANES, rows // CHUNKS, LANES), F32), SUM_SEMS]
        + fetch_scratch(fetched)
        + scatter_scratch(count, [grad_block]),
        6,
        (7, 2),
    )
    grad_in_z = jnp.einsum("rd,re->de", x_norm, d_z, preferred_element_type=F32)
    big_grads = [grad_gate, grad_up]
    big_grads += [owner_blocks(grad.astype(BF)) for grad in (grad_out_w, grad_in_z)]
    padded = lambda value: jnp.pad(value, ((0, 0), (0, LANES - value.shape[1])))
    taps_table = jnp.concatenate([conv_weight, skip_vec[None, :]], axis=0)
    taps_table = jnp.pad(taps_table, ((0, 2 * taps - taps_table.shape[0]), (0, 0)))
    big_ins = [x_conv, extended.reshape(-1, seqs, channels), projected] + big_grads
    block_rows_moved = moved_shapes(big_grads)
    bf_rows = pltpu.VMEM((4 * seqs, channels), BF)
    d_inner_low, ssm_sums, grad_xproj, grad_step_t, d_log, column_sums, *first_moved = state_call(
        backward_kernel,
        4,
        seqs,
        states,
        2 * states + 2,
        [parts, step, u_low, d_y, rate_rows, start, last, padded(dt_low)]
        + [padded(w_dt_cols), full_xproj, ssm_vec[None, :], taps_table]
        + big_ins,
        [
            shape((rows, channels), BF),
            shape((8, LANES), F32),
            shape((channels, LANES), F32),
            shape((channels, LANES), F32),
            shape((states, channels), F32),
            shape(((taps + 2) * seqs, channels), F32),
        ]
        + block_rows_moved,
        [
            pltpu.VMEM(((tokens + 1) * states, seqs, LANES), F32),
            pltpu.VMEM((rows, 2 * states * LANES), F32),
            pltpu.VMEM((rows, channels), F32),
            pltpu.VMEM((rows, channels), BF),
            pltpu.VMEM((2, rows, LANES), BF),
            pltpu.VMEM((2, rows, LANES), BF),
            pltpu.VMEM((4 * seqs, channels), F32),
            bf_rows,
            bf_rows,
            pltpu.SemaphoreType.DMA((2, 2)),
            pltpu.SemaphoreType.DMA((2,)),
            pltpu.SemaphoreType.DMA((channels // LANES + 2,)),
        ]
        + scatter_scratch(count, big_grads),
        30,
        (len(big_ins), len(block_rows_moved)),
    )
    grad_alog = d_log.T * rates
    columns = jnp.sum(column_sums.reshape(taps + 2, seqs, channels), axis=1)
    grad_ssm = ssm_sums[0]
    grad_ssm = grad_ssm * (lax.axis_index("head") == 0).astype(F32)
    small = pack(
        [
            grad_xproj,
            grad_step_t[:, :rank],
            grad_alog,
            columns[:taps].T,
            columns[taps][:, None],
            columns[taps + 1][:, None],
            grad_skip[:, None],
        ],
        [jnp.zeros_like(grad_norm2), grad_norm2, grad_ssm],
    )
    small = owner_blocks(small.reshape(-1, pack_width))
    kinds = len(big_grads)
    grad_input, norm1_sums, *owns, pack_given, pack_came = input_call(
        d_inner_low,
        d_z,
        in_x_blocks,
        mix_blocks,
        x_low,
        x_norm,
        norm1_vec[None, :],
        d_hidden,
        small,
        (
            [grad_down] + big_grads,
            down_moved[:1] + first_moved[:kinds],
            down_moved[1:] + first_moved[kinds:],
        ),
        x_in.shape,
    )
    own_down, own_gate, own_up, own_out, own_in_z, own_in_x = owns
    small = scatter_own(small, pack_given, pack_came)
    own_norm1 = lax.dynamic_slice_in_dim(norm1_sums[0], place * (width // count), width // count)
    small = jnp.concatenate([small[:per], head_total(small[per:], F32)])[None]
    small_fields, small_gains = unpack(small)
    return (
        block_out,
        grad_input,
        own_norm1,
        own_in_x,
        own_in_z,
        small_fields[3].T,
        small_fields[4][:, 0],
        small_fields[0],
        small_gains[2],
        small_fields[1].T,
        small_fields[5][:, 0],
        small_fields[2],
        small_fields[6][:, 0],
        own_out.T,
        small_gains[1],
        own_gate,
        own_up,
        own_down.T,
    )


def solution(mesh):
    placed = (
        P(None, "seq", None),
        P(None, "seq"),
        P("seq"),
        P("seq", "head"),
        P("seq", "head"),
        P(None, ("head", "seq")),
        P(("head", "seq")),
        P(("head", "seq"), None),
        P("seq"),
        P(None, ("head", "seq")),
        P(("head", "seq")),
        P(("head", "seq"), None),
        P(("head", "seq")),
        P("head", "seq"),
        P("seq"),
        P("seq", "head"),
        P("seq", "head"),
        P("head", "seq"),
        P(None, "seq", None),
    )
    return jax.shard_map(
        shards,
        mesh=mesh,
        in_specs=placed,
        out_specs=(
            P(None, "seq", None),
            P(None, "seq", None),
            P("seq"),
            P("seq", "head"),
            P("seq", "head"),
            P(None, ("head", "seq")),
            P(("head", "seq")),
            P(("head", "seq"), None),
            P("seq"),
            P(None, ("head", "seq")),
            P(("head", "seq")),
            P(("head", "seq"), None),
            P(("head", "seq")),
            P("head", "seq"),
            P("seq"),
            P("seq", "head"),
            P("seq", "head"),
            P("head", "seq"),
        ),
        check_vma=False,
    )
```
